32 devices in a mesh: shot: 2 (over x), freq: 16 (over z, y, core).
Axes of the slice: x: 2, y: 2, z: 4, core: 2. Of those that a mesh axis runs over, the one named last changes fastest.
Arguments:
- receiver_data: float32 [64, 2, 32, 1024], P(('shot', 'freq')), parts along dimension 0, may hold values from -6 to 6
- source_spectrum: float32 [32, 2], P('freq'), may hold values from -4 to 4
- filter_taps: float32 [32, 4, 6], P('freq'), may hold values from -1.5 to 1.5, as said below
- slowness: float32 [16, 32, 1024], P('freq'), may hold values from 0.5 to 2
- depth_owner: int32 [6], P('shot'), parts along dimension 0, may hold values from 0 to 15
- source_position: int32 [4], P('shot'), parts along dimension 0, may hold values from 0 to 31
Outputs:
- migrated_image: float32 [32, 32, 1024], P(('shot', 'freq')), parts along dimension 0
The draws below stay inside these ranges and needn't reach their ends.
There are 2 independent parts, one for each index of `shot`. The reference program is written for one: setup_inputs(seed, part) draws one part's arguments, and reference() takes and returns one part's arrays. A program takes and returns all parts, laid end to end along the dimension named above; an argument that names none is the same for every part. Nothing has to cross between parts.
Inputs may be any that keep to these rules, and one draw needn't show every extreme that they name: `filter_taps`: each frequency and direction holds three complex taps.
All inputs are finite; a program needn't handle non-finite values.
Results may differ from the reference program's by a relative error of at most 0.0001.
Values sent between devices are 32-bit elements; how exact they have to be, the bound alone decides.
No kernel may reach another device: no remote copies, remote signals or barrier semaphores. Data moves between devices by JAX's collectives and lax.ppermute only.
A program may use at most 64 MiB of HBM per device.

```python
import math
import jax
import jax.numpy as jnp
from jax import lax

NX = 32
NY = 1024
STEPS = 3
NF = 32
SLABS = 16


def draw_filter_taps(key, part):
    keys = jax.random.split(jax.random.fold_in(key, 17), 5)
    shape = (NF, 4)
    angles = jax.random.uniform(keys[0], shape, jnp.float32, -math.pi, math.pi)
    first_re = jax.random.uniform(keys[1], shape, jnp.float32, 0.04, 0.1)
    first_im = jax.random.uniform(keys[2], shape, jnp.float32, -0.1, 0.1)
    second_re = jax.random.uniform(keys[3], shape, jnp.float32, 0.02, 0.04)
    second_im = jax.random.uniform(keys[4], shape, jnp.float32, -0.04, 0.04)
    rot_re = jnp.cos(angles)
    rot_im = jnp.sin(angles)
    inner_re = rot_re * first_re - rot_im * first_im
    inner_im = rot_re * first_im + rot_im * first_re
    outer_re = rot_re * second_re - rot_im * second_im
    outer_im = rot_re * second_im + rot_im * second_re
    centre_re = rot_re - 2.0 * inner_re - 2.0 * outer_re
    centre_im = rot_im - 2.0 * inner_im - 2.0 * outer_im
    return jnp.stack([centre_re, centre_im, inner_re, inner_im, outer_re, outer_im], axis=-1).astype(jnp.float32)


def levels(rng, shape, shards, low, high):
    def one(dim, parts):
        steps = jax.random.uniform(jax.random.fold_in(jax.random.fold_in(rng, 6), dim), (parts,), jnp.float32, low / len(shards), high / len(shards))
        return jnp.repeat(jnp.exp(steps), shape[dim] // parts).reshape((-1,) + (1,) * (len(shape) - dim - 1))

    factor_of = one(*shards[0])
    for cut in shards[1:]:
        factor_of = factor_of * one(*cut)
    return factor_of


def gaussian(rng, dims, spread, most, cuts=(), kind=jnp.bfloat16):
    drawn = spread * jax.random.normal(rng, dims, jnp.float32)
    if cuts:
        drawn = drawn * levels(rng, dims, cuts, -0.22, 0.18)
    return jnp.clip(drawn, -most, most).astype(kind)


def setup_inputs(seed: int = 0, part: int = 0) -> dict:
    splits = jax.random.split(jax.random.key(seed), 7)
    own_keys = jax.random.split(jax.random.fold_in(splits[6], part), 7)
    receiver_data = gaussian(own_keys[0], (NF, 2, NX, NY), 1.0, 6.0, ((0, 16),), jnp.float32)
    source_spectrum = gaussian(splits[1], (NF, 2), 1.0, 4.0, ((0, 16),), jnp.float32)
    filter_taps = draw_filter_taps(jax.random.fold_in(splits[6], 71), part)
    slowness = jnp.clip(jnp.exp(math.log(2.0) - 1.3862944 * jax.random.uniform(splits[3], (SLABS, NX, NY), jnp.float32) ** levels(splits[3], (SLABS, NX, NY), ((0, 16),), -0.2, 0.2)), 0.5, 2.0)
    depth_owner = jax.random.randint(own_keys[4], (STEPS,), 0, SLABS).astype(jnp.int32)
    source_position = jax.random.randint(own_keys[5], (2,), 0, NX).astype(jnp.int32)
    return {"receiver_data": receiver_data, "source_spectrum": source_spectrum, "filter_taps": filter_taps, "slowness": slowness, "depth_owner": depth_owner, "source_position": source_position}


lens_rate = 3.0
wave_rate = 0.5
directions = ((1, 0), (0, 1), (1, 1), (1, -1))

def source_start(spectrum, position, freq_index, freq_total, height, breadth):
    src_row = position[0].astype(jnp.float32)
    src_col = position[1].astype(jnp.float32)
    row_axis = jnp.arange(height, dtype=jnp.float32)[:, None]
    col_axis = jnp.arange(breadth, dtype=jnp.float32)[None, :]
    distance = jnp.sqrt((row_axis - src_row) ** 2 + (col_axis - src_col) ** 2 + 1.0)
    amplitude = 1.0 / (1.0 + distance / (height / 4.0))
    wavenumber = (freq_index.astype(jnp.float32) + 1.0) * (wave_rate / freq_total)
    phase_map = wavenumber[:, None, None] * distance[None]
    base_re = amplitude[None] * jnp.cos(phase_map)
    base_im = -amplitude[None] * jnp.sin(phase_map)
    wave_re = spectrum[:, 0][:, None, None]
    wave_im = spectrum[:, 1][:, None, None]
    return jnp.stack([wave_re * base_re - wave_im * base_im, wave_re * base_im + wave_im * base_re], axis=1)

def complex_mul(values, coef_re, coef_im):
    coef_re = coef_re[:, None, None]
    coef_im = coef_im[:, None, None]
    return jnp.stack([values[:, 0] * coef_re - values[:, 1] * coef_im, values[:, 0] * coef_im + values[:, 1] * coef_re], axis=1)

def thin_lens(wavefield, layer_slab, freq_index, freq_total, handed):
    phases = (freq_index.astype(jnp.float32) + 1.0)[:, None, None] * (lens_rate / freq_total) * layer_slab[None]
    rot_re = jnp.cos(phases)
    rot_im = handed * jnp.sin(phases)
    part_re = wavefield[:, 0]
    part_im = wavefield[:, 1]
    return jnp.stack([part_re * rot_re - part_im * rot_im, part_re * rot_im + part_im * rot_re], axis=1)

def directional(wavefield, coeffs, step_x, step_y, handed):
    height = wavefield.shape[2]
    breadth = wavefield.shape[3]
    padded = jnp.pad(wavefield, ((0, 0), (0, 0), (2, 2), (2, 2)))

    def adjacent(offset):
        return padded[:, :, 2 + offset * step_x:2 + offset * step_x + height, 2 + offset * step_y:2 + offset * step_y + breadth]
    inner_pair = adjacent(1) + adjacent(-1)
    outer_pair = adjacent(2) + adjacent(-2)
    result = complex_mul(wavefield, coeffs[:, 0], handed * coeffs[:, 1])
    result = result + complex_mul(inner_pair, coeffs[:, 2], handed * coeffs[:, 3])
    return result + complex_mul(outer_pair, coeffs[:, 4], handed * coeffs[:, 5])

def depth_step(source, receiver, layer_slab, filter_taps, freq_index, freq_total):
    source = thin_lens(source, layer_slab, freq_index, freq_total, -1.0)
    receiver = thin_lens(receiver, layer_slab, freq_index, freq_total, 1.0)
    for direction, (step_x, step_y) in enumerate(directions):
        source = directional(source, filter_taps[:, direction], step_x, step_y, 1.0)
        receiver = directional(receiver, filter_taps[:, direction], step_x, step_y, -1.0)
    return (source, receiver)

def reference(receiver_data, source_spectrum, filter_taps, slowness, depth_owner, source_position):
    freq_index = jnp.arange(NF, dtype=jnp.int32)
    source = source_start(source_spectrum, source_position, freq_index, NF, NX, NY)
    receiver = receiver_data
    slab_ids = jnp.arange(SLABS, dtype=jnp.int32)
    migrated = jnp.zeros((SLABS, NX, NY), jnp.float32)
    for level in range(STEPS):
        layer_slab = lax.dynamic_index_in_dim(slowness, depth_owner[level].astype(jnp.int32), 0, keepdims=False)
        source, receiver = depth_step(source, receiver, layer_slab, filter_taps, freq_index, NF)
        correlation = lax.optimization_barrier(jnp.sum(source[:, 0] * receiver[:, 0] + source[:, 1] * receiver[:, 1], axis=0)) / math.sqrt(NF)
        owner_mask = (slab_ids == depth_owner[level]).astype(jnp.float32)
        migrated = migrated + owner_mask[:, None, None] * correlation[None]
    return migrated
```

```python
import functools
import math

import jax
import jax.numpy as jnp
from jax import lax
from jax.experimental import pallas as pl
from jax.experimental.pallas import tpu as pltpu
from jax.sharding import PartitionSpec as P

lens_rate = 3.0
wave_rate = 0.5
directions = ((1, 0), (0, 1), (1, 1), (1, -1))
LANES = 128
SUB = 8
REACH = 2
TWO_OVER_PI = 2.0 / math.pi
PI_2 = (1.5703125, 4.837512969970703125e-4, 7.54978995489188216e-8)


def cos_sin(x):
    turns = jnp.floor(x * TWO_OVER_PI + 0.5)
    r = x - turns * PI_2[0]
    r = r - turns * PI_2[1]
    r = r - turns * PI_2[2]
    r2 = r * r
    s = r + r * r2 * (-1.6666654611e-1 + r2 * (8.3321608736e-3 + r2 * -1.9515295891e-4))
    c = (1.0 - 0.5 * r2) + r2 * r2 * (
        4.166664568298827e-2 + r2 * (-1.388731625493765e-3 + r2 * 2.443315711809948e-5)
    )
    quadrant = turns.astype(jnp.int32)
    odd = (quadrant & 1) == 1
    cos_value = jnp.where(odd, s, c)
    sin_value = jnp.where(odd, c, s)
    cos_value = jnp.where(((quadrant + 1) & 2) == 2, -cos_value, cos_value)
    sin_value = jnp.where((quadrant & 2) == 2, -sin_value, sin_value)
    return cos_value, sin_value


def swap_segments(blocks):
    count = len(blocks)
    width = LANES // count
    lane = lax.broadcasted_iota(jnp.int32, (SUB, LANES), 1)
    step = 1
    while step < count:
        upper = ((lane // (width * step)) & 1) == 1
        swapped = list(blocks)
        for b in range(count):
            if b & step == 0:
                low, high = blocks[b], blocks[b + step]
                swapped[b] = jnp.where(upper, pltpu.roll(high, step * width, 1), low)
                swapped[b + step] = jnp.where(
                    upper, high, pltpu.roll(low, LANES - step * width, 1)
                )
        blocks = swapped
        step *= 2
    return blocks


def interleave(blocks):
    count = len(blocks)
    width = LANES // count
    lane = lax.broadcasted_iota(jnp.int32, (SUB, LANES), 1)
    pick = (lane % width) * count + lane // width
    return swap_segments([jnp.take_along_axis(b, pick, axis=1) for b in blocks])


def deinterleave(blocks):
    count = len(blocks)
    width = LANES // count
    lane = lax.broadcasted_iota(jnp.int32, (SUB, LANES), 1)
    pick = (lane % count) * width + lane // count
    return [jnp.take_along_axis(b, pick, axis=1) for b in swap_segments(blocks)]


def migrate_kernel(
    freq_total, base_ref, position_ref, spectrum_ref, taps_ref, receiver_ref, slab_ref, out_ref, a_ref, b_ref, v_ref, c_ref
):
    freq_local, _, height, breadth = receiver_ref.shape
    levels = slab_ref.shape[0]
    blocks = breadth // LANES
    groups = height // SUB
    lane = lax.broadcasted_iota(jnp.int32, (SUB, LANES), 1)
    row = lax.broadcasted_iota(jnp.int32, (SUB, LANES), 0)
    not_first = lane > 0
    not_last = lane < LANES - 1

    def load(ref, f, field, part, block, group, shift=0):
        return ref[f, field, part, block + REACH, pl.ds(SUB * (group + 1) + shift, SUB), :]

    def store(ref, f, field, part, block, group, value):
        ref[f, field, part, block + REACH, pl.ds(SUB * (group + 1), SUB), :] = value

    zero = jnp.zeros((SUB, LANES), jnp.float32)

    @pl.loop(0, freq_local)
    def _(f):
        for ref in (a_ref, b_ref):
            for field in range(2):
                for part in range(2):
                    for block in range(blocks + 2 * REACH):
                        ref[f, field, part, block, 0:SUB, :] = zero
                        ref[f, field, part, block, SUB * (groups + 1) : SUB * (groups + 2), :] = zero

    @pl.loop(0, freq_local)
    def _(f):
        for part in range(2):
            for g in range(groups):
                loaded = [
                    receiver_ref[f, part, SUB * g : SUB * (g + 1), LANES * b : LANES * (b + 1)]
                    for b in range(blocks)
                ]
                for b, value in enumerate(interleave(loaded)):
                    store(a_ref, f, 1, part, b, g, -value if part else value)

    src_row = position_ref[0].astype(jnp.float32)
    src_col = position_ref[1].astype(jnp.float32)

    def number(f):
        return (base_ref[0] + f).astype(jnp.float32) + 1.0

    for g in range(groups):
        for b in range(blocks):
            d_row = (row + SUB * g).astype(jnp.float32) - src_row
            d_col = (lane * blocks + b).astype(jnp.float32) - src_col
            distance = jnp.sqrt(d_row * d_row + d_col * d_col + 1.0)
            amplitude = 1.0 / (1.0 + distance / (height / 4.0))
            for f in range(freq_local):
                cos_value, sin_value = cos_sin(number(f) * (wave_rate / freq_total) * distance)
                base_re = amplitude * cos_value
                base_im = -amplitude * sin_value
                w_re, w_im = spectrum_ref[f, 0], spectrum_ref[f, 1]
                store(a_ref, f, 0, 0, b, g, w_re * base_re - w_im * base_im)
                store(a_ref, f, 0, 1, b, g, w_re * base_im + w_im * base_re)

    @pl.loop(0, levels)
    def _(t):
        for g in range(groups):
            loaded = [
                slab_ref[t, SUB * g : SUB * (g + 1), LANES * b : LANES * (b + 1)] for b in range(blocks)
            ]
            for b, value in enumerate(interleave(loaded)):
                v_ref[t, b, SUB * g : SUB * (g + 1), :] = value

    def lens(t):
        @pl.loop(0, freq_local)
        def _(f):
            rate = number(f) * (lens_rate / freq_total)
            for g in range(groups):
                for b in range(blocks):
                    cos_value, sin_value = cos_sin(rate * v_ref[t, b, SUB * g : SUB * (g + 1), :])
                    for field in range(2):
                        re = load(a_ref, f, field, 0, b, g)
                        im = load(a_ref, f, field, 1, b, g)
                        store(a_ref, f, field, 0, b, g, re * cos_value + im * sin_value)
                        store(a_ref, f, field, 1, b, g, im * cos_value - re * sin_value)

    def filtered(src, f, field, b, g, d, taps):
        step_x, step_y = directions[d]

        def at(part, k):
            return load(src, f, field, part, b + k * step_y, g, k * step_x)

        c0r, c0i, c1r, c1i, c2r, c2i = taps
        re, im = at(0, 0), at(1, 0)
        p1r, p1i = at(0, 1) + at(0, -1), at(1, 1) + at(1, -1)
        p2r, p2i = at(0, 2) + at(0, -2), at(1, 2) + at(1, -2)
        out_re = (re * c0r - im * c0i) + (p1r * c1r - p1i * c1i) + (p2r * c2r - p2i * c2i)
        out_im = (re * c0i + im * c0r) + (p1r * c1i + p1i * c1r) + (p2r * c2i + p2i * c2r)
        return out_re, out_im

    def sweep(src, dst, d):
        @pl.loop(0, freq_local)
        def _(f):
            taps = [taps_ref[f, d, i] for i in range(6)]

            @pl.loop(0, 2)
            def _(field):
                for g in range(groups):
                    for b in range(blocks):
                        for part, value in enumerate(filtered(src, f, field, b, g, d, taps)):
                            store(dst, f, field, part, b, g, value)
                            if b < REACH:
                                store(dst, f, field, part, b + blocks, g, jnp.where(not_last, pltpu.roll(value, LANES - 1, 1), 0.0))
                            if b >= blocks - REACH:
                                store(dst, f, field, part, b - blocks, g, jnp.where(not_first, pltpu.roll(value, 1, 1), 0.0))

    def last_sweep(src, dst, d, t):
        @pl.loop(0, freq_local)
        def _(f):
            taps = [taps_ref[f, d, i] for i in range(6)]
            for g in range(groups):
                for b in range(blocks):
                    s_re, s_im = filtered(src, f, 0, b, g, d, taps)
                    r_re, r_im = filtered(src, f, 1, b, g, d, taps)
                    store(dst, f, 0, 0, b, g, s_re)
                    store(dst, f, 0, 1, b, g, s_im)
                    store(dst, f, 1, 0, b, g, r_re)
                    store(dst, f, 1, 1, b, g, r_im)
                    term = s_re * r_re - s_im * r_im
                    at = (b, slice(SUB * g, SUB * (g + 1)))
                    c_ref[at] = jnp.where(f == 0, term, c_ref[at] + term)

    @pl.loop(0, levels)
    def _(t):
        lens(t)
        sweep(a_ref, b_ref, 0)
        sweep(b_ref, a_ref, 1)
        sweep(a_ref, b_ref, 2)
        last_sweep(b_ref, a_ref, 3, t)
        for g in range(groups):
            summed = [c_ref[b, SUB * g : SUB * (g + 1)] for b in range(blocks)]
            for b, value in enumerate(deinterleave(summed)):
                out_ref[t, SUB * g : SUB * (g + 1), LANES * b : LANES * (b + 1)] = value * (
                    1.0 / math.sqrt(freq_total)
                )


def migrate(receiver, slabs, spectrum, taps, position, base, freq_total):
    freq_local, _, height, breadth = receiver.shape
    levels = slabs.shape[0]
    blocks = breadth // LANES
    state = pltpu.VMEM((freq_local, 2, 2, blocks + 2 * REACH, height + 2 * SUB, LANES), jnp.float32)
    smem = pl.BlockSpec(memory_space=pltpu.SMEM)
    vmem = pl.BlockSpec(memory_space=pltpu.VMEM)
    return pl.pallas_call(
        functools.partial(migrate_kernel, freq_total),
        out_shape=jax.ShapeDtypeStruct((levels, height, breadth), jnp.float32),
        in_specs=[smem, smem, smem, smem, vmem, vmem],
        out_specs=vmem,
        scratch_shapes=[
            state,
            state,
            pltpu.VMEM((levels, blocks, height, LANES), jnp.float32),
            pltpu.VMEM((blocks, height, LANES), jnp.float32),
        ],
        compiler_params=pltpu.CompilerParams(vmem_limit_bytes=32 * 1024 * 1024),
    )(base, position, spectrum, taps, receiver, slabs)


def across(bit, size):
    return [(i, i ^ bit) for i in range(size)]


def exchange(value, bit, size):
    return lax.ppermute(value, "freq", across(bit, size))


def fetch_slabs(own, owners, rank, size):
    half = own.shape[0] // 2
    parity = rank & 1
    halves = own.reshape(2, half, own.shape[1])
    mine, other = halves[parity], halves[1 - parity]
    got = exchange(other, 1, size)
    mismatch = owners ^ rank
    carried = jnp.where(((mismatch & 1) == 0)[:, None, None], mine[None], got[None])
    bit = 2
    while bit < size:
        got = exchange(carried, bit, size)
        carried = jnp.where(((mismatch & bit) == 0)[:, None, None], carried, got)
        bit *= 2
    got = exchange(carried, 1, size)
    return jnp.where(
        parity == 0, jnp.concatenate([carried, got], axis=1), jnp.concatenate([got, carried], axis=1)
    )


def sum_over(partial, rank, size):
    levels, height, breadth = partial.shape
    parity = rank & 1
    halves = partial.reshape(levels, 2, height // 2, breadth)
    carried = halves[:, parity] + exchange(halves[:, 1 - parity], 1, size)
    bit = 2
    while bit < size:
        carried = carried + exchange(carried, bit, size)
        bit *= 2
    got = exchange(carried, 1, size)
    return jnp.where(
        parity == 0, jnp.concatenate([carried, got], axis=1), jnp.concatenate([got, carried], axis=1)
    )


def local(receiver_data, source_spectrum, filter_taps, slowness, depth_owner, source_position):
    freq_local = receiver_data.shape[0]
    size = lax.axis_size("freq")
    rank = lax.axis_index("freq")
    freq_total = size * freq_local
    slabs = fetch_slabs(slowness[0], depth_owner, rank, size)
    base = (rank * freq_local).astype(jnp.int32).reshape(1)
    partial = migrate(
        receiver_data, slabs, source_spectrum, filter_taps, source_position, base, freq_total
    )
    summed = sum_over(partial, rank, size)
    owned = (depth_owner == rank).astype(jnp.float32)
    return jnp.sum(summed * owned[:, None, None], axis=0)[None]


def solution(mesh):
    return jax.shard_map(
        local,
        mesh=mesh,
        in_specs=(
            P(("shot", "freq"), None, None, None),
            P("freq", None),
            P("freq", None, None),
            P("freq", None, None),
            P("shot"),
            P("shot"),
        ),
        out_specs=P(("shot", "freq"), None, None),
        check_vma=False,
    )
```

```python
import functools
import math

import jax
import jax.numpy as jnp
from jax import lax
from jax.experimental import pallas as pl
from jax.experimental.pallas import tpu as pltpu
from jax.sharding import PartitionSpec as P

lens_rate = 3.0
wave_rate = 0.5
directions = ((1, 0), (0, 1), (1, 1), (1, -1))
LANES = 128
SUB = 8
REACH = 2
TWO_OVER_PI = 2.0 / math.pi
PI_2 = (1.5703125, 4.837512969970703125e-4, 7.54978995489188216e-8)


def cos_sin(x):
    turns = jnp.floor(x * TWO_OVER_PI + 0.5)
    r = x - turns * PI_2[0]
    r = r - turns * PI_2[1]
    r = r - turns * PI_2[2]
    r2 = r * r
    s = r + r * r2 * (-1.6666654611e-1 + r2 * (8.3321608736e-3 + r2 * -1.9515295891e-4))
    c = (1.0 - 0.5 * r2) + r2 * r2 * (
        4.166664568298827e-2 + r2 * (-1.388731625493765e-3 + r2 * 2.443315711809948e-5)
    )
    quadrant = turns.astype(jnp.int32)
    odd = (quadrant & 1) == 1
    cos_value = jnp.where(odd, s, c)
    sin_value = jnp.where(odd, c, s)
    cos_value = jnp.where(((quadrant + 1) & 2) == 2, -cos_value, cos_value)
    sin_value = jnp.where((quadrant & 2) == 2, -sin_value, sin_value)
    return cos_value, sin_value


def swap_segments(blocks):
    count = len(blocks)
    width = LANES // count
    lane = lax.broadcasted_iota(jnp.int32, (SUB, LANES), 1)
    step = 1
    while step < count:
        upper = ((lane // (width * step)) & 1) == 1
        swapped = list(blocks)
        for b in range(count):
            if b & step == 0:
                low, high = blocks[b], blocks[b + step]
                swapped[b] = jnp.where(upper, pltpu.roll(high, step * width, 1), low)
                swapped[b + step] = jnp.where(
                    upper, high, pltpu.roll(low, LANES - step * width, 1)
                )
        blocks = swapped
        step *= 2
    return blocks


def interleave(blocks):
    count = len(blocks)
    width = LANES // count
    lane = lax.broadcasted_iota(jnp.int32, (SUB, LANES), 1)
    pick = (lane % width) * count + lane // width
    return swap_segments([jnp.take_along_axis(b, pick, axis=1) for b in blocks])


def deinterleave(blocks):
    count = len(blocks)
    width = LANES // count
    lane = lax.broadcasted_iota(jnp.int32, (SUB, LANES), 1)
    pick = (lane % count) * width + lane // count
    return [jnp.take_along_axis(b, pick, axis=1) for b in swap_segments(blocks)]


def tile(ref, f, field, part, block, group, shift=0):
    return ref.at[f, field, part, block, pl.ds(SUB * group + shift, SUB), :]


def prepare_kernel(
    freq_total,
    base_ref,
    position_ref,
    mismatch_ref,
    spectrum_ref,
    taps_ref,
    receiver_ref,
    field_ref,
    taps_out_ref,
    rate_ref,
    turn_ref,
):
    freq_local, _, height, breadth = receiver_ref.shape
    blocks = breadth // LANES
    groups = height // SUB
    lane = lax.broadcasted_iota(jnp.int32, (SUB, LANES), 1)
    row = lax.broadcasted_iota(jnp.int32, (SUB, LANES), 0)

    def number(f):
        return (base_ref[0] + f).astype(jnp.float32) + 1.0

    @pl.loop(0, freq_local)
    def _(f):
        for part in range(2):
            for g in range(groups):
                loaded = [
                    receiver_ref[f, part, SUB * g : SUB * (g + 1), LANES * b : LANES * (b + 1)]
                    for b in range(blocks)
                ]
                for b, value in enumerate(interleave(loaded)):
                    tile(field_ref, f, 1, part, b, g)[...] = -value if part else value
        for d in range(len(directions)):
            for i in range(6):
                taps_out_ref[f, d, i] = jnp.full((SUB, LANES), taps_ref[f, d, i], jnp.float32)
        rate_ref[f] = jnp.full((SUB, LANES), number(f) * (lens_rate / freq_total), jnp.float32)

    for t in range(mismatch_ref.shape[0]):
        turn_ref[t] = jnp.full((SUB, LANES), mismatch_ref[t], jnp.int32)

    src_row = position_ref[0].astype(jnp.float32)
    src_col = position_ref[1].astype(jnp.float32)
    for g in range(groups):
        for b in range(blocks):
            d_row = (row + SUB * g).astype(jnp.float32) - src_row
            d_col = (lane * blocks + b).astype(jnp.float32) - src_col
            distance = jnp.sqrt(d_row * d_row + d_col * d_col + 1.0)
            amplitude = 1.0 / (1.0 + distance / (height / 4.0))
            for f in range(freq_local):
                cos_value, sin_value = cos_sin(number(f) * (wave_rate / freq_total) * distance)
                base_re = amplitude * cos_value
                base_im = -amplitude * sin_value
                w_re, w_im = spectrum_ref[f, 0], spectrum_ref[f, 1]
                tile(field_ref, f, 0, 0, b, g)[...] = w_re * base_re - w_im * base_im
                tile(field_ref, f, 0, 1, b, g)[...] = w_re * base_im + w_im * base_re


def migrate_kernel(
    freq_total, field_ref, taps_ref, rate_ref, slab_ref, out_ref, a_ref, b_ref, v_ref, c_ref
):
    freq_local = field_ref.shape[0]
    levels, height, breadth = slab_ref.shape
    blocks = breadth // LANES
    groups = height // SUB
    lane = lax.broadcasted_iota(jnp.int32, (SUB, LANES), 1)
    not_first = lane > 0
    not_last = lane < LANES - 1

    def load(ref, f, field, part, block, group, shift=0):
        return tile(ref, f, field, part, block + REACH, group + 1, shift)[...]

    def store(ref, f, field, part, block, group, value):
        tile(ref, f, field, part, block + REACH, group + 1)[...] = value

    zero = jnp.zeros((SUB, LANES), jnp.float32)

    @pl.loop(0, freq_local)
    def _(f):
        for ref in (a_ref, b_ref):
            for field in range(2):
                for part in range(2):
                    for block in range(blocks + 2 * REACH):
                        tile(ref, f, field, part, block, 0)[...] = zero
                        tile(ref, f, field, part, block, groups + 1)[...] = zero

    @pl.loop(0, levels)
    def _(t):
        for g in range(groups):
            loaded = [
                slab_ref[t, SUB * g : SUB * (g + 1), LANES * b : LANES * (b + 1)] for b in range(blocks)
            ]
            for b, value in enumerate(interleave(loaded)):
                v_ref[t, b, SUB * g : SUB * (g + 1), :] = value

    def lens(t, get):
        @pl.loop(0, freq_local)
        def _(f):
            rate = rate_ref[f]
            for g in range(groups):
                for b in range(blocks):
                    cos_value, sin_value = cos_sin(rate * v_ref[t, b, SUB * g : SUB * (g + 1), :])
                    for field in range(2):
                        re, im = get(f, field, 0, b, g), get(f, field, 1, b, g)
                        store(a_ref, f, field, 0, b, g, re * cos_value + im * sin_value)
                        store(a_ref, f, field, 1, b, g, im * cos_value - re * sin_value)

    def filtered(src, f, field, b, g, d, taps):
        step_x, step_y = directions[d]

        def at(part, k):
            return load(src, f, field, part, b + k * step_y, g, k * step_x)

        c0r, c0i, c1r, c1i, c2r, c2i = taps
        re, im = at(0, 0), at(1, 0)
        p1r, p1i = at(0, 1) + at(0, -1), at(1, 1) + at(1, -1)
        p2r, p2i = at(0, 2) + at(0, -2), at(1, 2) + at(1, -2)
        out_re = (re * c0r - im * c0i) + (p1r * c1r - p1i * c1i) + (p2r * c2r - p2i * c2i)
        out_im = (re * c0i + im * c0r) + (p1r * c1i + p1i * c1r) + (p2r * c2i + p2i * c2r)
        return out_re, out_im

    def sweep(src, dst, d):
        @pl.loop(0, freq_local)
        def _(f):
            taps = [taps_ref[f, d, i] for i in range(6)]

            @pl.loop(0, 2)
            def _(field):
                for g in range(groups):
                    for b in range(blocks):
                        for part, value in enumerate(filtered(src, f, field, b, g, d, taps)):
                            store(dst, f, field, part, b, g, value)
                            if b < REACH:
                                beside = jnp.where(not_last, pltpu.roll(value, LANES - 1, 1), 0.0)
                                store(dst, f, field, part, b + blocks, g, beside)
                            if b >= blocks - REACH:
                                beside = jnp.where(not_first, pltpu.roll(value, 1, 1), 0.0)
                                store(dst, f, field, part, b - blocks, g, beside)

    def last_sweep(src, dst, d):
        @pl.loop(0, freq_local)
        def _(f):
            taps = [taps_ref[f, d, i] for i in range(6)]
            for g in range(groups):
                for b in range(blocks):
                    s_re, s_im = filtered(src, f, 0, b, g, d, taps)
                    r_re, r_im = filtered(src, f, 1, b, g, d, taps)
                    store(dst, f, 0, 0, b, g, s_re)
                    store(dst, f, 0, 1, b, g, s_im)
                    store(dst, f, 1, 0, b, g, r_re)
                    store(dst, f, 1, 1, b, g, r_im)
                    term = s_re * r_re - s_im * r_im
                    at = (b, slice(SUB * g, SUB * (g + 1)))
                    c_ref[at] = jnp.where(f == 0, term, c_ref[at] + term)

    def depth_step(t):
        sweep(a_ref, b_ref, 0)
        sweep(b_ref, a_ref, 1)
        sweep(a_ref, b_ref, 2)
        last_sweep(b_ref, a_ref, 3)
        for g in range(groups):
            summed = [c_ref[b, SUB * g : SUB * (g + 1)] for b in range(blocks)]
            for b, value in enumerate(deinterleave(summed)):
                out_ref[t, SUB * g : SUB * (g + 1), LANES * b : LANES * (b + 1)] = value * (
                    1.0 / math.sqrt(freq_total)
                )

    lens(0, lambda f, field, part, b, g: tile(field_ref, f, field, part, b, g)[...])

    @pl.loop(0, levels)
    def _(t):
        @pl.when(t > 0)
        def _():
            lens(t, lambda f, field, part, b, g: load(a_ref, f, field, part, b, g))

        depth_step(t)


SMEM = pl.BlockSpec(memory_space=pltpu.SMEM)
VMEM = pl.BlockSpec(memory_space=pltpu.VMEM)


def prepare(receiver, spectrum, taps, position, mismatch, base, freq_total):
    freq_local, _, height, breadth = receiver.shape
    blocks = breadth // LANES
    cells = freq_local * height * breadth
    return pl.pallas_call(
        functools.partial(prepare_kernel, freq_total),
        out_shape=(
            jax.ShapeDtypeStruct((freq_local, 2, 2, blocks, height, LANES), jnp.float32),
            jax.ShapeDtypeStruct((freq_local, len(directions), 6, SUB, LANES), jnp.float32),
            jax.ShapeDtypeStruct((freq_local, SUB, LANES), jnp.float32),
            jax.ShapeDtypeStruct((mismatch.shape[0], SUB, LANES), jnp.int32),
        ),
        in_specs=[SMEM, SMEM, SMEM, SMEM, SMEM, VMEM],
        out_specs=(VMEM, VMEM, VMEM, VMEM),
        cost_estimate=pl.CostEstimate(flops=100 * cells, bytes_accessed=24 * cells, transcendentals=0),
        compiler_params=pltpu.CompilerParams(vmem_limit_bytes=32 * 1024 * 1024),
    )(base, position, mismatch, spectrum, taps, receiver)


def migrate(field, taps, rate, slabs, freq_total):
    freq_local, _, _, blocks, height, _ = field.shape
    levels = slabs.shape[0]
    state = pltpu.VMEM((freq_local, 2, 2, blocks + 2 * REACH, height + 2 * SUB, LANES), jnp.float32)
    return pl.pallas_call(
        functools.partial(migrate_kernel, freq_total),
        out_shape=jax.ShapeDtypeStruct(slabs.shape, jnp.float32),
        in_specs=[VMEM, VMEM, VMEM, VMEM],
        out_specs=VMEM,
        scratch_shapes=[
            state,
            state,
            pltpu.VMEM((levels, blocks, height, LANES), jnp.float32),
            pltpu.VMEM((blocks, height, LANES), jnp.float32),
        ],
        compiler_params=pltpu.CompilerParams(vmem_limit_bytes=32 * 1024 * 1024),
    )(field, taps, rate, slabs)


def exchange(value, mask, size):
    return lax.ppermute(value, "freq", [(i, i ^ mask) for i in range(size)])


def plan(size, height):
    split, cross = [], []
    bit = 1
    while bit < size:
        if len(split) < 2 and (height >> (len(split) + 1)) % SUB == 0:
            split.append(bit)
        else:
            cross.append((bit, bit | sum(b for b, _ in cross)))
        bit *= 2
    return split, cross


def halves_of(value, upper):
    half = value.shape[-2] // 2
    low, high = value[..., :half, :], value[..., half:, :]
    return jnp.where(upper, high, low), jnp.where(upper, low, high)


def joined(mine, other, upper):
    return jnp.where(
        upper, jnp.concatenate([other, mine], axis=-2), jnp.concatenate([mine, other], axis=-2)
    )


def fetch_slabs(own, mismatch, turn, rank, size):
    split, cross = plan(size, own.shape[0])
    held = own[None]
    wanted = jnp.zeros_like(mismatch)
    for i, bit in enumerate(split):
        upper = (rank & bit) != 0
        if i == 0:
            got, _ = halves_of(exchange(held, bit, size), upper)
            mine, _ = halves_of(held, upper)
        else:
            mine, other = halves_of(held, upper)
            got = exchange(other, bit, size)
        wanted = wanted + jnp.where((mismatch & bit) != 0, held.shape[0], 0)
        held = jnp.concatenate([mine, got], axis=0)
    carried = jnp.broadcast_to(held[:1], (mismatch.shape[0], *held.shape[1:]))
    for c in range(1, held.shape[0]):
        carried = jnp.where((wanted == c)[:, None, None], held[c][None], carried)
    for bit, mask in cross:
        got = exchange(carried, mask, size)
        keep = (mismatch & bit)[:, None, None] if bit != cross[-1][0] else turn[:, :1, :1] & bit
        carried = jnp.where(keep == 0, carried, got)
    for bit in reversed(split):
        carried = joined(carried, exchange(carried, bit, size), (rank & bit) != 0)
    return carried


def sums_to_owner(partial, owners, rank, size):
    split, cross = plan(size, partial.shape[1])
    carried = partial
    for bit in split:
        mine, other = halves_of(carried, (rank & bit) != 0)
        carried = mine + exchange(other, bit, size)
    for _, mask in cross:
        carried = carried + exchange(carried, mask, size)

    def slot(place):
        return jnp.sum(jnp.where((owners == place)[:, None, None], carried, 0.0), axis=0)

    near = [0]
    for bit in split:
        near = near + [n | bit for n in near]
    slots = {n: slot(rank ^ n) for n in near}
    for bit in reversed(split):
        sent = [n for n in near if n & bit]
        near = [n for n in near if not n & bit]
        got = exchange(jnp.stack([slots[n] for n in sent]), bit, size)
        upper = (rank & bit) != 0
        slots = {n: joined(slots[n], got[sent.index(n | bit)], upper) for n in near}
    return slots[0]


def local(receiver_data, source_spectrum, filter_taps, slowness, depth_owner, source_position):
    freq_local = receiver_data.shape[0]
    size = lax.axis_size("freq")
    rank = lax.axis_index("freq")
    freq_total = size * freq_local
    base = (rank * freq_local).astype(jnp.int32).reshape(1)
    mismatch = depth_owner ^ rank
    field, taps, rate, turn = prepare(
        receiver_data, source_spectrum, filter_taps, source_position, mismatch, base, freq_total
    )
    slabs = fetch_slabs(slowness[0], mismatch, turn, rank, size)
    partial = migrate(field, taps, rate, slabs, freq_total)
    return sums_to_owner(partial, depth_owner, rank, size)[None]


def solution(mesh):
    return jax.shard_map(
        local,
        mesh=mesh,
        in_specs=(
            P(("shot", "freq"), None, None, None),
            P("freq", None),
            P("freq", None, None),
            P("freq", None, None),
            P("shot"),
            P("shot"),
        ),
        out_specs=P(("shot", "freq"), None, None),
        check_vma=False,
    )
```

```python
import functools
import math

import jax
import jax.numpy as jnp
from jax import lax
from jax.experimental import pallas as pl
from jax.experimental.pallas import tpu as pltpu
from jax.sharding import PartitionSpec as P

lens_rate = 3.0
wave_rate = 0.5
directions = ((1, 0), (0, 1), (1, 1), (1, -1))
LANES = 128
SUB = 8
REACH = 2
TWO_OVER_PI = 2.0 / math.pi
PI_2 = (1.5703125, 4.837512969970703125e-4, 7.54978995489188216e-8)


def cos_sin(x):
    turns = jnp.floor(x * TWO_OVER_PI + 0.5)
    r = x - turns * PI_2[0]
    r = r - turns * PI_2[1]
    r = r - turns * PI_2[2]
    r2 = r * r
    s = r + r * r2 * (-1.6666654611e-1 + r2 * (8.3321608736e-3 + r2 * -1.9515295891e-4))
    c = (1.0 - 0.5 * r2) + r2 * r2 * (
        4.166664568298827e-2 + r2 * (-1.388731625493765e-3 + r2 * 2.443315711809948e-5)
    )
    quadrant = turns.astype(jnp.int32)
    odd = (quadrant & 1) == 1
    cos_value = jnp.where(odd, s, c)
    sin_value = jnp.where(odd, c, s)
    cos_value = jnp.where(((quadrant + 1) & 2) == 2, -cos_value, cos_value)
    sin_value = jnp.where((quadrant & 2) == 2, -sin_value, sin_value)
    return cos_value, sin_value


def quotient(x, divisor):
    return jnp.floor((x.astype(jnp.float32) + 0.5) * (1.0 / divisor)).astype(jnp.int32)


def columns():
    return lax.broadcasted_iota(jnp.int32, (SUB, LANES), 1)


def interleave(blocks):
    count = len(blocks)
    out = []
    for c in range(count):
        column = columns() * count + c
        pick, source = column & (LANES - 1), column >> (LANES.bit_length() - 1)
        value = jnp.take_along_axis(blocks[0], pick, axis=1)
        for b in range(1, count):
            value = jnp.where(source == b, jnp.take_along_axis(blocks[b], pick, axis=1), value)
        out.append(value)
    return out


def deinterleave(blocks):
    count = len(blocks)
    out = []
    for b in range(count):
        column = columns() + LANES * b
        pick = quotient(column, count)
        source = column - pick * count
        value = jnp.take_along_axis(blocks[0], pick, axis=1)
        for c in range(1, count):
            value = jnp.where(source == c, jnp.take_along_axis(blocks[c], pick, axis=1), value)
        out.append(value)
    return out


def tile(ref, f, field, part, block, group, shift=0):
    return ref.at[f, field, part, block, pl.ds(SUB * group + shift, SUB), :]


def prepare_kernel(
    freq_total,
    base_ref,
    place_ref,
    mismatch_ref,
    own_ref,
    own_scalars_ref,
    near_ref,
    near_scalars_ref,
    field_ref,
    taps_out_ref,
    rate_ref,
    turn_ref,
):
    freq_local, _, height, breadth = own_ref.shape
    blocks = breadth // LANES
    groups = height // SUB
    lane = columns()
    row = lax.broadcasted_iota(jnp.int32, (SUB, LANES), 0)
    taps_count = len(directions) * 6

    def scalar(ref, i):
        at = LANES * (i % blocks)
        return jnp.broadcast_to(ref[i // blocks : i // blocks + 1, at : at + LANES], (SUB, LANES))

    def number(side, f):
        return (base_ref[side] + f).astype(jnp.float32) + 1.0

    both = ((own_ref, own_scalars_ref), (near_ref, near_scalars_ref))
    for side, (receiver_ref, scalars_ref) in enumerate(both):
        for f in range(freq_local):
            for d in range(len(directions)):
                for i in range(6):
                    taps_out_ref[side * freq_local + f, d, i] = scalar(scalars_ref, f * taps_count + d * 6 + i)
            rate_ref[side * freq_local + f] = jnp.full(
                (SUB, LANES), number(side, f) * (lens_rate / freq_total), jnp.float32
            )

        @pl.loop(0, freq_local)
        def _(f):
            for part in range(2):
                for g in range(groups):
                    loaded = [
                        receiver_ref[f, part, SUB * g : SUB * (g + 1), LANES * b : LANES * (b + 1)]
                        for b in range(blocks)
                    ]
                    for b, value in enumerate(interleave(loaded)):
                        at = tile(field_ref, side * freq_local + f, 1, part, b, g)
                        at[...] = -value if part else value

    for t in range(mismatch_ref.shape[0]):
        turn_ref[t] = jnp.full((SUB, LANES), mismatch_ref[t], jnp.int32)

    src_row = place_ref[0].astype(jnp.float32)
    src_col = place_ref[1].astype(jnp.float32)
    first_col = place_ref[2]
    for g in range(groups):
        for b in range(blocks):
            d_row = (row + SUB * g).astype(jnp.float32) - src_row
            d_col = (lane * blocks + (first_col + b)).astype(jnp.float32) - src_col
            distance = jnp.sqrt(d_row * d_row + d_col * d_col + 1.0)
            amplitude = 1.0 / (1.0 + distance / (height / 4.0))
            for side, (_, scalars_ref) in enumerate(both):
                for f in range(freq_local):
                    cos_value, sin_value = cos_sin(number(side, f) * (wave_rate / freq_total) * distance)
                    base_re = amplitude * cos_value
                    base_im = -amplitude * sin_value
                    w_re = scalar(scalars_ref, freq_local * taps_count + 2 * f)
                    w_im = scalar(scalars_ref, freq_local * taps_count + 2 * f + 1)
                    at = side * freq_local + f
                    tile(field_ref, at, 0, 0, b, g)[...] = w_re * base_re - w_im * base_im
                    tile(field_ref, at, 0, 1, b, g)[...] = w_re * base_im + w_im * base_re


def migrate_kernel(
    freq_total, field_ref, taps_ref, rate_ref, slab_ref, out_ref, a_ref, b_ref, v_ref, c_ref
):
    freq_local = field_ref.shape[0]
    levels, height, breadth = slab_ref.shape
    blocks = breadth // LANES
    groups = height // SUB
    lane = lax.broadcasted_iota(jnp.int32, (SUB, LANES), 1)
    not_first = lane > 0
    not_last = lane < LANES - 1

    def load(ref, f, field, part, block, group, shift=0):
        return tile(ref, f, field, part, block + REACH, group + 1, shift)[...]

    def store(ref, f, field, part, block, group, value):
        tile(ref, f, field, part, block + REACH, group + 1)[...] = value

    zero = jnp.zeros((SUB, LANES), jnp.float32)

    @pl.loop(0, freq_local)
    def _(f):
        for ref in (a_ref, b_ref):
            for field in range(2):
                for part in range(2):
                    for block in range(blocks + 2 * REACH):
                        tile(ref, f, field, part, block, 0)[...] = zero
                        tile(ref, f, field, part, block, groups + 1)[...] = zero

    def rows_of(g):
        return pl.ds(pl.multiple_of(SUB * g, SUB), SUB)

    def take_slab(t, g):
        rows = rows_of(g)
        loaded = [slab_ref[t, rows, LANES * b : LANES * (b + 1)] for b in range(blocks)]
        for b, value in enumerate(interleave(loaded)):
            v_ref[t, b, rows, :] = value

    def give_sum(t, g):
        rows = rows_of(g)
        for b, value in enumerate(deinterleave([c_ref[t, b, rows] for b in range(blocks)])):
            out_ref[t, rows, LANES * b : LANES * (b + 1)] = value * (1.0 / math.sqrt(freq_total))

    def beside(work, t, f):
        share = -(-groups // freq_local)
        for k in range(share):
            work(t, jnp.minimum(f * share + k, groups - 1))

    for g in range(groups):
        take_slab(0, g)

    def lens(t, get):
        @pl.loop(0, freq_local)
        def _(f):
            rate = rate_ref[f]
            for g in range(groups):
                for b in range(blocks):
                    cos_value, sin_value = cos_sin(rate * v_ref[t, b, SUB * g : SUB * (g + 1), :])
                    for field in range(2):
                        re, im = get(f, field, 0, b, g), get(f, field, 1, b, g)
                        store(a_ref, f, field, 0, b, g, re * cos_value + im * sin_value)
                        store(a_ref, f, field, 1, b, g, im * cos_value - re * sin_value)

    def filtered(src, f, field, b, g, d, taps):
        step_x, step_y = directions[d]

        def at(part, k):
            return load(src, f, field, part, b + k * step_y, g, k * step_x)

        c0r, c0i, c1r, c1i, c2r, c2i = taps
        re, im = at(0, 0), at(1, 0)
        p1r, p1i = at(0, 1) + at(0, -1), at(1, 1) + at(1, -1)
        p2r, p2i = at(0, 2) + at(0, -2), at(1, 2) + at(1, -2)
        out_re = (re * c0r - im * c0i) + (p1r * c1r - p1i * c1i) + (p2r * c2r - p2i * c2i)
        out_im = (re * c0i + im * c0r) + (p1r * c1i + p1i * c1r) + (p2r * c2i + p2i * c2r)
        return out_re, out_im

    def sweep(src, dst, d, work=None, level=None):
        @pl.loop(0, freq_local)
        def _(f):
            taps = [taps_ref[f, d, i] for i in range(6)]
            if work is not None:
                beside(work, level, f)
            for field in range(2):
                for g in range(groups):
                    for b in range(blocks):
                        for part, value in enumerate(filtered(src, f, field, b, g, d, taps)):
                            store(dst, f, field, part, b, g, value)
                            if b < REACH:
                                edge = jnp.where(not_last, pltpu.roll(value, LANES - 1, 1), 0.0)
                                store(dst, f, field, part, b + blocks, g, edge)
                            if b >= blocks - REACH:
                                edge = jnp.where(not_first, pltpu.roll(value, 1, 1), 0.0)
                                store(dst, f, field, part, b - blocks, g, edge)

    def last_sweep(src, dst, d, t):
        @pl.loop(0, freq_local)
        def _(f):
            taps = [taps_ref[f, d, i] for i in range(6)]
            for g in range(groups):
                for b in range(blocks):
                    s_re, s_im = filtered(src, f, 0, b, g, d, taps)
                    r_re, r_im = filtered(src, f, 1, b, g, d, taps)
                    store(dst, f, 0, 0, b, g, s_re)
                    store(dst, f, 0, 1, b, g, s_im)
                    store(dst, f, 1, 0, b, g, r_re)
                    store(dst, f, 1, 1, b, g, r_im)
                    term = s_re * r_re - s_im * r_im
                    at = (t, b, slice(SUB * g, SUB * (g + 1)))
                    c_ref[at] = jnp.where(f == 0, term, c_ref[at] + term)

    def depth_step(t):
        sweep(a_ref, b_ref, 0, take_slab, jnp.minimum(t + 1, levels - 1))
        sweep(b_ref, a_ref, 1, give_sum, jnp.maximum(t - 1, 0))
        sweep(a_ref, b_ref, 2)
        last_sweep(b_ref, a_ref, 3, t)

    lens(0, lambda f, field, part, b, g: tile(field_ref, f, field, part, b, g)[...])

    @pl.loop(0, levels)
    def _(t):
        @pl.when(t > 0)
        def _():
            lens(t, lambda f, field, part, b, g: load(a_ref, f, field, part, b, g))

        depth_step(t)

    for g in range(groups):
        give_sum(levels - 1, g)


SMEM = pl.BlockSpec(memory_space=pltpu.SMEM)
VMEM = pl.BlockSpec(memory_space=pltpu.VMEM)


def prepare(own, own_scalars, near, near_scalars, place, mismatch, base, freq_total):
    freq_local, _, height, breadth = own.shape
    blocks = breadth // LANES
    cells = 2 * freq_local * height * breadth
    return pl.pallas_call(
        functools.partial(prepare_kernel, freq_total),
        out_shape=(
            jax.ShapeDtypeStruct((2 * freq_local, 2, 2, blocks, height, LANES), jnp.float32),
            jax.ShapeDtypeStruct((2 * freq_local, len(directions), 6, SUB, LANES), jnp.float32),
            jax.ShapeDtypeStruct((2 * freq_local, SUB, LANES), jnp.float32),
            jax.ShapeDtypeStruct((mismatch.shape[0], SUB, LANES), jnp.int32),
        ),
        in_specs=[SMEM, SMEM, SMEM, VMEM, VMEM, VMEM, VMEM],
        out_specs=(VMEM, VMEM, VMEM, VMEM),
        cost_estimate=pl.CostEstimate(flops=100 * cells, bytes_accessed=24 * cells, transcendentals=0),
        compiler_params=pltpu.CompilerParams(vmem_limit_bytes=32 * 1024 * 1024),
    )(base, place, mismatch, own, own_scalars, near, near_scalars)


def migrate(field, taps, rate, slabs, freq_total):
    freq_local, _, _, blocks, height, _ = field.shape
    levels = slabs.shape[0]
    state = pltpu.VMEM((freq_local, 2, 2, blocks + 2 * REACH, height + 2 * SUB, LANES), jnp.float32)
    return pl.pallas_call(
        functools.partial(migrate_kernel, freq_total),
        out_shape=jax.ShapeDtypeStruct(slabs.shape, jnp.float32),
        in_specs=[VMEM, VMEM, VMEM, VMEM],
        out_specs=VMEM,
        scratch_shapes=[
            state,
            state,
            pltpu.VMEM((levels, blocks, height, LANES), jnp.float32),
            pltpu.VMEM((levels, blocks, height, LANES), jnp.float32),
        ],
        compiler_params=pltpu.CompilerParams(vmem_limit_bytes=32 * 1024 * 1024),
    )(field, taps, rate, slabs)


def exchange(value, mask, size):
    return lax.ppermute(value, "freq", [(i, i ^ mask) for i in range(size)])


NEAR_ROWS = 1
NEAR_COLUMNS = 2


def far_bits(size):
    found = []
    bit = 2 * NEAR_COLUMNS
    while bit < size:
        found.append((bit, bit | sum(b for b, _ in found)))
        bit *= 2
    return found


def rows_split(value, upper):
    half = value.shape[-2] // 2
    low, high = value[..., :half, :], value[..., half:, :]
    return jnp.where(upper, high, low), jnp.where(upper, low, high)


def columns_split(value, upper, width):
    low, high = value[..., :width], value[..., value.shape[-1] - width :]
    return jnp.where(upper, high, low), jnp.where(upper, low, high)


def joined(mine, other, upper, axis):
    return jnp.where(
        upper, jnp.concatenate([other, mine], axis=axis), jnp.concatenate([mine, other], axis=axis)
    )


def fetch_slabs(own, mismatch, turn, rank, size, width):
    upper_rows = (rank & NEAR_ROWS) != 0
    upper_columns = (rank & NEAR_COLUMNS) != 0
    got, _ = rows_split(exchange(own, NEAR_ROWS, size), upper_rows)
    mine, _ = rows_split(own, upper_rows)
    held = jnp.stack([mine, got])
    mine, other = columns_split(held, upper_columns, width)
    held = jnp.concatenate([mine, exchange(other, NEAR_COLUMNS, size)], axis=0)
    wanted = mismatch & (NEAR_ROWS | NEAR_COLUMNS)
    carried = jnp.broadcast_to(held[:1], (mismatch.shape[0], *held.shape[1:]))
    for c in range(1, held.shape[0]):
        carried = jnp.where((wanted == c)[:, None, None], held[c][None], carried)
    far = far_bits(size)
    for bit, mask in far:
        got = exchange(carried, mask, size)
        keep = (mismatch & bit)[:, None, None] if bit != far[-1][0] else turn[:, :1, :1] & bit
        carried = jnp.where(keep == 0, carried, got)
    return joined(carried, exchange(carried, NEAR_ROWS, size), upper_rows, -2)


def sums_to_owner(partial, owners, rank, size, half):
    upper_rows = (rank & NEAR_ROWS) != 0
    upper_columns = (rank & NEAR_COLUMNS) != 0
    partial, _ = columns_split(partial, upper_columns, half)
    mine, other = rows_split(partial, upper_rows)
    carried = mine + exchange(other, NEAR_ROWS, size)
    for _, mask in far_bits(size):
        carried = carried + exchange(carried, mask, size)

    def slot(place):
        return jnp.sum(jnp.where((owners == place)[:, None, None], carried, 0.0), axis=0)

    mine = jnp.stack([slot(rank), slot(rank ^ NEAR_ROWS)])
    other = jnp.stack([slot(rank ^ NEAR_COLUMNS), slot(rank ^ NEAR_ROWS ^ NEAR_COLUMNS)])
    both = joined(mine, exchange(other, NEAR_COLUMNS, size), upper_columns, -1)
    return joined(both[0], exchange(both[1], NEAR_ROWS, size), upper_rows, -2)


def local(receiver_data, source_spectrum, filter_taps, slowness, depth_owner, source_position):
    freq_local, _, height, breadth = receiver_data.shape
    levels = depth_owner.shape[0]
    size = lax.axis_size("freq")
    rank = lax.axis_index("freq")
    freq_total = size * freq_local
    half = breadth // 2
    border = REACH * sum(1 for _, step_y in directions if step_y) * levels
    width = -(-(half + border) // LANES) * LANES
    upper_columns = (rank & NEAR_COLUMNS) != 0

    scalars = jnp.concatenate([filter_taps.reshape(-1), source_spectrum.reshape(-1)])
    scalar_rows = -(-scalars.shape[0] * LANES // (width * SUB)) * SUB
    scalars = jnp.pad(scalars, (0, scalar_rows * width // LANES - scalars.shape[0]))
    scalars = jnp.repeat(scalars, LANES).reshape(scalar_rows, width)
    own, sent = columns_split(receiver_data, upper_columns, width)
    sent = jnp.concatenate([sent.reshape(-1, width), scalars], axis=0)
    near = exchange(sent, NEAR_COLUMNS, size)
    near, near_scalars = near[:-scalar_rows].reshape(own.shape), near[-scalar_rows:]

    mismatch = depth_owner ^ rank
    first_column = jnp.where(upper_columns, breadth - width, 0).astype(jnp.int32).reshape(1)
    place = jnp.concatenate([source_position, first_column])
    base = (jnp.stack([rank, rank ^ NEAR_COLUMNS]) * freq_local).astype(jnp.int32)
    field, taps, rate, turn = prepare(
        own, scalars, near, near_scalars, place, mismatch, base, freq_total
    )
    slabs = fetch_slabs(slowness[0], mismatch, turn, rank, size, width)
    partial = migrate(field, taps, rate, slabs, freq_total)
    return sums_to_owner(partial, depth_owner, rank, size, half)[None]


def solution(mesh):
    return jax.shard_map(
        local,
        mesh=mesh,
        in_specs=(
            P(("shot", "freq"), None, None, None),
            P("freq", None),
            P("freq", None, None),
            P("freq", None, None),
            P("shot"),
            P("shot"),
        ),
        out_specs=P(("shot", "freq"), None, None),
        check_vma=False,
    )
```

```python
import functools
import math

import jax
import jax.numpy as jnp
from jax import lax
from jax.experimental import pallas as pl
from jax.experimental.pallas import tpu as pltpu
from jax.sharding import PartitionSpec as P

lens_rate = 3.0
wave_rate = 0.5
directions = ((1, 0), (0, 1), (1, 1), (1, -1))
LANES = 128
SUB = 8
REACH = 2
NEAR_ROWS = 1
NEAR_COLUMNS = 2
TWO_OVER_PI = 2.0 / math.pi
PI_2 = (1.5703125, 4.837512969970703125e-4, 7.54978995489188216e-8)


def cos_sin(x):
    turns = jnp.floor(x * TWO_OVER_PI + 0.5)
    r = x - turns * PI_2[0]
    r = r - turns * PI_2[1]
    r = r - turns * PI_2[2]
    r2 = r * r
    s = r + r * r2 * (-1.6666654611e-1 + r2 * (8.3321608736e-3 + r2 * -1.9515295891e-4))
    c = (1.0 - 0.5 * r2) + r2 * r2 * (
        4.166664568298827e-2 + r2 * (-1.388731625493765e-3 + r2 * 2.443315711809948e-5)
    )
    quadrant = turns.astype(jnp.int32)
    odd = (quadrant & 1) == 1
    cos_value = jnp.where(odd, s, c)
    sin_value = jnp.where(odd, c, s)
    cos_value = jnp.where(((quadrant + 1) & 2) == 2, -cos_value, cos_value)
    sin_value = jnp.where((quadrant & 2) == 2, -sin_value, sin_value)
    return cos_value, sin_value


def quotient(x, divisor):
    return jnp.floor((x.astype(jnp.float32) + 0.5) * (1.0 / divisor)).astype(jnp.int32)


def columns():
    return lax.broadcasted_iota(jnp.int32, (SUB, LANES), 1)


def interleave(blocks):
    count = len(blocks)
    out = []
    for c in range(count):
        column = columns() * count + c
        pick, source = column & (LANES - 1), column >> (LANES.bit_length() - 1)
        value = jnp.take_along_axis(blocks[0], pick, axis=1)
        for b in range(1, count):
            value = jnp.where(source == b, jnp.take_along_axis(blocks[b], pick, axis=1), value)
        out.append(value)
    return out


def deinterleave(blocks):
    count = len(blocks)
    out = []
    for b in range(count):
        column = columns() + LANES * b
        pick = quotient(column, count)
        source = column - pick * count
        value = jnp.take_along_axis(blocks[0], pick, axis=1)
        for c in range(1, count):
            value = jnp.where(source == c, jnp.take_along_axis(blocks[c], pick, axis=1), value)
        out.append(value)
    return out


def tile(ref, f, field, part, block, group, shift=0):
    return ref.at[f, field, part, block, pl.ds(SUB * group + shift, SUB), :]


def spread_turn(owner_ref, turn_ref):
    for t in range(owner_ref.shape[0]):
        turn_ref[t] = jnp.full((SUB, LANES), owner_ref[t] ^ lax.axis_index("freq"), jnp.int32)


def pack_kernel(owner_ref, taps_ref, spectrum_ref, receiver_ref, slab_ref, out_ref, turn_ref):
    spread_turn(owner_ref, turn_ref)
    freq_local, _, height, breadth = receiver_ref.shape
    width = out_ref.shape[1]
    start = jnp.where((lax.axis_index("freq") & NEAR_COLUMNS) != 0, 0, breadth - width)
    row = 0
    for f in range(freq_local):
        for part in range(2):
            for b in range(width // LANES):
                column = pl.ds(pl.multiple_of(start + LANES * b, LANES), LANES)
                out_ref[row : row + height, LANES * b : LANES * (b + 1)] = receiver_ref[f, part, :, column]
            row += height
    scalars = [
        taps_ref[f, d, i] for f in range(freq_local) for d in range(len(directions)) for i in range(6)
    ] + [spectrum_ref[f, i] for f in range(freq_local) for i in range(2)]
    lane = columns()
    for b in range(width // LANES):
        value = jnp.zeros((SUB, LANES), jnp.float32)
        for i, scalar in enumerate(scalars[LANES * b : LANES * (b + 1)]):
            value = jnp.where(lane == i, scalar, value)
        out_ref[row : row + SUB, LANES * b : LANES * (b + 1)] = value


def prepare(freq_total, rank, first_column, owner_ref, position_ref, block_of, taps_of, wave_of, results):
    field_ref, taps_out_ref, rate_ref, turn_ref = results
    freq_local, _, _, blocks, height, _ = field_ref.shape
    groups = height // SUB
    lane = columns()
    row = lax.broadcasted_iota(jnp.int32, (SUB, LANES), 0)

    def number(f):
        return (rank * freq_local + f).astype(jnp.float32) + 1.0

    for f in range(freq_local):
        for d in range(len(directions)):
            for i in range(6):
                taps_out_ref[f, d, i] = jnp.broadcast_to(taps_of(f, d, i), (SUB, LANES))
        rate_ref[f] = jnp.full((SUB, LANES), number(f) * (lens_rate / freq_total), jnp.float32)
    spread_turn(owner_ref, turn_ref)

    @pl.loop(0, freq_local)
    def _(f):
        for part in range(2):
            for g in range(groups):
                loaded = [block_of(f, part, g, b) for b in range(blocks)]
                for b, value in enumerate(interleave(loaded)):
                    tile(field_ref, f, 1, part, b, g)[...] = -value if part else value

    src_row = position_ref[0].astype(jnp.float32)
    src_col = position_ref[1].astype(jnp.float32)
    waves = [(wave_of(f, 0), wave_of(f, 1)) for f in range(freq_local)]
    for g in range(groups):
        for b in range(blocks):
            d_row = (row + SUB * g).astype(jnp.float32) - src_row
            d_col = (lane * blocks + (first_column + b)).astype(jnp.float32) - src_col
            distance = jnp.sqrt(d_row * d_row + d_col * d_col + 1.0)
            amplitude = 1.0 / (1.0 + distance / (height / 4.0))
            for f, (w_re, w_im) in enumerate(waves):
                cos_value, sin_value = cos_sin(number(f) * (wave_rate / freq_total) * distance)
                base_re = amplitude * cos_value
                base_im = -amplitude * sin_value
                tile(field_ref, f, 0, 0, b, g)[...] = w_re * base_re - w_im * base_im
                tile(field_ref, f, 0, 1, b, g)[...] = w_re * base_im + w_im * base_re


def prepare_own_kernel(
    freq_total, owner_ref, position_ref, taps_ref, spectrum_ref, receiver_ref, *results
):
    blocks = results[0].shape[3]
    here = lax.axis_index("freq")
    first_column = jnp.where((here & NEAR_COLUMNS) != 0, receiver_ref.shape[3] - blocks * LANES, 0)

    def block_of(f, part, g, b):
        column = pl.ds(pl.multiple_of(first_column + LANES * b, LANES), LANES)
        return receiver_ref[f, part, SUB * g : SUB * (g + 1), column]

    prepare(
        freq_total,
        here,
        first_column,
        owner_ref,
        position_ref,
        block_of,
        lambda f, d, i: taps_ref[f, d, i],
        lambda f, i: spectrum_ref[f, i],
        results,
    )


def prepare_near_kernel(freq_total, breadth, owner_ref, position_ref, packed_ref, *results):
    freq_local, _, _, blocks, height, _ = results[0].shape
    here = lax.axis_index("freq")
    first_column = jnp.where((here & NEAR_COLUMNS) != 0, breadth - blocks * LANES, 0)
    rows = freq_local * 2 * height
    taps_count = len(directions) * 6

    def block_of(f, part, g, b):
        row = pl.multiple_of((2 * f + part) * height + SUB * g, SUB)
        return packed_ref[pl.ds(row, SUB), LANES * b : LANES * (b + 1)]

    def scalar(i):
        return jnp.broadcast_to(packed_ref[rows : rows + SUB, i : i + 1], (SUB, LANES))

    prepare(
        freq_total,
        here ^ NEAR_COLUMNS,
        first_column,
        owner_ref,
        position_ref,
        block_of,
        lambda f, d, i: scalar(f * taps_count + 6 * d + i),
        lambda f, i: scalar(freq_local * taps_count + 2 * f + i),
        results,
    )


def migrate_kernel(
    freq_total,
    own_ref,
    own_taps_ref,
    own_rate_ref,
    near_ref,
    near_taps_ref,
    near_rate_ref,
    slab_ref,
    out_ref,
    a_ref,
    b_ref,
    v_ref,
    c_ref,
    taps_ref,
    rate_ref,
):
    freq_own = own_ref.shape[0]
    freq_local = 2 * freq_own
    levels, height, breadth = slab_ref.shape
    blocks = breadth // LANES
    groups = height // SUB
    lane = lax.broadcasted_iota(jnp.int32, (SUB, LANES), 1)
    not_first = lane > 0
    not_last = lane < LANES - 1

    def load(ref, f, field, part, block, group, shift=0):
        return tile(ref, f, field, part, block + REACH, group + 1, shift)[...]

    def store(ref, f, field, part, block, group, value):
        tile(ref, f, field, part, block + REACH, group + 1)[...] = value

    for side, (one_taps_ref, one_rate_ref) in enumerate(
        ((own_taps_ref, own_rate_ref), (near_taps_ref, near_rate_ref))
    ):
        for f in range(freq_own):
            rate_ref[side * freq_own + f] = one_rate_ref[f]
            for d in range(len(directions)):
                for i in range(6):
                    taps_ref[side * freq_own + f, d, i] = one_taps_ref[f, d, i]

    zero = jnp.zeros((SUB, LANES), jnp.float32)

    @pl.loop(0, freq_local)
    def _(f):
        for ref in (a_ref, b_ref):
            for field in range(2):
                for part in range(2):
                    for block in range(blocks + 2 * REACH):
                        tile(ref, f, field, part, block, 0)[...] = zero
                        tile(ref, f, field, part, block, groups + 1)[...] = zero

    def rows_of(g):
        return pl.ds(pl.multiple_of(SUB * g, SUB), SUB)

    def take_slab(t, g):
        rows = rows_of(g)
        loaded = [slab_ref[t, rows, LANES * b : LANES * (b + 1)] for b in range(blocks)]
        for b, value in enumerate(interleave(loaded)):
            v_ref[t, b, rows, :] = value

    def give_sum(t, g):
        rows = rows_of(g)
        for b, value in enumerate(deinterleave([c_ref[t, b, rows] for b in range(blocks)])):
            out_ref[t, rows, LANES * b : LANES * (b + 1)] = value * (1.0 / math.sqrt(freq_total))

    def beside(work, t, f):
        share = -(-groups // freq_local)
        for k in range(share):
            work(t, jnp.minimum(f * share + k, groups - 1))

    for g in range(groups):
        take_slab(0, g)

    def lens(t, get, first, count):
        @pl.loop(first, first + count)
        def _(f):
            rate = rate_ref[f]
            for g in range(groups):
                for b in range(blocks):
                    cos_value, sin_value = cos_sin(rate * v_ref[t, b, SUB * g : SUB * (g + 1), :])
                    for field in range(2):
                        re, im = get(f, field, 0, b, g), get(f, field, 1, b, g)
                        store(a_ref, f, field, 0, b, g, re * cos_value + im * sin_value)
                        store(a_ref, f, field, 1, b, g, im * cos_value - re * sin_value)

    def filtered(src, f, field, b, g, d, taps):
        step_x, step_y = directions[d]

        def at(part, k):
            return load(src, f, field, part, b + k * step_y, g, k * step_x)

        c0r, c0i, c1r, c1i, c2r, c2i = taps
        re, im = at(0, 0), at(1, 0)
        p1r, p1i = at(0, 1) + at(0, -1), at(1, 1) + at(1, -1)
        p2r, p2i = at(0, 2) + at(0, -2), at(1, 2) + at(1, -2)
        out_re = (re * c0r - im * c0i) + (p1r * c1r - p1i * c1i) + (p2r * c2r - p2i * c2i)
        out_im = (re * c0i + im * c0r) + (p1r * c1i + p1i * c1r) + (p2r * c2i + p2i * c2r)
        return out_re, out_im

    def sweep(src, dst, d, work=None, level=None):
        @pl.loop(0, freq_local)
        def _(f):
            taps = [taps_ref[f, d, i] for i in range(6)]
            if work is not None:
                beside(work, level, f)
            for field in range(2):
                for g in range(groups):
                    for b in range(blocks):
                        for part, value in enumerate(filtered(src, f, field, b, g, d, taps)):
                            store(dst, f, field, part, b, g, value)
                            if b < REACH:
                                edge = jnp.where(not_last, pltpu.roll(value, LANES - 1, 1), 0.0)
                                store(dst, f, field, part, b + blocks, g, edge)
                            if b >= blocks - REACH:
                                edge = jnp.where(not_first, pltpu.roll(value, 1, 1), 0.0)
                                store(dst, f, field, part, b - blocks, g, edge)

    def last_sweep(src, dst, d, t):
        @pl.loop(0, freq_local)
        def _(f):
            taps = [taps_ref[f, d, i] for i in range(6)]
            for g in range(groups):
                for b in range(blocks):
                    s_re, s_im = filtered(src, f, 0, b, g, d, taps)
                    r_re, r_im = filtered(src, f, 1, b, g, d, taps)
                    store(dst, f, 0, 0, b, g, s_re)
                    store(dst, f, 0, 1, b, g, s_im)
                    store(dst, f, 1, 0, b, g, r_re)
                    store(dst, f, 1, 1, b, g, r_im)
                    term = s_re * r_re - s_im * r_im
                    at = (t, b, slice(SUB * g, SUB * (g + 1)))
                    c_ref[at] = jnp.where(f == 0, term, c_ref[at] + term)

    def depth_step(t):
        sweep(a_ref, b_ref, 0, take_slab, jnp.minimum(t + 1, levels - 1))
        sweep(b_ref, a_ref, 1, give_sum, jnp.maximum(t - 1, 0))
        sweep(a_ref, b_ref, 2)
        last_sweep(b_ref, a_ref, 3, t)

    for side, ref in enumerate((own_ref, near_ref)):
        first = side * freq_own

        def surface(f, field, part, b, g, ref=ref, first=first):
            return tile(ref, f - first, field, part, b, g)[...]

        lens(0, surface, first, freq_own)

    @pl.loop(0, levels)
    def _(t):
        @pl.when(t > 0)
        def _():
            lens(t, lambda f, field, part, b, g: load(a_ref, f, field, part, b, g), 0, freq_local)

        depth_step(t)

    for g in range(groups):
        give_sum(levels - 1, g)


SMEM = pl.BlockSpec(memory_space=pltpu.SMEM)
VMEM = pl.BlockSpec(memory_space=pltpu.VMEM)


def pack(owners, taps, spectrum, receiver, slab, width):
    freq_local, _, height, _ = receiver.shape
    rows = freq_local * 2 * height + SUB
    return pl.pallas_call(
        pack_kernel,
        out_shape=(
            jax.ShapeDtypeStruct((rows, width), jnp.float32),
            jax.ShapeDtypeStruct((owners.shape[0], SUB, LANES), jnp.int32),
        ),
        in_specs=[SMEM, SMEM, SMEM, VMEM, pl.BlockSpec(memory_space=pl.ANY)],
        out_specs=(VMEM, VMEM),
        cost_estimate=pl.CostEstimate(flops=0, bytes_accessed=8 * rows * width, transcendentals=0),
        compiler_params=pltpu.CompilerParams(vmem_limit_bytes=32 * 1024 * 1024),
    )(owners, taps, spectrum, receiver, slab)


def prepared(kernel, shape, levels, width, specs, operands):
    freq_local, _, height, _ = shape
    cells = freq_local * height * width
    return pl.pallas_call(
        kernel,
        out_shape=(
            jax.ShapeDtypeStruct((freq_local, 2, 2, width // LANES, height, LANES), jnp.float32),
            jax.ShapeDtypeStruct((freq_local, len(directions), 6, SUB, LANES), jnp.float32),
            jax.ShapeDtypeStruct((freq_local, SUB, LANES), jnp.float32),
            jax.ShapeDtypeStruct((levels, SUB, LANES), jnp.int32),
        ),
        in_specs=specs,
        out_specs=(VMEM, VMEM, VMEM, VMEM),
        cost_estimate=pl.CostEstimate(flops=100 * cells, bytes_accessed=24 * cells, transcendentals=0),
        compiler_params=pltpu.CompilerParams(vmem_limit_bytes=32 * 1024 * 1024),
    )(*operands)


def migrate(own, near, slabs, freq_total):
    freq_own, _, _, blocks, height, _ = own[0].shape
    freq_local = 2 * freq_own
    levels = slabs.shape[0]
    state = pltpu.VMEM((freq_local, 2, 2, blocks + 2 * REACH, height + 2 * SUB, LANES), jnp.float32)
    return pl.pallas_call(
        functools.partial(migrate_kernel, freq_total),
        out_shape=jax.ShapeDtypeStruct(slabs.shape, jnp.float32),
        in_specs=[VMEM] * 7,
        out_specs=VMEM,
        scratch_shapes=[
            state,
            state,
            pltpu.VMEM((levels, blocks, height, LANES), jnp.float32),
            pltpu.VMEM((levels, blocks, height, LANES), jnp.float32),
            pltpu.VMEM((freq_local, len(directions), 6, SUB, LANES), jnp.float32),
            pltpu.VMEM((freq_local, SUB, LANES), jnp.float32),
        ],
        compiler_params=pltpu.CompilerParams(vmem_limit_bytes=32 * 1024 * 1024),
    )(*own, *near, slabs)


def exchange(value, mask, size):
    return lax.ppermute(value, "freq", [(i, i ^ mask) for i in range(size)])


def far_bits(size):
    found = []
    bit = 2 * NEAR_COLUMNS
    while bit < size:
        found.append((bit, bit | sum(b for b, _ in found)))
        bit *= 2
    return found


def rows_split(value, upper):
    half = value.shape[-2] // 2
    low, high = value[..., :half, :], value[..., half:, :]
    return jnp.where(upper, high, low), jnp.where(upper, low, high)


def columns_split(value, upper, width):
    low, high = value[..., :width], value[..., value.shape[-1] - width :]
    return jnp.where(upper, high, low), jnp.where(upper, low, high)


def joined(mine, other, upper, axis):
    return jnp.where(
        upper, jnp.concatenate([other, mine], axis=axis), jnp.concatenate([mine, other], axis=axis)
    )


def fetch_slabs(own, got, turns, rank, size, width):
    upper_rows = (rank & NEAR_ROWS) != 0
    upper_columns = (rank & NEAR_COLUMNS) != 0
    mine, _ = rows_split(own, upper_rows)
    got, _ = rows_split(got, upper_rows)
    held = jnp.stack([mine, got])
    mine, other = columns_split(held, upper_columns, width)
    held = jnp.concatenate([mine, exchange(other, NEAR_COLUMNS, size)], axis=0)
    wanted = turns[0][:, :1, :1] & (NEAR_ROWS | NEAR_COLUMNS)
    carried = jnp.broadcast_to(held[:1], (wanted.shape[0], *held.shape[1:]))
    for c in range(1, held.shape[0]):
        carried = jnp.where(wanted == c, held[c][None], carried)
    far = far_bits(size)
    for i, (bit, mask) in enumerate(far):
        got = exchange(carried, mask, size)
        turn = turns[2 if i == len(far) - 1 else 1][:, :1, :1]
        carried = jnp.where((turn & bit) == 0, carried, got)
    return joined(carried, exchange(carried, NEAR_ROWS, size), upper_rows, -2)


def sums_to_owner(partial, owners, rank, size, half):
    upper_rows = (rank & NEAR_ROWS) != 0
    upper_columns = (rank & NEAR_COLUMNS) != 0
    partial, _ = columns_split(partial, upper_columns, half)
    mine, other = rows_split(partial, upper_rows)
    carried = mine + exchange(other, NEAR_ROWS, size)
    for _, mask in far_bits(size):
        carried = carried + exchange(carried, mask, size)

    def slot(place):
        return jnp.sum(jnp.where((owners == place)[:, None, None], carried, 0.0), axis=0)

    mine = jnp.stack([slot(rank), slot(rank ^ NEAR_ROWS)])
    other = jnp.stack([slot(rank ^ NEAR_COLUMNS), slot(rank ^ NEAR_ROWS ^ NEAR_COLUMNS)])
    both = joined(mine, exchange(other, NEAR_COLUMNS, size), upper_columns, -1)
    return joined(both[0], exchange(both[1], NEAR_ROWS, size), upper_rows, -2)


def local(receiver_data, source_spectrum, filter_taps, slowness, depth_owner, source_position):
    freq_local, _, height, breadth = receiver_data.shape
    levels = depth_owner.shape[0]
    size = lax.axis_size("freq")
    rank = lax.axis_index("freq")
    freq_total = size * freq_local
    half = breadth // 2
    border = REACH * sum(1 for _, step_y in directions if step_y) * levels
    width = -(-(half + border) // LANES) * LANES
    shape = receiver_data.shape

    near_slab = exchange(slowness[0], NEAR_ROWS, size)
    packed, pack_turn = pack(
        depth_owner, filter_taps, source_spectrum, receiver_data, near_slab, width
    )
    packed = exchange(packed, NEAR_COLUMNS, size)
    *own, own_turn = prepared(
        functools.partial(prepare_own_kernel, freq_total),
        shape,
        levels,
        width,
        [SMEM, SMEM, SMEM, SMEM, VMEM],
        (depth_owner, source_position, filter_taps, source_spectrum, receiver_data),
    )
    *near, near_turn = prepared(
        functools.partial(prepare_near_kernel, freq_total, breadth),
        shape,
        levels,
        width,
        [SMEM, SMEM, VMEM],
        (depth_owner, source_position, packed),
    )
    turns = (pack_turn, own_turn, near_turn)
    slabs = fetch_slabs(slowness[0], near_slab, turns, rank, size, width)
    partial = migrate(own, near, slabs, freq_total)
    return sums_to_owner(partial, depth_owner, rank, size, half)[None]


def solution(mesh):
    return jax.shard_map(
        local,
        mesh=mesh,
        in_specs=(
            P(("shot", "freq"), None, None, None),
            P("freq", None),
            P("freq", None, None),
            P("freq", None, None),
            P("shot"),
            P("shot"),
        ),
        out_specs=P(("shot", "freq"), None, None),
        check_vma=False,
    )
```

```python
import functools
import math

import jax
import jax.numpy as jnp
from jax import lax
from jax.experimental import pallas as pl
from jax.experimental.pallas import tpu as pltpu
from jax.sharding import PartitionSpec as P

lens_rate = 3.0
wave_rate = 0.5
directions = ((1, 0), (0, 1), (1, 1), (1, -1))
LANES = 128
SUB = 8
REACH = 2
NEAR_ROWS = 1
NEAR_COLUMNS = 2
TWO_OVER_PI = 2.0 / math.pi
PI_2 = (1.5703125, 4.837512969970703125e-4, 7.54978995489188216e-8)


def cos_sin(x):
    turns = jnp.floor(x * TWO_OVER_PI + 0.5)
    r = x - turns * PI_2[0]
    r = r - turns * PI_2[1]
    r = r - turns * PI_2[2]
    r2 = r * r
    s = r + r * r2 * (-1.6666654611e-1 + r2 * (8.3321608736e-3 + r2 * -1.9515295891e-4))
    c = (1.0 - 0.5 * r2) + r2 * r2 * (
        4.166664568298827e-2 + r2 * (-1.388731625493765e-3 + r2 * 2.443315711809948e-5)
    )
    quadrant = turns.astype(jnp.int32)
    odd = (quadrant & 1) == 1
    cos_value = jnp.where(odd, s, c)
    sin_value = jnp.where(odd, c, s)
    cos_value = jnp.where(((quadrant + 1) & 2) == 2, -cos_value, cos_value)
    sin_value = jnp.where((quadrant & 2) == 2, -sin_value, sin_value)
    return cos_value, sin_value


def quotient(x, divisor):
    return jnp.floor((x.astype(jnp.float32) + 0.5) * (1.0 / divisor)).astype(jnp.int32)


def columns():
    return lax.broadcasted_iota(jnp.int32, (SUB, LANES), 1)


def interleave(blocks):
    count = len(blocks)
    out = []
    for c in range(count):
        column = columns() * count + c
        pick, source = column & (LANES - 1), column >> (LANES.bit_length() - 1)
        value = jnp.take_along_axis(blocks[0], pick, axis=1)
        for b in range(1, count):
            value = jnp.where(source == b, jnp.take_along_axis(blocks[b], pick, axis=1), value)
        out.append(value)
    return out


def deinterleave(blocks):
    count = len(blocks)
    out = []
    for b in range(count):
        column = columns() + LANES * b
        pick = quotient(column, count)
        source = column - pick * count
        value = jnp.take_along_axis(blocks[0], pick, axis=1)
        for c in range(1, count):
            value = jnp.where(source == c, jnp.take_along_axis(blocks[c], pick, axis=1), value)
        out.append(value)
    return out


def tile(ref, f, field, part, block, group, shift=0):
    return ref.at[f, field, part, block, pl.ds(SUB * group + shift, SUB), :]


def spread_turn(owner_ref, turn_ref):
    for t in range(owner_ref.shape[0]):
        turn_ref[t] = jnp.full((SUB, LANES), owner_ref[t] ^ lax.axis_index("freq"), jnp.int32)


def tail_of(ref, rows, i):
    across = ref.shape[1] // LANES
    down = rows + SUB * (i // across)
    return ref.at[down : down + SUB, LANES * (i % across) : LANES * (i % across + 1)]


def tail_rows(freq_local, height, half, border):
    strips = -(-freq_local * 2 * (height // SUB) // (LANES // border))
    scalars = -(-freq_local * (len(directions) * 6 + 2) // LANES)
    return SUB * -(-(strips + scalars) // (half // LANES)), strips


def pack_kernel(border, taps_ref, spectrum_ref, receiver_ref, slab_ref, out_ref):
    freq_local, _, height, breadth = receiver_ref.shape
    half = out_ref.shape[1]
    groups = height // SUB
    _, strips = tail_rows(freq_local, height, half, border)
    lane = columns()
    to_lower = (lax.axis_index("freq") & NEAR_COLUMNS) != 0
    start = jnp.where(to_lower, 0, breadth - half)
    beside = pl.ds(pl.multiple_of(jnp.where(to_lower, half, half - LANES), LANES), LANES)
    rows = freq_local * 2 * height
    per = LANES // border
    strip = [jnp.zeros((SUB, LANES), jnp.float32) for _ in range(strips)]
    for f in range(freq_local):
        for part in range(2):
            row = (2 * f + part) * height
            for b in range(half // LANES):
                column = pl.ds(pl.multiple_of(start + LANES * b, LANES), LANES)
                out_ref[row : row + height, LANES * b : LANES * (b + 1)] = receiver_ref[f, part, :, column]
            for g in range(groups):
                value = receiver_ref[f, part, SUB * g : SUB * (g + 1), beside]
                value = jnp.where(to_lower, value, pltpu.roll(value, border, 1))
                i, at = divmod((2 * f + part) * groups + g, per)
                if at:
                    value = pltpu.roll(value, border * at, 1)
                strip[i] = jnp.where((lane >= border * at) & (lane < border * (at + 1)), value, strip[i])
    for i, value in enumerate(strip):
        tail_of(out_ref, rows, i)[...] = value
    scalars = [
        taps_ref[f, d, i] for f in range(freq_local) for d in range(len(directions)) for i in range(6)
    ] + [spectrum_ref[f, i] for f in range(freq_local) for i in range(2)]
    for b in range(-(-len(scalars) // LANES)):
        value = jnp.zeros((SUB, LANES), jnp.float32)
        for i, scalar in enumerate(scalars[LANES * b : LANES * (b + 1)]):
            value = jnp.where(lane == i, scalar, value)
        tail_of(out_ref, rows, strips + b)[...] = value


def prepare(freq_total, rank, first_column, owner_ref, position_ref, block_of, taps_of, wave_of, results):
    field_ref, taps_out_ref, rate_ref, turn_ref = results
    freq_local, _, _, blocks, height, _ = field_ref.shape
    groups = height // SUB
    lane = columns()
    row = lax.broadcasted_iota(jnp.int32, (SUB, LANES), 0)

    def number(f):
        return (rank * freq_local + f).astype(jnp.float32) + 1.0

    for f in range(freq_local):
        for d in range(len(directions)):
            for i in range(6):
                taps_out_ref[f, d, i] = jnp.broadcast_to(taps_of(f, d, i), (SUB, LANES))
        rate_ref[f] = jnp.full((SUB, LANES), number(f) * (lens_rate / freq_total), jnp.float32)
    spread_turn(owner_ref, turn_ref)

    for f in range(freq_local):
        for part in range(2):
            for g in range(groups):
                loaded = [block_of(f, part, g, b) for b in range(blocks)]
                for b, value in enumerate(interleave(loaded)):
                    tile(field_ref, f, 1, part, b, g)[...] = -value if part else value

    src_row = position_ref[0].astype(jnp.float32)
    src_col = position_ref[1].astype(jnp.float32)
    waves = [(wave_of(f, 0), wave_of(f, 1)) for f in range(freq_local)]
    for g in range(groups):
        for b in range(blocks):
            d_row = (row + SUB * g).astype(jnp.float32) - src_row
            d_col = (lane * blocks + (first_column + b)).astype(jnp.float32) - src_col
            distance = jnp.sqrt(d_row * d_row + d_col * d_col + 1.0)
            amplitude = 1.0 / (1.0 + distance / (height / 4.0))
            for f, (w_re, w_im) in enumerate(waves):
                cos_value, sin_value = cos_sin(number(f) * (wave_rate / freq_total) * distance)
                base_re = amplitude * cos_value
                base_im = -amplitude * sin_value
                tile(field_ref, f, 0, 0, b, g)[...] = w_re * base_re - w_im * base_im
                tile(field_ref, f, 0, 1, b, g)[...] = w_re * base_im + w_im * base_re


def prepare_own_kernel(
    freq_total, owner_ref, position_ref, taps_ref, spectrum_ref, receiver_ref, packed_ref, *results
):
    blocks = results[0].shape[3]
    here = lax.axis_index("freq")
    first_column = jnp.where((here & NEAR_COLUMNS) != 0, receiver_ref.shape[3] - blocks * LANES, 0)

    def block_of(f, part, g, b):
        column = pl.ds(pl.multiple_of(first_column + LANES * b, LANES), LANES)
        return receiver_ref[f, part, SUB * g : SUB * (g + 1), column]

    prepare(
        freq_total,
        here,
        first_column,
        owner_ref,
        position_ref,
        block_of,
        lambda f, d, i: taps_ref[f, d, i],
        lambda f, i: spectrum_ref[f, i],
        results,
    )


def prepare_near_kernel(freq_total, breadth, border, owner_ref, position_ref, packed_ref, *results):
    freq_local, _, _, blocks, height, _ = results[0].shape
    half = packed_ref.shape[1]
    groups = height // SUB
    here = lax.axis_index("freq")
    upper = (here & NEAR_COLUMNS) != 0
    first_column = jnp.where(upper, breadth - blocks * LANES, 0)
    rows = freq_local * 2 * height
    _, strips = tail_rows(freq_local, height, half, border)
    per = LANES // border
    taps_count = len(directions) * 6
    lane = columns()

    def main(f, part, g, b):
        row = (2 * f + part) * height + SUB * g
        return packed_ref[row : row + SUB, LANES * b : LANES * (b + 1)]

    def beside(f, part, g):
        i, at = divmod((2 * f + part) * groups + g, per)
        value = tail_of(packed_ref, rows, i)[...]
        if at:
            value = pltpu.roll(value, LANES - border * at, 1)
        value = jnp.where(lane < border, value, 0.0)
        return jnp.where(upper, pltpu.roll(value, LANES - border, 1), value)

    def block_of(f, part, g, b):
        if b == 0:
            return jnp.where(upper, beside(f, part, g), main(f, part, g, 0))
        if b == blocks - 1:
            return jnp.where(upper, main(f, part, g, b - 1), beside(f, part, g))
        return jnp.where(upper, main(f, part, g, b - 1), main(f, part, g, b))

    def scalar(i):
        value = tail_of(packed_ref, rows, strips + i // LANES)[...]
        return jnp.broadcast_to(value[:, i % LANES : i % LANES + 1], (SUB, LANES))

    prepare(
        freq_total,
        here ^ NEAR_COLUMNS,
        first_column,
        owner_ref,
        position_ref,
        block_of,
        lambda f, d, i: scalar(f * taps_count + 6 * d + i),
        lambda f, i: scalar(freq_local * taps_count + 2 * f + i),
        results,
    )


def migrate_kernel(
    freq_total,
    own_ref,
    own_taps_ref,
    own_rate_ref,
    near_ref,
    near_taps_ref,
    near_rate_ref,
    slab_ref,
    out_ref,
    a_ref,
    b_ref,
    v_ref,
    c_ref,
    taps_ref,
    rate_ref,
):
    freq_own = own_ref.shape[0]
    freq_local = 2 * freq_own
    levels, height, breadth = slab_ref.shape
    blocks = breadth // LANES
    groups = height // SUB
    lane = lax.broadcasted_iota(jnp.int32, (SUB, LANES), 1)
    not_first = lane > 0
    not_last = lane < LANES - 1

    def load(ref, f, field, part, block, group, shift=0):
        return tile(ref, f, field, part, block + REACH, group + 1, shift)[...]

    def store(ref, f, field, part, block, group, value):
        tile(ref, f, field, part, block + REACH, group + 1)[...] = value

    for side, (one_taps_ref, one_rate_ref) in enumerate(
        ((own_taps_ref, own_rate_ref), (near_taps_ref, near_rate_ref))
    ):
        for f in range(freq_own):
            rate_ref[side * freq_own + f] = one_rate_ref[f]
            for d in range(len(directions)):
                for i in range(6):
                    taps_ref[side * freq_own + f, d, i] = one_taps_ref[f, d, i]

    zero = jnp.zeros((SUB, LANES), jnp.float32)

    @pl.loop(0, freq_local)
    def _(f):
        for ref in (a_ref, b_ref):
            for field in range(2):
                for part in range(2):
                    for block in range(blocks + 2 * REACH):
                        tile(ref, f, field, part, block, 0)[...] = zero
                        tile(ref, f, field, part, block, groups + 1)[...] = zero

    def rows_of(g):
        return pl.ds(pl.multiple_of(SUB * g, SUB), SUB)

    def take_slab(t, g):
        rows = rows_of(g)
        loaded = [slab_ref[t, rows, LANES * b : LANES * (b + 1)] for b in range(blocks)]
        for b, value in enumerate(interleave(loaded)):
            v_ref[t, b, rows, :] = value

    def give_sum(t, g):
        rows = rows_of(g)
        for b, value in enumerate(deinterleave([c_ref[t, b, rows] for b in range(blocks)])):
            out_ref[t, rows, LANES * b : LANES * (b + 1)] = value * (1.0 / math.sqrt(freq_total))

    def beside(work, t, f):
        share = -(-groups // freq_local)
        for k in range(share):
            work(t, jnp.minimum(f * share + k, groups - 1))

    for g in range(groups):
        take_slab(0, g)

    def lens(t, get, first, count):
        @pl.loop(first, first + count)
        def _(f):
            rate = rate_ref[f]
            for g in range(groups):
                for b in range(blocks):
                    cos_value, sin_value = cos_sin(rate * v_ref[t, b, SUB * g : SUB * (g + 1), :])
                    for field in range(2):
                        re, im = get(f, field, 0, b, g), get(f, field, 1, b, g)
                        store(a_ref, f, field, 0, b, g, re * cos_value + im * sin_value)
                        store(a_ref, f, field, 1, b, g, im * cos_value - re * sin_value)

    def filtered(src, f, field, b, g, d, taps):
        step_x, step_y = directions[d]

        def at(part, k):
            return load(src, f, field, part, b + k * step_y, g, k * step_x)

        c0r, c0i, c1r, c1i, c2r, c2i = taps
        re, im = at(0, 0), at(1, 0)
        p1r, p1i = at(0, 1) + at(0, -1), at(1, 1) + at(1, -1)
        p2r, p2i = at(0, 2) + at(0, -2), at(1, 2) + at(1, -2)
        out_re = (re * c0r - im * c0i) + (p1r * c1r - p1i * c1i) + (p2r * c2r - p2i * c2i)
        out_im = (re * c0i + im * c0r) + (p1r * c1i + p1i * c1r) + (p2r * c2i + p2i * c2r)
        return out_re, out_im

    def sweep(src, dst, d, work=None, level=None):
        @pl.loop(0, freq_local)
        def _(f):
            taps = [taps_ref[f, d, i] for i in range(6)]
            if work is not None:
                beside(work, level, f)
            for field in range(2):
                for g in range(groups):
                    for b in range(blocks):
                        for part, value in enumerate(filtered(src, f, field, b, g, d, taps)):
                            store(dst, f, field, part, b, g, value)
                            if b < REACH:
                                edge = jnp.where(not_last, pltpu.roll(value, LANES - 1, 1), 0.0)
                                store(dst, f, field, part, b + blocks, g, edge)
                            if b >= blocks - REACH:
                                edge = jnp.where(not_first, pltpu.roll(value, 1, 1), 0.0)
                                store(dst, f, field, part, b - blocks, g, edge)

    def last_sweep(src, dst, d, t):
        @pl.loop(0, freq_local)
        def _(f):
            taps = [taps_ref[f, d, i] for i in range(6)]
            for g in range(groups):
                for b in range(blocks):
                    s_re, s_im = filtered(src, f, 0, b, g, d, taps)
                    r_re, r_im = filtered(src, f, 1, b, g, d, taps)
                    store(dst, f, 0, 0, b, g, s_re)
                    store(dst, f, 0, 1, b, g, s_im)
                    store(dst, f, 1, 0, b, g, r_re)
                    store(dst, f, 1, 1, b, g, r_im)
                    term = s_re * r_re - s_im * r_im
                    at = (t, b, slice(SUB * g, SUB * (g + 1)))
                    c_ref[at] = jnp.where(f == 0, term, c_ref[at] + term)

    def depth_step(t):
        sweep(a_ref, b_ref, 0, take_slab, jnp.minimum(t + 1, levels - 1))
        sweep(b_ref, a_ref, 1, give_sum, jnp.maximum(t - 1, 0))
        sweep(a_ref, b_ref, 2)
        last_sweep(b_ref, a_ref, 3, t)

    for side, ref in enumerate((own_ref, near_ref)):
        first = side * freq_own

        def surface(f, field, part, b, g, ref=ref, first=first):
            return tile(ref, f - first, field, part, b, g)[...]

        lens(0, surface, first, freq_own)

    @pl.loop(0, levels)
    def _(t):
        @pl.when(t > 0)
        def _():
            lens(t, lambda f, field, part, b, g: load(a_ref, f, field, part, b, g), 0, freq_local)

        depth_step(t)

    for g in range(groups):
        give_sum(levels - 1, g)


SMEM = pl.BlockSpec(memory_space=pltpu.SMEM)
VMEM = pl.BlockSpec(memory_space=pltpu.VMEM)


def pack(taps, spectrum, receiver, slab, half, border):
    freq_local, _, height, _ = receiver.shape
    rows = freq_local * 2 * height + tail_rows(freq_local, height, half, border)[0]
    return pl.pallas_call(
        functools.partial(pack_kernel, border),
        out_shape=jax.ShapeDtypeStruct((rows, half), jnp.float32),
        in_specs=[SMEM, SMEM, VMEM, pl.BlockSpec(memory_space=pl.ANY)],
        out_specs=VMEM,
        cost_estimate=pl.CostEstimate(flops=0, bytes_accessed=8 * rows * half, transcendentals=0),
        compiler_params=pltpu.CompilerParams(vmem_limit_bytes=32 * 1024 * 1024),
    )(taps, spectrum, receiver, slab)


def prepared(kernel, shape, levels, width, specs, operands):
    freq_local, _, height, _ = shape
    cells = freq_local * height * width
    return pl.pallas_call(
        kernel,
        out_shape=(
            jax.ShapeDtypeStruct((freq_local, 2, 2, width // LANES, height, LANES), jnp.float32),
            jax.ShapeDtypeStruct((freq_local, len(directions), 6, SUB, LANES), jnp.float32),
            jax.ShapeDtypeStruct((freq_local, SUB, LANES), jnp.float32),
            jax.ShapeDtypeStruct((levels, SUB, LANES), jnp.int32),
        ),
        in_specs=specs,
        out_specs=(VMEM, VMEM, VMEM, VMEM),
        cost_estimate=pl.CostEstimate(flops=100 * cells, bytes_accessed=24 * cells, transcendentals=0),
        compiler_params=pltpu.CompilerParams(vmem_limit_bytes=32 * 1024 * 1024),
    )(*operands)


def migrate(own, near, slabs, freq_total):
    freq_own, _, _, blocks, height, _ = own[0].shape
    freq_local = 2 * freq_own
    levels = slabs.shape[0]
    state = pltpu.VMEM((freq_local, 2, 2, blocks + 2 * REACH, height + 2 * SUB, LANES), jnp.float32)
    return pl.pallas_call(
        functools.partial(migrate_kernel, freq_total),
        out_shape=jax.ShapeDtypeStruct(slabs.shape, jnp.float32),
        in_specs=[VMEM] * 7,
        out_specs=VMEM,
        scratch_shapes=[
            state,
            state,
            pltpu.VMEM((levels, blocks, height, LANES), jnp.float32),
            pltpu.VMEM((levels, blocks, height, LANES), jnp.float32),
            pltpu.VMEM((freq_local, len(directions), 6, SUB, LANES), jnp.float32),
            pltpu.VMEM((freq_local, SUB, LANES), jnp.float32),
        ],
        compiler_params=pltpu.CompilerParams(vmem_limit_bytes=32 * 1024 * 1024),
    )(*own, *near, slabs)


def exchange(value, mask, size):
    return lax.ppermute(value, "freq", [(i, i ^ mask) for i in range(size)])


def far_bits(size):
    found = []
    bit = 2 * NEAR_COLUMNS
    while bit < size:
        found.append((bit, bit | sum(b for b, _ in found)))
        bit *= 2
    return found


def rows_split(value, upper):
    half = value.shape[-2] // 2
    low, high = value[..., :half, :], value[..., half:, :]
    return jnp.where(upper, high, low), jnp.where(upper, low, high)


def columns_split(value, upper, width):
    low, high = value[..., :width], value[..., value.shape[-1] - width :]
    return jnp.where(upper, high, low), jnp.where(upper, low, high)


def joined(mine, other, upper, axis):
    return jnp.where(
        upper, jnp.concatenate([other, mine], axis=axis), jnp.concatenate([mine, other], axis=axis)
    )


def fetch_slabs(own, got, turns, rank, size, width):
    upper_rows = (rank & NEAR_ROWS) != 0
    upper_columns = (rank & NEAR_COLUMNS) != 0
    mine, _ = rows_split(own, upper_rows)
    got, _ = rows_split(got, upper_rows)
    held = jnp.stack([mine, got])
    mine, other = columns_split(held, upper_columns, width)
    held = jnp.concatenate([mine, exchange(other, NEAR_COLUMNS, size)], axis=0)
    wanted = turns[0][:, :1, :1] & (NEAR_ROWS | NEAR_COLUMNS)
    carried = jnp.broadcast_to(held[:1], (wanted.shape[0], *held.shape[1:]))
    for c in range(1, held.shape[0]):
        carried = jnp.where(wanted == c, held[c][None], carried)
    far = far_bits(size)
    for i, (bit, mask) in enumerate(far):
        got = exchange(carried, mask, size)
        turn = turns[1 if i == len(far) - 1 else 0][:, :1, :1]
        carried = jnp.where((turn & bit) == 0, carried, got)
    return joined(carried, exchange(carried, NEAR_ROWS, size), upper_rows, -2)


def sums_to_owner(partial, owners, rank, size, half):
    upper_rows = (rank & NEAR_ROWS) != 0
    upper_columns = (rank & NEAR_COLUMNS) != 0
    partial, _ = columns_split(partial, upper_columns, half)
    mine, other = rows_split(partial, upper_rows)
    carried = mine + exchange(other, NEAR_ROWS, size)
    for _, mask in far_bits(size):
        carried = carried + exchange(carried, mask, size)

    def slot(place):
        return jnp.sum(jnp.where((owners == place)[:, None, None], carried, 0.0), axis=0)

    mine = jnp.stack([slot(rank), slot(rank ^ NEAR_ROWS)])
    other = jnp.stack([slot(rank ^ NEAR_COLUMNS), slot(rank ^ NEAR_ROWS ^ NEAR_COLUMNS)])
    both = joined(mine, exchange(other, NEAR_COLUMNS, size), upper_columns, -1)
    return joined(both[0], exchange(both[1], NEAR_ROWS, size), upper_rows, -2)


def local(receiver_data, source_spectrum, filter_taps, slowness, depth_owner, source_position):
    freq_local, _, height, breadth = receiver_data.shape
    levels = depth_owner.shape[0]
    size = lax.axis_size("freq")
    rank = lax.axis_index("freq")
    freq_total = size * freq_local
    half = breadth // 2
    border = REACH * sum(1 for _, step_y in directions if step_y) * levels
    width = half + LANES
    shape = receiver_data.shape

    near_slab = exchange(slowness[0], NEAR_ROWS, size)
    packed = pack(
        filter_taps, source_spectrum, receiver_data, near_slab, half, border
    )
    arrived = exchange(packed, NEAR_COLUMNS, size)
    *own, own_turn = prepared(
        functools.partial(prepare_own_kernel, freq_total),
        shape,
        levels,
        width,
        [SMEM, SMEM, SMEM, SMEM, VMEM, pl.BlockSpec(memory_space=pl.ANY)],
        (depth_owner, source_position, filter_taps, source_spectrum, receiver_data, packed),
    )
    *near, near_turn = prepared(
        functools.partial(prepare_near_kernel, freq_total, breadth, border),
        shape,
        levels,
        width,
        [SMEM, SMEM, VMEM],
        (depth_owner, source_position, arrived),
    )
    turns = (own_turn, near_turn)
    slabs = fetch_slabs(slowness[0], near_slab, turns, rank, size, width)
    partial = migrate(own, near, slabs, freq_total)
    return sums_to_owner(partial, depth_owner, rank, size, half)[None]


def solution(mesh):
    return jax.shard_map(
        local,
        mesh=mesh,
        in_specs=(
            P(("shot", "freq"), None, None, None),
            P("freq", None),
            P("freq", None, None),
            P("freq", None, None),
            P("shot"),
            P("shot"),
        ),
        out_specs=P(("shot", "freq"), None, None),
        check_vma=False,
    )
```

```python
import functools
import math

import jax
import jax.numpy as jnp
from jax import lax
from jax.experimental import pallas as pl
from jax.experimental.pallas import tpu as pltpu
from jax.sharding import PartitionSpec as P

lens_rate = 3.0
wave_rate = 0.5
greatest_slowness = 2.0
directions = ((1, 0), (0, 1), (1, 1), (1, -1))
LANES = 128
SUB = 8
REACH = 2
NEAR_ROWS = 1
NEAR_COLUMNS = 2
TWO_OVER_PI = 2.0 / math.pi
PI_2 = (1.5703125, 4.837512969970703125e-4, 7.54978995489188216e-8)


def small_cos_sin(r):
    r2 = r * r
    s = r + r * r2 * (-1.6666654611e-1 + r2 * (8.3321608736e-3 + r2 * -1.9515295891e-4))
    c = (1.0 - 0.5 * r2) + r2 * r2 * (
        4.166664568298827e-2 + r2 * (-1.388731625493765e-3 + r2 * 2.443315711809948e-5)
    )
    return c, s


def cos_sin(x):
    turns = jnp.floor(x * TWO_OVER_PI + 0.5)
    r = x - turns * PI_2[0]
    r = r - turns * PI_2[1]
    r = r - turns * PI_2[2]
    c, s = small_cos_sin(r)
    quadrant = turns.astype(jnp.int32)
    odd = (quadrant & 1) == 1
    cos_value = jnp.where(odd, s, c)
    sin_value = jnp.where(odd, c, s)
    cos_value = jnp.where(((quadrant + 1) & 2) == 2, -cos_value, cos_value)
    sin_value = jnp.where((quadrant & 2) == 2, -sin_value, sin_value)
    return cos_value, sin_value


def quotient(x, divisor):
    return jnp.floor((x.astype(jnp.float32) + 0.5) * (1.0 / divisor)).astype(jnp.int32)


def columns():
    return lax.broadcasted_iota(jnp.int32, (SUB, LANES), 1)


def interleave(blocks, shifts=None):
    count = len(blocks)
    out = []
    for c in range(count):
        column = columns() * count + c
        pick, source = column & (LANES - 1), column >> (LANES.bit_length() - 1)
        value = None
        for b in range(count):
            at = pick if shifts is None or shifts[b] is None else (pick + shifts[b]) & (LANES - 1)
            found = jnp.take_along_axis(blocks[b], at, axis=1)
            value = found if value is None else jnp.where(source == b, found, value)
        out.append(value)
    return out


def deinterleave(blocks):
    count = len(blocks)
    out = []
    for b in range(count):
        column = columns() + LANES * b
        pick = quotient(column, count)
        source = column - pick * count
        value = jnp.take_along_axis(blocks[0], pick, axis=1)
        for c in range(1, count):
            value = jnp.where(source == c, jnp.take_along_axis(blocks[c], pick, axis=1), value)
        out.append(value)
    return out


def tile(ref, f, field, part, block, group, shift=0):
    return ref.at[f, field, part, block, pl.ds(SUB * group + shift, SUB), :]


def spread_turn(owner_ref, turn_ref):
    for t in range(owner_ref.shape[0]):
        turn_ref[t] = jnp.full((SUB, LANES), owner_ref[t] ^ lax.axis_index("freq"), jnp.int32)


def tail_of(ref, rows, i):
    across = ref.shape[1] // LANES
    down = rows + SUB * (i // across)
    return ref.at[down : down + SUB, LANES * (i % across) : LANES * (i % across + 1)]


def tail_rows(freq_local, height, half, border):
    strips = -(-freq_local * 2 * (height // SUB) // (LANES // border))
    scalars = -(-freq_local * (len(directions) * 6 + 2) // LANES)
    return SUB * -(-(strips + scalars) // (half // LANES)), strips


def pack_kernel(border, taps_ref, spectrum_ref, receiver_ref, slab_ref, out_ref):
    freq_local, _, height, breadth = receiver_ref.shape
    half = out_ref.shape[1]
    groups = height // SUB
    _, strips = tail_rows(freq_local, height, half, border)
    lane = columns()
    to_lower = (lax.axis_index("freq") & NEAR_COLUMNS) != 0
    start = jnp.where(to_lower, 0, breadth - half)
    beside = pl.ds(pl.multiple_of(jnp.where(to_lower, half, half - LANES), LANES), LANES)
    rows = freq_local * 2 * height
    per = LANES // border
    strip = [jnp.zeros((SUB, LANES), jnp.float32) for _ in range(strips)]
    for f in range(freq_local):
        for part in range(2):
            row = (2 * f + part) * height
            for b in range(half // LANES):
                column = pl.ds(pl.multiple_of(start + LANES * b, LANES), LANES)
                out_ref[row : row + height, LANES * b : LANES * (b + 1)] = receiver_ref[f, part, :, column]
            for g in range(groups):
                value = receiver_ref[f, part, SUB * g : SUB * (g + 1), beside]
                value = jnp.where(to_lower, value, pltpu.roll(value, border, 1))
                i, at = divmod((2 * f + part) * groups + g, per)
                if at:
                    value = pltpu.roll(value, border * at, 1)
                strip[i] = jnp.where((lane >= border * at) & (lane < border * (at + 1)), value, strip[i])
    for i, value in enumerate(strip):
        tail_of(out_ref, rows, i)[...] = value
    scalars = [
        taps_ref[f, d, i] for f in range(freq_local) for d in range(len(directions)) for i in range(6)
    ] + [spectrum_ref[f, i] for f in range(freq_local) for i in range(2)]
    for b in range(-(-len(scalars) // LANES)):
        value = jnp.zeros((SUB, LANES), jnp.float32)
        for i, scalar in enumerate(scalars[LANES * b : LANES * (b + 1)]):
            value = jnp.where(lane == i, scalar, value)
        tail_of(out_ref, rows, strips + b)[...] = value


def prepare(freq_total, rank, first_column, owner_ref, position_ref, window_of, taps_of, wave_of, results):
    field_ref, taps_out_ref, rate_ref, turn_ref = results
    freq_local, _, _, blocks, height, _ = field_ref.shape
    groups = height // SUB
    lane = columns()
    row = lax.broadcasted_iota(jnp.int32, (SUB, LANES), 0)

    def number(f):
        return (rank * freq_local + f).astype(jnp.float32) + 1.0

    for f in range(freq_local):
        for d in range(len(directions)):
            for i in range(6):
                taps_out_ref[f, d, i] = jnp.broadcast_to(taps_of(f, d, i), (SUB, LANES))
        rate_ref[f] = jnp.full((SUB, LANES), number(f) * (lens_rate / freq_total), jnp.float32)
    spread_turn(owner_ref, turn_ref)

    for f in range(freq_local):
        for part in range(2):
            for g in range(groups):
                for b, value in enumerate(window_of(f, part, g)):
                    tile(field_ref, f, 1, part, b, g)[...] = -value if part else value

    src_row = position_ref[0].astype(jnp.float32)
    src_col = position_ref[1].astype(jnp.float32)
    waves = [(wave_of(f, 0), wave_of(f, 1)) for f in range(freq_local)]
    for g in range(groups):
        for b in range(blocks):
            d_row = (row + SUB * g).astype(jnp.float32) - src_row
            d_col = (lane * blocks + (first_column + b)).astype(jnp.float32) - src_col
            distance = jnp.sqrt(d_row * d_row + d_col * d_col + 1.0)
            amplitude = 1.0 / (1.0 + distance / (height / 4.0))
            for f, (w_re, w_im) in enumerate(waves):
                cos_value, sin_value = cos_sin(number(f) * (wave_rate / freq_total) * distance)
                base_re = amplitude * cos_value
                base_im = -amplitude * sin_value
                tile(field_ref, f, 0, 0, b, g)[...] = w_re * base_re - w_im * base_im
                tile(field_ref, f, 0, 1, b, g)[...] = w_re * base_im + w_im * base_re


def prepare_own_kernel(
    freq_total, owner_ref, position_ref, taps_ref, spectrum_ref, receiver_ref, packed_ref, *results
):
    blocks = results[0].shape[3]
    here = lax.axis_index("freq")
    first_column = jnp.where((here & NEAR_COLUMNS) != 0, receiver_ref.shape[3] - blocks * LANES, 0)

    def window_of(f, part, g):
        starts = [pl.multiple_of(first_column + LANES * b, LANES) for b in range(blocks)]
        return interleave(
            [receiver_ref[f, part, SUB * g : SUB * (g + 1), pl.ds(start, LANES)] for start in starts]
        )

    prepare(
        freq_total,
        here,
        first_column,
        owner_ref,
        position_ref,
        window_of,
        lambda f, d, i: taps_ref[f, d, i],
        lambda f, i: spectrum_ref[f, i],
        results,
    )


def prepare_near_kernel(freq_total, breadth, border, owner_ref, position_ref, packed_ref, *results):
    freq_local, _, _, blocks, height, _ = results[0].shape
    half = packed_ref.shape[1]
    groups = height // SUB
    here = lax.axis_index("freq")
    upper = (here & NEAR_COLUMNS) != 0
    first_column = jnp.where(upper, breadth - blocks * LANES, 0)
    rows = freq_local * 2 * height
    _, strips = tail_rows(freq_local, height, half, border)
    per = LANES // border
    taps_count = len(directions) * 6
    lane = columns()

    def main(f, part, g, b):
        row = (2 * f + part) * height + SUB * g
        return packed_ref[row : row + SUB, LANES * b : LANES * (b + 1)]

    def window_of(f, part, g):
        i, at = divmod((2 * f + part) * groups + g, per)
        strip = tail_of(packed_ref, rows, i)[...]
        mains = [main(f, part, g, b) for b in range(blocks - 1)]
        found = [strip if b == 0 else mains[b - 1] for b in range(blocks)]
        lower = mains + [strip]
        shifts = [None] * blocks
        shifts[0] = jnp.where(upper, border * (at + 1), 0)
        shifts[-1] = jnp.where(upper, 0, border * at)
        return interleave([jnp.where(upper, u, v) for u, v in zip(found, lower)], shifts)

    def scalar(i):
        value = tail_of(packed_ref, rows, strips + i // LANES)[...]
        return jnp.broadcast_to(value[:, i % LANES : i % LANES + 1], (SUB, LANES))

    prepare(
        freq_total,
        here ^ NEAR_COLUMNS,
        first_column,
        owner_ref,
        position_ref,
        window_of,
        lambda f, d, i: scalar(f * taps_count + 6 * d + i),
        lambda f, i: scalar(freq_local * taps_count + 2 * f + i),
        results,
    )


def migrate_kernel(
    freq_total,
    own_ref,
    own_taps_ref,
    own_rate_ref,
    near_ref,
    near_taps_ref,
    near_rate_ref,
    slab_ref,
    out_ref,
    a_ref,
    b_ref,
    v_ref,
    c_ref,
    taps_ref,
    rate_ref,
):
    freq_own = own_ref.shape[0]
    freq_local = 2 * freq_own
    levels, height, breadth = slab_ref.shape
    blocks = breadth // LANES
    groups = height // SUB
    lane = lax.broadcasted_iota(jnp.int32, (SUB, LANES), 1)
    not_first = lane > 0
    not_last = lane < LANES - 1

    def load(ref, f, field, part, block, group, shift=0):
        return tile(ref, f, field, part, block + REACH, group + 1, shift)[...]

    def store(ref, f, field, part, block, group, value):
        tile(ref, f, field, part, block + REACH, group + 1)[...] = value

    for side, (one_taps_ref, one_rate_ref) in enumerate(
        ((own_taps_ref, own_rate_ref), (near_taps_ref, near_rate_ref))
    ):
        for f in range(freq_own):
            rate_ref[side * freq_own + f] = one_rate_ref[f]
            for d in range(len(directions)):
                for i in range(6):
                    taps_ref[side * freq_own + f, d, i] = one_taps_ref[f, d, i]

    zero = jnp.zeros((SUB, LANES), jnp.float32)

    @pl.loop(0, freq_local)
    def _(f):
        for ref in (a_ref, b_ref):
            for field in range(2):
                for part in range(2):
                    for block in range(blocks + 2 * REACH):
                        tile(ref, f, field, part, block, 0)[...] = zero
                        tile(ref, f, field, part, block, groups + 1)[...] = zero

    def rows_of(g):
        return pl.ds(pl.multiple_of(SUB * g, SUB), SUB)

    def take_slab(t, g):
        rows = rows_of(g)
        loaded = [slab_ref[t, rows, LANES * b : LANES * (b + 1)] for b in range(blocks)]
        for b, value in enumerate(interleave(loaded)):
            v_ref[t, b, rows, :] = value

    def give_sum(t, g):
        rows = rows_of(g)
        for b, value in enumerate(deinterleave([c_ref[t, b, rows] for b in range(blocks)])):
            out_ref[t, rows, LANES * b : LANES * (b + 1)] = value * (1.0 / math.sqrt(freq_total))

    def beside(work, t, f):
        share = -(-groups // freq_local)
        for k in range(share):
            work(t, jnp.minimum(f * share + k, groups - 1))

    for g in range(groups):
        take_slab(0, g)

    def lens(t, get, first):
        step_rate = lens_rate / freq_total
        step = small_cos_sin if step_rate * greatest_slowness < math.pi / 4.0 else cos_sin
        for g in range(groups):
            for b in range(blocks):
                slow = v_ref[t, b, SUB * g : SUB * (g + 1), :]
                cos_value, sin_value = cos_sin(rate_ref[first] * slow)
                if freq_own > 1:
                    cos_step, sin_step = step(step_rate * slow)
                for f in range(freq_own):
                    if f:
                        cos_value, sin_value = (
                            cos_value * cos_step - sin_value * sin_step,
                            sin_value * cos_step + cos_value * sin_step,
                        )
                    for field in range(2):
                        re, im = get(first + f, field, 0, b, g), get(first + f, field, 1, b, g)
                        store(a_ref, first + f, field, 0, b, g, re * cos_value + im * sin_value)
                        store(a_ref, first + f, field, 1, b, g, im * cos_value - re * sin_value)

    def filtered(src, f, field, b, g, d, taps):
        step_x, step_y = directions[d]

        def at(part, k):
            return load(src, f, field, part, b + k * step_y, g, k * step_x)

        c0r, c0i, c1r, c1i, c2r, c2i = taps
        re, im = at(0, 0), at(1, 0)
        p1r, p1i = at(0, 1) + at(0, -1), at(1, 1) + at(1, -1)
        p2r, p2i = at(0, 2) + at(0, -2), at(1, 2) + at(1, -2)
        out_re = (re * c0r - im * c0i) + (p1r * c1r - p1i * c1i) + (p2r * c2r - p2i * c2i)
        out_im = (re * c0i + im * c0r) + (p1r * c1i + p1i * c1r) + (p2r * c2i + p2i * c2r)
        return out_re, out_im

    def sweep(src, dst, d, work=None, level=None):
        @pl.loop(0, freq_local)
        def _(f):
            taps = [taps_ref[f, d, i] for i in range(6)]
            if work is not None:
                beside(work, level, f)
            for field in range(2):
                for g in range(groups):
                    for b in range(blocks):
                        for part, value in enumerate(filtered(src, f, field, b, g, d, taps)):
                            store(dst, f, field, part, b, g, value)
                            if b < REACH:
                                edge = jnp.where(not_last, pltpu.roll(value, LANES - 1, 1), 0.0)
                                store(dst, f, field, part, b + blocks, g, edge)
                            if b >= blocks - REACH:
                                edge = jnp.where(not_first, pltpu.roll(value, 1, 1), 0.0)
                                store(dst, f, field, part, b - blocks, g, edge)

    def last_sweep(src, dst, d, t):
        @pl.loop(0, freq_local)
        def _(f):
            taps = [taps_ref[f, d, i] for i in range(6)]
            for g in range(groups):
                for b in range(blocks):
                    s_re, s_im = filtered(src, f, 0, b, g, d, taps)
                    r_re, r_im = filtered(src, f, 1, b, g, d, taps)
                    store(dst, f, 0, 0, b, g, s_re)
                    store(dst, f, 0, 1, b, g, s_im)
                    store(dst, f, 1, 0, b, g, r_re)
                    store(dst, f, 1, 1, b, g, r_im)
                    term = s_re * r_re - s_im * r_im
                    at = (t, b, slice(SUB * g, SUB * (g + 1)))
                    c_ref[at] = jnp.where(f == 0, term, c_ref[at] + term)

    def depth_step(t):
        sweep(a_ref, b_ref, 0, take_slab, jnp.minimum(t + 1, levels - 1))
        sweep(b_ref, a_ref, 1, give_sum, jnp.maximum(t - 1, 0))
        sweep(a_ref, b_ref, 2)
        last_sweep(b_ref, a_ref, 3, t)

    for side, ref in enumerate((own_ref, near_ref)):
        first = side * freq_own

        def surface(f, field, part, b, g, ref=ref, first=first):
            return tile(ref, f - first, field, part, b, g)[...]

        lens(0, surface, first)

    @pl.loop(0, levels)
    def _(t):
        @pl.when(t > 0)
        def _():
            @pl.loop(0, 2)
            def _(side):
                lens(t, lambda f, field, part, b, g: load(a_ref, f, field, part, b, g), side * freq_own)

        depth_step(t)

    for g in range(groups):
        give_sum(levels - 1, g)


SMEM = pl.BlockSpec(memory_space=pltpu.SMEM)
VMEM = pl.BlockSpec(memory_space=pltpu.VMEM)


def pack(taps, spectrum, receiver, slab, half, border):
    freq_local, _, height, _ = receiver.shape
    rows = freq_local * 2 * height + tail_rows(freq_local, height, half, border)[0]
    return pl.pallas_call(
        functools.partial(pack_kernel, border),
        out_shape=jax.ShapeDtypeStruct((rows, half), jnp.float32),
        in_specs=[SMEM, SMEM, VMEM, pl.BlockSpec(memory_space=pl.ANY)],
        out_specs=VMEM,
        cost_estimate=pl.CostEstimate(flops=0, bytes_accessed=8 * rows * half, transcendentals=0),
        compiler_params=pltpu.CompilerParams(vmem_limit_bytes=32 * 1024 * 1024),
    )(taps, spectrum, receiver, slab)


def prepared(kernel, shape, levels, width, specs, operands):
    freq_local, _, height, _ = shape
    cells = freq_local * height * width
    return pl.pallas_call(
        kernel,
        out_shape=(
            jax.ShapeDtypeStruct((freq_local, 2, 2, width // LANES, height, LANES), jnp.float32),
            jax.ShapeDtypeStruct((freq_local, len(directions), 6, SUB, LANES), jnp.float32),
            jax.ShapeDtypeStruct((freq_local, SUB, LANES), jnp.float32),
            jax.ShapeDtypeStruct((levels, SUB, LANES), jnp.int32),
        ),
        in_specs=specs,
        out_specs=(VMEM, VMEM, VMEM, VMEM),
        cost_estimate=pl.CostEstimate(flops=100 * cells, bytes_accessed=24 * cells, transcendentals=0),
        compiler_params=pltpu.CompilerParams(vmem_limit_bytes=32 * 1024 * 1024),
    )(*operands)


def migrate(own, near, slabs, freq_total):
    freq_own, _, _, blocks, height, _ = own[0].shape
    freq_local = 2 * freq_own
    levels = slabs.shape[0]
    state = pltpu.VMEM((freq_local, 2, 2, blocks + 2 * REACH, height + 2 * SUB, LANES), jnp.float32)
    return pl.pallas_call(
        functools.partial(migrate_kernel, freq_total),
        out_shape=jax.ShapeDtypeStruct(slabs.shape, jnp.float32),
        in_specs=[VMEM] * 7,
        out_specs=VMEM,
        scratch_shapes=[
            state,
            state,
            pltpu.VMEM((levels, blocks, height, LANES), jnp.float32),
            pltpu.VMEM((levels, blocks, height, LANES), jnp.float32),
            pltpu.VMEM((freq_local, len(directions), 6, SUB, LANES), jnp.float32),
            pltpu.VMEM((freq_local, SUB, LANES), jnp.float32),
        ],
        compiler_params=pltpu.CompilerParams(vmem_limit_bytes=32 * 1024 * 1024),
    )(*own, *near, slabs)


def exchange(value, mask, size):
    return lax.ppermute(value, "freq", [(i, i ^ mask) for i in range(size)])


def far_bits(size):
    found = []
    bit = 2 * NEAR_COLUMNS
    while bit < size:
        found.append((bit, bit | sum(b for b, _ in found)))
        bit *= 2
    return found


def rows_split(value, upper):
    half = value.shape[-2] // 2
    low, high = value[..., :half, :], value[..., half:, :]
    return jnp.where(upper, high, low), jnp.where(upper, low, high)


def columns_split(value, upper, width):
    low, high = value[..., :width], value[..., value.shape[-1] - width :]
    return jnp.where(upper, high, low), jnp.where(upper, low, high)


def joined(mine, other, upper, axis):
    return jnp.where(
        upper, jnp.concatenate([other, mine], axis=axis), jnp.concatenate([mine, other], axis=axis)
    )


def fetch_slabs(own, got, turns, rank, size, width):
    upper_rows = (rank & NEAR_ROWS) != 0
    upper_columns = (rank & NEAR_COLUMNS) != 0
    mine, _ = rows_split(own, upper_rows)
    got, _ = rows_split(got, upper_rows)
    held = jnp.stack([mine, got])
    mine, other = columns_split(held, upper_columns, width)
    held = jnp.concatenate([mine, exchange(other, NEAR_COLUMNS, size)], axis=0)
    wanted = turns[0][:, :1, :1] & (NEAR_ROWS | NEAR_COLUMNS)
    carried = jnp.broadcast_to(held[:1], (wanted.shape[0], *held.shape[1:]))
    for c in range(1, held.shape[0]):
        carried = jnp.where(wanted == c, held[c][None], carried)
    far = far_bits(size)
    for i, (bit, mask) in enumerate(far):
        got = exchange(carried, mask, size)
        turn = turns[1 if i == len(far) - 1 else 0][:, :1, :1]
        carried = jnp.where((turn & bit) == 0, carried, got)
    return joined(carried, exchange(carried, NEAR_ROWS, size), upper_rows, -2)


def sums_to_owner(partial, owners, rank, size, half):
    upper_rows = (rank & NEAR_ROWS) != 0
    upper_columns = (rank & NEAR_COLUMNS) != 0
    partial, _ = columns_split(partial, upper_columns, half)
    mine, other = rows_split(partial, upper_rows)
    carried = mine + exchange(other, NEAR_ROWS, size)
    for _, mask in far_bits(size):
        carried = carried + exchange(carried, mask, size)

    def slot(place):
        return jnp.sum(jnp.where((owners == place)[:, None, None], carried, 0.0), axis=0)

    mine = jnp.stack([slot(rank), slot(rank ^ NEAR_ROWS)])
    other = jnp.stack([slot(rank ^ NEAR_COLUMNS), slot(rank ^ NEAR_ROWS ^ NEAR_COLUMNS)])
    both = joined(mine, exchange(other, NEAR_COLUMNS, size), upper_columns, -1)
    return joined(both[0], exchange(both[1], NEAR_ROWS, size), upper_rows, -2)


def local(receiver_data, source_spectrum, filter_taps, slowness, depth_owner, source_position):
    freq_local, _, height, breadth = receiver_data.shape
    levels = depth_owner.shape[0]
    size = lax.axis_size("freq")
    rank = lax.axis_index("freq")
    freq_total = size * freq_local
    half = breadth // 2
    border = REACH * sum(1 for _, step_y in directions if step_y) * levels
    width = half + LANES
    shape = receiver_data.shape

    near_slab = exchange(slowness[0], NEAR_ROWS, size)
    packed = pack(
        filter_taps, source_spectrum, receiver_data, near_slab, half, border
    )
    arrived = exchange(packed, NEAR_COLUMNS, size)
    *own, own_turn = prepared(
        functools.partial(prepare_own_kernel, freq_total),
        shape,
        levels,
        width,
        [SMEM, SMEM, SMEM, SMEM, VMEM, pl.BlockSpec(memory_space=pl.ANY)],
        (depth_owner, source_position, filter_taps, source_spectrum, receiver_data, packed),
    )
    *near, near_turn = prepared(
        functools.partial(prepare_near_kernel, freq_total, breadth, border),
        shape,
        levels,
        width,
        [SMEM, SMEM, VMEM],
        (depth_owner, source_position, arrived),
    )
    turns = (own_turn, near_turn)
    slabs = fetch_slabs(slowness[0], near_slab, turns, rank, size, width)
    partial = migrate(own, near, slabs, freq_total)
    return sums_to_owner(partial, depth_owner, rank, size, half)[None]


def solution(mesh):
    return jax.shard_map(
        local,
        mesh=mesh,
        in_specs=(
            P(("shot", "freq"), None, None, None),
            P("freq", None),
            P("freq", None, None),
            P("freq", None, None),
            P("shot"),
            P("shot"),
        ),
        out_specs=P(("shot", "freq"), None, None),
        check_vma=False,
    )
```

```python
import functools
import math

import jax
import jax.numpy as jnp
from jax import lax
from jax.experimental import pallas as pl
from jax.experimental.pallas import tpu as pltpu
from jax.sharding import PartitionSpec as P

lens_rate = 3.0
wave_rate = 0.5
greatest_slowness = 2.0
directions = ((1, 0), (0, 1), (1, 1), (1, -1))
LANES = 128
SUB = 8
UNROLL = 2
REACH = 2
NEAR_ROWS = 1
NEAR_COLUMNS = 2
TWO_OVER_PI = 2.0 / math.pi
PI_2 = (1.5703125, 4.837512969970703125e-4, 7.54978995489188216e-8)


def small_cos_sin(r):
    r2 = r * r
    s = r + r * r2 * (-1.6666654611e-1 + r2 * (8.3321608736e-3 + r2 * -1.9515295891e-4))
    c = (1.0 - 0.5 * r2) + r2 * r2 * (
        4.166664568298827e-2 + r2 * (-1.388731625493765e-3 + r2 * 2.443315711809948e-5)
    )
    return c, s


def cos_sin(x):
    turns = jnp.floor(x * TWO_OVER_PI + 0.5)
    r = x - turns * PI_2[0]
    r = r - turns * PI_2[1]
    r = r - turns * PI_2[2]
    c, s = small_cos_sin(r)
    quadrant = turns.astype(jnp.int32)
    odd = (quadrant & 1) == 1
    cos_value = jnp.where(odd, s, c)
    sin_value = jnp.where(odd, c, s)
    cos_value = jnp.where(((quadrant + 1) & 2) == 2, -cos_value, cos_value)
    sin_value = jnp.where((quadrant & 2) == 2, -sin_value, sin_value)
    return cos_value, sin_value


def quotient(x, divisor):
    return jnp.floor((x.astype(jnp.float32) + 0.5) * (1.0 / divisor)).astype(jnp.int32)


def columns():
    return lax.broadcasted_iota(jnp.int32, (SUB, LANES), 1)


def interleave(blocks, shifts=None):
    count = len(blocks)
    out = []
    for c in range(count):
        column = columns() * count + c
        pick, source = column & (LANES - 1), column >> (LANES.bit_length() - 1)
        value = None
        for b in range(count):
            at = pick if shifts is None or shifts[b] is None else (pick + shifts[b]) & (LANES - 1)
            found = jnp.take_along_axis(blocks[b], at, axis=1)
            value = found if value is None else jnp.where(source == b, found, value)
        out.append(value)
    return out


def deinterleave(blocks):
    count = len(blocks)
    out = []
    for b in range(count):
        column = columns() + LANES * b
        pick = quotient(column, count)
        source = column - pick * count
        value = jnp.take_along_axis(blocks[0], pick, axis=1)
        for c in range(1, count):
            value = jnp.where(source == c, jnp.take_along_axis(blocks[c], pick, axis=1), value)
        out.append(value)
    return out


def tile(ref, f, field, part, block, group, shift=0):
    return ref.at[f, field, part, block, pl.ds(SUB * group + shift, SUB), :]


def spread_turn(owner_ref, turn_ref):
    for t in range(owner_ref.shape[0]):
        turn_ref[t] = jnp.full((SUB, LANES), owner_ref[t] ^ lax.axis_index("freq"), jnp.int32)


def tail_of(ref, rows, i):
    across = ref.shape[1] // LANES
    down = rows + SUB * (i // across)
    return ref.at[down : down + SUB, LANES * (i % across) : LANES * (i % across + 1)]


def tail_rows(freq_local, height, half, border):
    strips = -(-freq_local * 2 * (height // SUB) // (LANES // border))
    scalars = -(-freq_local * (len(directions) * 6 + 2) // LANES)
    return SUB * -(-(strips + scalars) // (half // LANES)), strips


def pack_kernel(border, taps_ref, spectrum_ref, receiver_ref, slab_ref, out_ref):
    freq_local, _, height, breadth = receiver_ref.shape
    half = out_ref.shape[1]
    groups = height // SUB
    _, strips = tail_rows(freq_local, height, half, border)
    lane = columns()
    to_lower = (lax.axis_index("freq") & NEAR_COLUMNS) != 0
    start = jnp.where(to_lower, 0, breadth - half)
    beside = pl.ds(pl.multiple_of(jnp.where(to_lower, half, half - LANES), LANES), LANES)
    rows = freq_local * 2 * height
    per = LANES // border
    strip = [jnp.zeros((SUB, LANES), jnp.float32) for _ in range(strips)]
    for f in range(freq_local):
        for part in range(2):
            row = (2 * f + part) * height
            for b in range(half // LANES):
                column = pl.ds(pl.multiple_of(start + LANES * b, LANES), LANES)
                out_ref[row : row + height, LANES * b : LANES * (b + 1)] = receiver_ref[f, part, :, column]
            for g in range(groups):
                value = receiver_ref[f, part, SUB * g : SUB * (g + 1), beside]
                value = jnp.where(to_lower, value, pltpu.roll(value, border, 1))
                i, at = divmod((2 * f + part) * groups + g, per)
                if at:
                    value = pltpu.roll(value, border * at, 1)
                strip[i] = jnp.where((lane >= border * at) & (lane < border * (at + 1)), value, strip[i])
    for i, value in enumerate(strip):
        tail_of(out_ref, rows, i)[...] = value
    scalars = [
        taps_ref[f, d, i] for f in range(freq_local) for d in range(len(directions)) for i in range(6)
    ] + [spectrum_ref[f, i] for f in range(freq_local) for i in range(2)]
    for b in range(-(-len(scalars) // LANES)):
        value = jnp.zeros((SUB, LANES), jnp.float32)
        for i, scalar in enumerate(scalars[LANES * b : LANES * (b + 1)]):
            value = jnp.where(lane == i, scalar, value)
        tail_of(out_ref, rows, strips + b)[...] = value


def prepare(freq_total, rank, first_column, owner_ref, position_ref, window_of, taps_of, wave_of, results):
    field_ref, taps_out_ref, rate_ref, turn_ref = results
    freq_local, _, _, blocks, height, _ = field_ref.shape
    groups = height // SUB
    lane = columns()
    row = lax.broadcasted_iota(jnp.int32, (SUB, LANES), 0)

    def number(f):
        return (rank * freq_local + f).astype(jnp.float32) + 1.0

    for f in range(freq_local):
        for d in range(len(directions)):
            for i in range(6):
                taps_out_ref[f, d, i] = jnp.broadcast_to(taps_of(f, d, i), (SUB, LANES))
        rate_ref[f] = jnp.full((SUB, LANES), number(f) * (lens_rate / freq_total), jnp.float32)
    spread_turn(owner_ref, turn_ref)

    for f in range(freq_local):
        for part in range(2):
            for g in range(groups):
                for b, value in enumerate(window_of(f, part, g)):
                    tile(field_ref, f, 1, part, b, g)[...] = -value if part else value

    src_row = position_ref[0].astype(jnp.float32)
    src_col = position_ref[1].astype(jnp.float32)
    waves = [(wave_of(f, 0), wave_of(f, 1)) for f in range(freq_local)]
    for g in range(groups):
        for b in range(blocks):
            d_row = (row + SUB * g).astype(jnp.float32) - src_row
            d_col = (lane * blocks + (first_column + b)).astype(jnp.float32) - src_col
            distance = jnp.sqrt(d_row * d_row + d_col * d_col + 1.0)
            amplitude = 1.0 / (1.0 + distance / (height / 4.0))
            for f, (w_re, w_im) in enumerate(waves):
                cos_value, sin_value = cos_sin(number(f) * (wave_rate / freq_total) * distance)
                base_re = amplitude * cos_value
                base_im = -amplitude * sin_value
                tile(field_ref, f, 0, 0, b, g)[...] = w_re * base_re - w_im * base_im
                tile(field_ref, f, 0, 1, b, g)[...] = w_re * base_im + w_im * base_re


def prepare_own_kernel(
    freq_total, owner_ref, position_ref, taps_ref, spectrum_ref, receiver_ref, packed_ref, *results
):
    blocks = results[0].shape[3]
    here = lax.axis_index("freq")
    first_column = jnp.where((here & NEAR_COLUMNS) != 0, receiver_ref.shape[3] - blocks * LANES, 0)

    def window_of(f, part, g):
        starts = [pl.multiple_of(first_column + LANES * b, LANES) for b in range(blocks)]
        return interleave(
            [receiver_ref[f, part, SUB * g : SUB * (g + 1), pl.ds(start, LANES)] for start in starts]
        )

    prepare(
        freq_total,
        here,
        first_column,
        owner_ref,
        position_ref,
        window_of,
        lambda f, d, i: taps_ref[f, d, i],
        lambda f, i: spectrum_ref[f, i],
        results,
    )


def prepare_near_kernel(freq_total, breadth, border, owner_ref, position_ref, packed_ref, *results):
    freq_local, _, _, blocks, height, _ = results[0].shape
    half = packed_ref.shape[1]
    groups = height // SUB
    here = lax.axis_index("freq")
    upper = (here & NEAR_COLUMNS) != 0
    first_column = jnp.where(upper, breadth - blocks * LANES, 0)
    rows = freq_local * 2 * height
    _, strips = tail_rows(freq_local, height, half, border)
    per = LANES // border
    taps_count = len(directions) * 6
    lane = columns()

    def main(f, part, g, b):
        row = (2 * f + part) * height + SUB * g
        return packed_ref[row : row + SUB, LANES * b : LANES * (b + 1)]

    def window_of(f, part, g):
        i, at = divmod((2 * f + part) * groups + g, per)
        strip = tail_of(packed_ref, rows, i)[...]
        mains = [main(f, part, g, b) for b in range(blocks - 1)]
        found = [strip if b == 0 else mains[b - 1] for b in range(blocks)]
        lower = mains + [strip]
        shifts = [None] * blocks
        shifts[0] = jnp.where(upper, border * (at + 1), 0)
        shifts[-1] = jnp.where(upper, 0, border * at)
        return interleave([jnp.where(upper, u, v) for u, v in zip(found, lower)], shifts)

    def scalar(i):
        value = tail_of(packed_ref, rows, strips + i // LANES)[...]
        return jnp.broadcast_to(value[:, i % LANES : i % LANES + 1], (SUB, LANES))

    prepare(
        freq_total,
        here ^ NEAR_COLUMNS,
        first_column,
        owner_ref,
        position_ref,
        window_of,
        lambda f, d, i: scalar(f * taps_count + 6 * d + i),
        lambda f, i: scalar(freq_local * taps_count + 2 * f + i),
        results,
    )


def migrate_kernel(
    freq_total,
    own_ref,
    own_taps_ref,
    own_rate_ref,
    near_ref,
    near_taps_ref,
    near_rate_ref,
    slab_ref,
    out_ref,
    a_ref,
    b_ref,
    v_ref,
    c_ref,
    taps_ref,
    rate_ref,
):
    freq_own = own_ref.shape[0]
    freq_local = 2 * freq_own
    levels, height, breadth = slab_ref.shape
    blocks = breadth // LANES
    groups = height // SUB
    lane = lax.broadcasted_iota(jnp.int32, (SUB, LANES), 1)
    not_first = lane > 0
    not_last = lane < LANES - 1

    def load(ref, f, field, part, block, group, shift=0):
        return tile(ref, f, field, part, block + REACH, group + 1, shift)[...]

    def store(ref, f, field, part, block, group, value):
        tile(ref, f, field, part, block + REACH, group + 1)[...] = value

    for side, (one_taps_ref, one_rate_ref) in enumerate(
        ((own_taps_ref, own_rate_ref), (near_taps_ref, near_rate_ref))
    ):
        for f in range(freq_own):
            rate_ref[side * freq_own + f] = one_rate_ref[f]
            for d in range(len(directions)):
                for i in range(6):
                    taps_ref[side * freq_own + f, d, i] = one_taps_ref[f, d, i]

    zero = jnp.zeros((SUB, LANES), jnp.float32)

    @pl.loop(0, freq_local)
    def _(f):
        for ref in (a_ref, b_ref):
            for field in range(2):
                for part in range(2):
                    for block in range(blocks + 2 * REACH):
                        tile(ref, f, field, part, block, 0)[...] = zero
                        tile(ref, f, field, part, block, groups + 1)[...] = zero

    def rows_of(g):
        return pl.ds(pl.multiple_of(SUB * g, SUB), SUB)

    def take_slab(t, g):
        rows = rows_of(g)
        loaded = [slab_ref[t, rows, LANES * b : LANES * (b + 1)] for b in range(blocks)]
        for b, value in enumerate(interleave(loaded)):
            v_ref[t, b, rows, :] = value

    def give_sum(t, g):
        rows = rows_of(g)
        for b, value in enumerate(deinterleave([c_ref[t, b, rows] for b in range(blocks)])):
            out_ref[t, rows, LANES * b : LANES * (b + 1)] = value * (1.0 / math.sqrt(freq_total))

    def beside(work, t, f):
        share = -(-groups // freq_local)
        for k in range(share):
            work(t, jnp.minimum(f * share + k, groups - 1))

    for g in range(groups):
        take_slab(0, g)

    def lens(t, get, first):
        step_rate = lens_rate / freq_total
        step = small_cos_sin if step_rate * greatest_slowness < math.pi / 4.0 else cos_sin
        for g in range(groups):
            for b in range(blocks):
                slow = v_ref[t, b, SUB * g : SUB * (g + 1), :]
                cos_value, sin_value = cos_sin(rate_ref[first] * slow)
                if freq_own > 1:
                    cos_step, sin_step = step(step_rate * slow)
                for f in range(freq_own):
                    if f:
                        cos_value, sin_value = (
                            cos_value * cos_step - sin_value * sin_step,
                            sin_value * cos_step + cos_value * sin_step,
                        )
                    for field in range(2):
                        re, im = get(first + f, field, 0, b, g), get(first + f, field, 1, b, g)
                        store(a_ref, first + f, field, 0, b, g, re * cos_value + im * sin_value)
                        store(a_ref, first + f, field, 1, b, g, im * cos_value - re * sin_value)

    def filtered(src, f, field, b, g, d, taps):
        step_x, step_y = directions[d]

        def at(part, k):
            return load(src, f, field, part, b + k * step_y, g, k * step_x)

        c0r, c0i, c1r, c1i, c2r, c2i = taps
        re, im = at(0, 0), at(1, 0)
        p1r, p1i = at(0, 1) + at(0, -1), at(1, 1) + at(1, -1)
        p2r, p2i = at(0, 2) + at(0, -2), at(1, 2) + at(1, -2)
        both = (re + im) * c0r + (p1r + p1i) * c1r + (p2r + p2i) * c2r
        from_re = re * (c0i - c0r) + p1r * (c1i - c1r) + p2r * (c2i - c2r)
        from_im = im * (c0r + c0i) + p1i * (c1r + c1i) + p2i * (c2r + c2i)
        return both - from_im, both + from_re

    def sweep(src, dst, d, work=None, level=None):
        @pl.loop(0, freq_local, unroll=UNROLL)
        def _(f):
            taps = [taps_ref[f, d, i] for i in range(6)]
            if work is not None:
                beside(work, level, f)
            for field in range(2):
                for g in range(groups):
                    for b in range(blocks):
                        for part, value in enumerate(filtered(src, f, field, b, g, d, taps)):
                            store(dst, f, field, part, b, g, value)
                            if b < REACH:
                                edge = jnp.where(not_last, pltpu.roll(value, LANES - 1, 1), 0.0)
                                store(dst, f, field, part, b + blocks, g, edge)
                            if b >= blocks - REACH:
                                edge = jnp.where(not_first, pltpu.roll(value, 1, 1), 0.0)
                                store(dst, f, field, part, b - blocks, g, edge)

    def last_sweep(src, dst, d, t):
        @pl.loop(0, freq_local, unroll=UNROLL)
        def _(f):
            taps = [taps_ref[f, d, i] for i in range(6)]
            for g in range(groups):
                for b in range(blocks):
                    s_re, s_im = filtered(src, f, 0, b, g, d, taps)
                    r_re, r_im = filtered(src, f, 1, b, g, d, taps)
                    store(dst, f, 0, 0, b, g, s_re)
                    store(dst, f, 0, 1, b, g, s_im)
                    store(dst, f, 1, 0, b, g, r_re)
                    store(dst, f, 1, 1, b, g, r_im)
                    term = s_re * r_re - s_im * r_im
                    at = (t, b, slice(SUB * g, SUB * (g + 1)))
                    c_ref[at] = jnp.where(f == 0, term, c_ref[at] + term)

    def depth_step(t):
        sweep(a_ref, b_ref, 0, take_slab, jnp.minimum(t + 1, levels - 1))
        sweep(b_ref, a_ref, 1, give_sum, jnp.maximum(t - 1, 0))
        sweep(a_ref, b_ref, 2)
        last_sweep(b_ref, a_ref, 3, t)

    for side, ref in enumerate((own_ref, near_ref)):
        first = side * freq_own

        def surface(f, field, part, b, g, ref=ref, first=first):
            return tile(ref, f - first, field, part, b, g)[...]

        lens(0, surface, first)

    @pl.loop(0, levels)
    def _(t):
        @pl.when(t > 0)
        def _():
            @pl.loop(0, 2)
            def _(side):
                lens(t, lambda f, field, part, b, g: load(a_ref, f, field, part, b, g), side * freq_own)

        depth_step(t)

    for g in range(groups):
        give_sum(levels - 1, g)


SMEM = pl.BlockSpec(memory_space=pltpu.SMEM)
VMEM = pl.BlockSpec(memory_space=pltpu.VMEM)


def pack(taps, spectrum, receiver, slab, half, border):
    freq_local, _, height, _ = receiver.shape
    rows = freq_local * 2 * height + tail_rows(freq_local, height, half, border)[0]
    return pl.pallas_call(
        functools.partial(pack_kernel, border),
        out_shape=jax.ShapeDtypeStruct((rows, half), jnp.float32),
        in_specs=[SMEM, SMEM, VMEM, pl.BlockSpec(memory_space=pl.ANY)],
        out_specs=VMEM,
        cost_estimate=pl.CostEstimate(flops=0, bytes_accessed=8 * rows * half, transcendentals=0),
        compiler_params=pltpu.CompilerParams(vmem_limit_bytes=32 * 1024 * 1024),
    )(taps, spectrum, receiver, slab)


def prepared(kernel, shape, levels, width, specs, operands):
    freq_local, _, height, _ = shape
    cells = freq_local * height * width
    return pl.pallas_call(
        kernel,
        out_shape=(
            jax.ShapeDtypeStruct((freq_local, 2, 2, width // LANES, height, LANES), jnp.float32),
            jax.ShapeDtypeStruct((freq_local, len(directions), 6, SUB, LANES), jnp.float32),
            jax.ShapeDtypeStruct((freq_local, SUB, LANES), jnp.float32),
            jax.ShapeDtypeStruct((levels, SUB, LANES), jnp.int32),
        ),
        in_specs=specs,
        out_specs=(VMEM, VMEM, VMEM, VMEM),
        cost_estimate=pl.CostEstimate(flops=100 * cells, bytes_accessed=24 * cells, transcendentals=0),
        compiler_params=pltpu.CompilerParams(vmem_limit_bytes=32 * 1024 * 1024),
    )(*operands)


def migrate(own, near, slabs, freq_total):
    freq_own, _, _, blocks, height, _ = own[0].shape
    freq_local = 2 * freq_own
    levels = slabs.shape[0]
    state = pltpu.VMEM((freq_local, 2, 2, blocks + 2 * REACH, height + 2 * SUB, LANES), jnp.float32)
    return pl.pallas_call(
        functools.partial(migrate_kernel, freq_total),
        out_shape=jax.ShapeDtypeStruct(slabs.shape, jnp.float32),
        in_specs=[VMEM] * 7,
        out_specs=VMEM,
        scratch_shapes=[
            state,
            state,
            pltpu.VMEM((levels, blocks, height, LANES), jnp.float32),
            pltpu.VMEM((levels, blocks, height, LANES), jnp.float32),
            pltpu.VMEM((freq_local, len(directions), 6, SUB, LANES), jnp.float32),
            pltpu.VMEM((freq_local, SUB, LANES), jnp.float32),
        ],
        compiler_params=pltpu.CompilerParams(vmem_limit_bytes=32 * 1024 * 1024),
    )(*own, *near, slabs)


def exchange(value, mask, size):
    return lax.ppermute(value, "freq", [(i, i ^ mask) for i in range(size)])


def far_bits(size):
    found = []
    bit = 2 * NEAR_COLUMNS
    while bit < size:
        found.append((bit, bit | sum(b for b, _ in found)))
        bit *= 2
    return found


def rows_split(value, upper):
    half = value.shape[-2] // 2
    low, high = value[..., :half, :], value[..., half:, :]
    return jnp.where(upper, high, low), jnp.where(upper, low, high)


def columns_split(value, upper, width):
    low, high = value[..., :width], value[..., value.shape[-1] - width :]
    return jnp.where(upper, high, low), jnp.where(upper, low, high)


def joined(mine, other, upper, axis):
    return jnp.where(
        upper, jnp.concatenate([other, mine], axis=axis), jnp.concatenate([mine, other], axis=axis)
    )


def fetch_slabs(own, got, turns, rank, size, width):
    upper_rows = (rank & NEAR_ROWS) != 0
    upper_columns = (rank & NEAR_COLUMNS) != 0
    mine, _ = rows_split(own, upper_rows)
    got, _ = rows_split(got, upper_rows)
    held = jnp.stack([mine, got])
    mine, other = columns_split(held, upper_columns, width)
    held = jnp.concatenate([mine, exchange(other, NEAR_COLUMNS, size)], axis=0)
    wanted = turns[0][:, :1, :1] & (NEAR_ROWS | NEAR_COLUMNS)
    carried = jnp.broadcast_to(held[:1], (wanted.shape[0], *held.shape[1:]))
    for c in range(1, held.shape[0]):
        carried = jnp.where(wanted == c, held[c][None], carried)
    far = far_bits(size)
    for i, (bit, mask) in enumerate(far):
        got = exchange(carried, mask, size)
        turn = turns[1 if i == len(far) - 1 else 0][:, :1, :1]
        carried = jnp.where((turn & bit) == 0, carried, got)
    return joined(carried, exchange(carried, NEAR_ROWS, size), upper_rows, -2)


def sums_to_owner(partial, owners, rank, size, half):
    upper_rows = (rank & NEAR_ROWS) != 0
    upper_columns = (rank & NEAR_COLUMNS) != 0
    partial, _ = columns_split(partial, upper_columns, half)
    mine, other = rows_split(partial, upper_rows)
    carried = mine + exchange(other, NEAR_ROWS, size)
    for _, mask in far_bits(size):
        carried = carried + exchange(carried, mask, size)

    def slot(place):
        return jnp.sum(jnp.where((owners == place)[:, None, None], carried, 0.0), axis=0)

    mine = jnp.stack([slot(rank), slot(rank ^ NEAR_ROWS)])
    other = jnp.stack([slot(rank ^ NEAR_COLUMNS), slot(rank ^ NEAR_ROWS ^ NEAR_COLUMNS)])
    both = joined(mine, exchange(other, NEAR_COLUMNS, size), upper_columns, -1)
    return joined(both[0], exchange(both[1], NEAR_ROWS, size), upper_rows, -2)


def local(receiver_data, source_spectrum, filter_taps, slowness, depth_owner, source_position):
    freq_local, _, height, breadth = receiver_data.shape
    levels = depth_owner.shape[0]
    size = lax.axis_size("freq")
    rank = lax.axis_index("freq")
    freq_total = size * freq_local
    half = breadth // 2
    border = REACH * sum(1 for _, step_y in directions if step_y) * levels
    width = half + LANES
    shape = receiver_data.shape

    near_slab = exchange(slowness[0], NEAR_ROWS, size)
    packed = pack(
        filter_taps, source_spectrum, receiver_data, near_slab, half, border
    )
    arrived = exchange(packed, NEAR_COLUMNS, size)
    *own, own_turn = prepared(
        functools.partial(prepare_own_kernel, freq_total),
        shape,
        levels,
        width,
        [SMEM, SMEM, SMEM, SMEM, VMEM, pl.BlockSpec(memory_space=pl.ANY)],
        (depth_owner, source_position, filter_taps, source_spectrum, receiver_data, packed),
    )
    *near, near_turn = prepared(
        functools.partial(prepare_near_kernel, freq_total, breadth, border),
        shape,
        levels,
        width,
        [SMEM, SMEM, VMEM],
        (depth_owner, source_position, arrived),
    )
    turns = (own_turn, near_turn)
    slabs = fetch_slabs(slowness[0], near_slab, turns, rank, size, width)
    partial = migrate(own, near, slabs, freq_total)
    return sums_to_owner(partial, depth_owner, rank, size, half)[None]


def solution(mesh):
    return jax.shard_map(
        local,
        mesh=mesh,
        in_specs=(
            P(("shot", "freq"), None, None, None),
            P("freq", None),
            P("freq", None, None),
            P("freq", None, None),
            P("shot"),
            P("shot"),
        ),
        out_specs=P(("shot", "freq"), None, None),
        check_vma=False,
    )
```

```python
import functools
import math

import jax
import jax.numpy as jnp
from jax import lax
from jax.experimental import pallas as pl
from jax.experimental.pallas import tpu as pltpu
from jax.sharding import PartitionSpec as P

lens_rate = 3.0
wave_rate = 0.5
greatest_slowness = 2.0
directions = ((1, 0), (0, 1), (1, 1), (1, -1))
LANES = 128
SUB = 8
UNROLL = 2
REACH = 2
NEAR_ROWS = 1
NEAR_COLUMNS = 2
TWO_OVER_PI = 2.0 / math.pi
PI_2 = (1.5703125, 4.837512969970703125e-4, 7.54978995489188216e-8)


def small_cos_sin(r):
    r2 = r * r
    s = r + r * r2 * (-1.6666654611e-1 + r2 * (8.3321608736e-3 + r2 * -1.9515295891e-4))
    c = (1.0 - 0.5 * r2) + r2 * r2 * (
        4.166664568298827e-2 + r2 * (-1.388731625493765e-3 + r2 * 2.443315711809948e-5)
    )
    return c, s


def cos_sin(x):
    turns = jnp.floor(x * TWO_OVER_PI + 0.5)
    r = x - turns * PI_2[0]
    r = r - turns * PI_2[1]
    r = r - turns * PI_2[2]
    c, s = small_cos_sin(r)
    quadrant = turns.astype(jnp.int32)
    odd = (quadrant & 1) == 1
    cos_value = jnp.where(odd, s, c)
    sin_value = jnp.where(odd, c, s)
    cos_value = jnp.where(((quadrant + 1) & 2) == 2, -cos_value, cos_value)
    sin_value = jnp.where((quadrant & 2) == 2, -sin_value, sin_value)
    return cos_value, sin_value


def quotient(x, divisor):
    return jnp.floor((x.astype(jnp.float32) + 0.5) * (1.0 / divisor)).astype(jnp.int32)


def columns():
    return lax.broadcasted_iota(jnp.int32, (SUB, LANES), 1)


def interleave(blocks, shifts=None):
    count = len(blocks)
    out = []
    for c in range(count):
        column = columns() * count + c
        pick, source = column & (LANES - 1), column >> (LANES.bit_length() - 1)
        value = None
        for b in range(count):
            at = pick if shifts is None or shifts[b] is None else (pick + shifts[b]) & (LANES - 1)
            found = jnp.take_along_axis(blocks[b], at, axis=1)
            value = found if value is None else jnp.where(source == b, found, value)
        out.append(value)
    return out


def deinterleave(blocks):
    count = len(blocks)
    out = []
    for b in range(count):
        column = columns() + LANES * b
        pick = quotient(column, count)
        source = column - pick * count
        value = jnp.take_along_axis(blocks[0], pick, axis=1)
        for c in range(1, count):
            value = jnp.where(source == c, jnp.take_along_axis(blocks[c], pick, axis=1), value)
        out.append(value)
    return out


def tile(ref, f, field, part, block, group, shift=0):
    return ref.at[f, field, part, block, pl.ds(SUB * group + shift, SUB), :]


def spread_turn(owner_ref, turn_ref):
    for t in range(owner_ref.shape[0]):
        turn_ref[t] = jnp.full((SUB, LANES), owner_ref[t] ^ lax.axis_index("freq"), jnp.int32)


def tail_of(ref, rows, i):
    across = ref.shape[1] // LANES
    down = rows + SUB * (i // across)
    return ref.at[down : down + SUB, LANES * (i % across) : LANES * (i % across + 1)]


def tail_rows(freq_local, height, half, border):
    strips = -(-freq_local * 2 * (height // SUB) // (LANES // border))
    scalars = -(-freq_local * (len(directions) * 6 + 2) // LANES)
    return SUB * -(-(strips + scalars) // (half // LANES)), strips


def pack_kernel(border, taps_ref, spectrum_ref, receiver_ref, slab_ref, out_ref):
    freq_local, _, height, breadth = receiver_ref.shape
    half = out_ref.shape[1]
    groups = height // SUB
    _, strips = tail_rows(freq_local, height, half, border)
    lane = columns()
    to_lower = (lax.axis_index("freq") & NEAR_COLUMNS) != 0
    start = jnp.where(to_lower, 0, breadth - half)
    beside = pl.ds(pl.multiple_of(jnp.where(to_lower, half, half - LANES), LANES), LANES)
    rows = freq_local * 2 * height
    per = LANES // border
    strip = [jnp.zeros((SUB, LANES), jnp.float32) for _ in range(strips)]
    for f in range(freq_local):
        for part in range(2):
            row = (2 * f + part) * height
            for b in range(half // LANES):
                column = pl.ds(pl.multiple_of(start + LANES * b, LANES), LANES)
                out_ref[row : row + height, LANES * b : LANES * (b + 1)] = receiver_ref[f, part, :, column]
            for g in range(groups):
                value = receiver_ref[f, part, SUB * g : SUB * (g + 1), beside]
                value = jnp.where(to_lower, value, pltpu.roll(value, border, 1))
                i, at = divmod((2 * f + part) * groups + g, per)
                if at:
                    value = pltpu.roll(value, border * at, 1)
                strip[i] = jnp.where((lane >= border * at) & (lane < border * (at + 1)), value, strip[i])
    for i, value in enumerate(strip):
        tail_of(out_ref, rows, i)[...] = value
    scalars = [
        taps_ref[f, d, i] for f in range(freq_local) for d in range(len(directions)) for i in range(6)
    ] + [spectrum_ref[f, i] for f in range(freq_local) for i in range(2)]
    for b in range(-(-len(scalars) // LANES)):
        value = jnp.zeros((SUB, LANES), jnp.float32)
        for i, scalar in enumerate(scalars[LANES * b : LANES * (b + 1)]):
            value = jnp.where(lane == i, scalar, value)
        tail_of(out_ref, rows, strips + b)[...] = value


def prepare(freq_total, rank, first_column, owner_ref, position_ref, window_of, taps_of, wave_of, results):
    field_ref, taps_out_ref, rate_ref, turn_ref = results
    freq_local, _, _, blocks, height, _ = field_ref.shape
    groups = height // SUB
    lane = columns()
    row = lax.broadcasted_iota(jnp.int32, (SUB, LANES), 0)

    def number(f):
        return (rank * freq_local + f).astype(jnp.float32) + 1.0

    for f in range(freq_local):
        for d in range(len(directions)):
            for i in range(6):
                taps_out_ref[f, d, i] = jnp.broadcast_to(taps_of(f, d, i), (SUB, LANES))
        rate_ref[f] = jnp.full((SUB, LANES), number(f) * (lens_rate / freq_total), jnp.float32)
    spread_turn(owner_ref, turn_ref)

    for f in range(freq_local):
        for part in range(2):
            for g in range(groups):
                for b, value in enumerate(window_of(f, part, g)):
                    tile(field_ref, f, 1, part, b, g)[...] = -value if part else value

    src_row = position_ref[0].astype(jnp.float32)
    src_col = position_ref[1].astype(jnp.float32)
    waves = [(wave_of(f, 0), wave_of(f, 1)) for f in range(freq_local)]
    for g in range(groups):
        for b in range(blocks):
            d_row = (row + SUB * g).astype(jnp.float32) - src_row
            d_col = (lane * blocks + (first_column + b)).astype(jnp.float32) - src_col
            distance = jnp.sqrt(d_row * d_row + d_col * d_col + 1.0)
            amplitude = 1.0 / (1.0 + distance / (height / 4.0))
            for f, (w_re, w_im) in enumerate(waves):
                cos_value, sin_value = cos_sin(number(f) * (wave_rate / freq_total) * distance)
                base_re = amplitude * cos_value
                base_im = -amplitude * sin_value
                tile(field_ref, f, 0, 0, b, g)[...] = w_re * base_re - w_im * base_im
                tile(field_ref, f, 0, 1, b, g)[...] = w_re * base_im + w_im * base_re


def prepare_own_kernel(
    freq_total, owner_ref, position_ref, taps_ref, spectrum_ref, receiver_ref, packed_ref, *results
):
    blocks = results[0].shape[3]
    here = lax.axis_index("freq")
    first_column = jnp.where((here & NEAR_COLUMNS) != 0, receiver_ref.shape[3] - blocks * LANES, 0)

    def window_of(f, part, g):
        starts = [pl.multiple_of(first_column + LANES * b, LANES) for b in range(blocks)]
        return interleave(
            [receiver_ref[f, part, SUB * g : SUB * (g + 1), pl.ds(start, LANES)] for start in starts]
        )

    prepare(
        freq_total,
        here,
        first_column,
        owner_ref,
        position_ref,
        window_of,
        lambda f, d, i: taps_ref[f, d, i],
        lambda f, i: spectrum_ref[f, i],
        results,
    )


def prepare_near_kernel(freq_total, breadth, border, owner_ref, position_ref, packed_ref, *results):
    freq_local, _, _, blocks, height, _ = results[0].shape
    half = packed_ref.shape[1]
    groups = height // SUB
    here = lax.axis_index("freq")
    upper = (here & NEAR_COLUMNS) != 0
    first_column = jnp.where(upper, breadth - blocks * LANES, 0)
    rows = freq_local * 2 * height
    _, strips = tail_rows(freq_local, height, half, border)
    per = LANES // border
    taps_count = len(directions) * 6
    lane = columns()

    def main(f, part, g, b):
        row = (2 * f + part) * height + SUB * g
        return packed_ref[row : row + SUB, LANES * b : LANES * (b + 1)]

    def window_of(f, part, g):
        i, at = divmod((2 * f + part) * groups + g, per)
        strip = tail_of(packed_ref, rows, i)[...]
        mains = [main(f, part, g, b) for b in range(blocks - 1)]
        found = [strip if b == 0 else mains[b - 1] for b in range(blocks)]
        lower = mains + [strip]
        shifts = [None] * blocks
        shifts[0] = jnp.where(upper, border * (at + 1), 0)
        shifts[-1] = jnp.where(upper, 0, border * at)
        return interleave([jnp.where(upper, u, v) for u, v in zip(found, lower)], shifts)

    def scalar(i):
        value = tail_of(packed_ref, rows, strips + i // LANES)[...]
        return jnp.broadcast_to(value[:, i % LANES : i % LANES + 1], (SUB, LANES))

    prepare(
        freq_total,
        here ^ NEAR_COLUMNS,
        first_column,
        owner_ref,
        position_ref,
        window_of,
        lambda f, d, i: scalar(f * taps_count + 6 * d + i),
        lambda f, i: scalar(freq_local * taps_count + 2 * f + i),
        results,
    )


def migrate_kernel(
    freq_total,
    own_ref,
    own_taps_ref,
    own_rate_ref,
    near_ref,
    near_taps_ref,
    near_rate_ref,
    slab_ref,
    out_ref,
    a_ref,
    b_ref,
    v_ref,
    c_ref,
    taps_ref,
    rate_ref,
):
    freq_own = own_ref.shape[0]
    freq_local = 2 * freq_own
    levels, height, breadth = slab_ref.shape
    blocks = breadth // LANES
    groups = height // SUB
    lane = lax.broadcasted_iota(jnp.int32, (SUB, LANES), 1)
    not_first = lane > 0
    not_last = lane < LANES - 1

    def load(ref, f, field, part, block, group, shift=0):
        return tile(ref, f, field, part, block + REACH, group + 1, shift)[...]

    def store(ref, f, field, part, block, group, value):
        tile(ref, f, field, part, block + REACH, group + 1)[...] = value

    for side, (one_taps_ref, one_rate_ref) in enumerate(
        ((own_taps_ref, own_rate_ref), (near_taps_ref, near_rate_ref))
    ):
        for f in range(freq_own):
            rate_ref[side * freq_own + f] = one_rate_ref[f]
            for d in range(len(directions)):
                for i in range(6):
                    taps_ref[side * freq_own + f, d, i] = one_taps_ref[f, d, i]

    zero = jnp.zeros((SUB, LANES), jnp.float32)

    @pl.loop(0, freq_local)
    def _(f):
        for ref in (a_ref, b_ref):
            for field in range(2):
                for part in range(2):
                    for block in range(blocks + 2 * REACH):
                        tile(ref, f, field, part, block, 0)[...] = zero
                        tile(ref, f, field, part, block, groups + 1)[...] = zero

    def rows_of(g):
        return pl.ds(pl.multiple_of(SUB * g, SUB), SUB)

    def take_slab(t, g):
        rows = rows_of(g)
        loaded = [slab_ref[t, rows, LANES * b : LANES * (b + 1)] for b in range(blocks)]
        for b, value in enumerate(interleave(loaded)):
            v_ref[t, b, rows, :] = value

    def give_sum(t, g):
        rows = rows_of(g)
        for b, value in enumerate(deinterleave([c_ref[t, b, rows] for b in range(blocks)])):
            out_ref[t, rows, LANES * b : LANES * (b + 1)] = value * (1.0 / math.sqrt(freq_total))

    def beside(work, t, f):
        share = -(-groups // freq_local)
        for k in range(share):
            work(t, jnp.minimum(f * share + k, groups - 1))

    for g in range(groups):
        take_slab(0, g)

    def lens(t, get):
        step_rate = lens_rate / freq_total
        step = small_cos_sin if step_rate * greatest_slowness < math.pi / 4.0 else cos_sin
        apart = NEAR_COLUMNS * freq_own
        side = jnp.where((lax.axis_index("freq") & NEAR_COLUMNS) != 0, -1.0, 1.0)

        def plus(one, other):
            return one[0] * other[0] - one[1] * other[1], one[1] * other[0] + one[0] * other[1]

        for g in range(groups):
            for b in range(blocks):
                slow = v_ref[t, b, SUB * g : SUB * (g + 1), :]
                by_one = step(step_rate * slow)
                far = by_one
                if apart & (apart - 1) == 0:
                    for _ in range(apart.bit_length() - 1):
                        far = far[0] * far[0] - far[1] * far[1], 2.0 * far[0] * far[1]
                else:
                    far = cos_sin(apart * step_rate * slow)
                own = [cos_sin(rate_ref[0] * slow)]
                near = [plus(own[0], (far[0], side * far[1]))]
                for _ in range(1, freq_own):
                    own.append(plus(own[-1], by_one))
                    near.append(plus(near[-1], by_one))
                for f, (cos_value, sin_value) in enumerate(own + near):
                    for field in range(2):
                        re, im = get(f, field, 0, b, g), get(f, field, 1, b, g)
                        store(a_ref, f, field, 0, b, g, re * cos_value + im * sin_value)
                        store(a_ref, f, field, 1, b, g, im * cos_value - re * sin_value)

    def filtered(src, f, field, b, g, d, taps):
        step_x, step_y = directions[d]

        def at(part, k):
            return load(src, f, field, part, b + k * step_y, g, k * step_x)

        c0r, c0i, c1r, c1i, c2r, c2i = taps
        re, im = at(0, 0), at(1, 0)
        p1r, p1i = at(0, 1) + at(0, -1), at(1, 1) + at(1, -1)
        p2r, p2i = at(0, 2) + at(0, -2), at(1, 2) + at(1, -2)
        both = (re + im) * c0r + (p1r + p1i) * c1r + (p2r + p2i) * c2r
        from_re = re * (c0i - c0r) + p1r * (c1i - c1r) + p2r * (c2i - c2r)
        from_im = im * (c0r + c0i) + p1i * (c1r + c1i) + p2i * (c2r + c2i)
        return both - from_im, both + from_re

    def sweep(src, dst, d, work=None, level=None):
        @pl.loop(0, freq_local, unroll=UNROLL)
        def _(f):
            taps = [taps_ref[f, d, i] for i in range(6)]
            if work is not None:
                beside(work, level, f)
            for field in range(2):
                for g in range(groups):
                    for b in range(blocks):
                        for part, value in enumerate(filtered(src, f, field, b, g, d, taps)):
                            store(dst, f, field, part, b, g, value)
                            if b < REACH:
                                edge = jnp.where(not_last, pltpu.roll(value, LANES - 1, 1), 0.0)
                                store(dst, f, field, part, b + blocks, g, edge)
                            if b >= blocks - REACH:
                                edge = jnp.where(not_first, pltpu.roll(value, 1, 1), 0.0)
                                store(dst, f, field, part, b - blocks, g, edge)

    def last_sweep(src, dst, d, t):
        @pl.loop(0, freq_local, unroll=UNROLL)
        def _(f):
            taps = [taps_ref[f, d, i] for i in range(6)]
            for g in range(groups):
                for b in range(blocks):
                    s_re, s_im = filtered(src, f, 0, b, g, d, taps)
                    r_re, r_im = filtered(src, f, 1, b, g, d, taps)
                    store(dst, f, 0, 0, b, g, s_re)
                    store(dst, f, 0, 1, b, g, s_im)
                    store(dst, f, 1, 0, b, g, r_re)
                    store(dst, f, 1, 1, b, g, r_im)
                    term = s_re * r_re - s_im * r_im
                    at = (t, b, slice(SUB * g, SUB * (g + 1)))
                    c_ref[at] = jnp.where(f == 0, term, c_ref[at] + term)

    def depth_step(t):
        sweep(a_ref, b_ref, 0, take_slab, jnp.minimum(t + 1, levels - 1))
        sweep(b_ref, a_ref, 1, give_sum, jnp.maximum(t - 1, 0))
        sweep(a_ref, b_ref, 2)
        last_sweep(b_ref, a_ref, 3, t)

    def surface(f, field, part, b, g):
        ref = own_ref if f < freq_own else near_ref
        return tile(ref, f % freq_own, field, part, b, g)[...]

    lens(0, surface)

    @pl.loop(0, levels)
    def _(t):
        @pl.when(t > 0)
        def _():
            lens(t, lambda f, field, part, b, g: load(a_ref, f, field, part, b, g))

        depth_step(t)

    for g in range(groups):
        give_sum(levels - 1, g)


SMEM = pl.BlockSpec(memory_space=pltpu.SMEM)
VMEM = pl.BlockSpec(memory_space=pltpu.VMEM)


def pack(taps, spectrum, receiver, slab, half, border):
    freq_local, _, height, _ = receiver.shape
    rows = freq_local * 2 * height + tail_rows(freq_local, height, half, border)[0]
    return pl.pallas_call(
        functools.partial(pack_kernel, border),
        out_shape=jax.ShapeDtypeStruct((rows, half), jnp.float32),
        in_specs=[SMEM, SMEM, VMEM, pl.BlockSpec(memory_space=pl.ANY)],
        out_specs=VMEM,
        cost_estimate=pl.CostEstimate(flops=0, bytes_accessed=8 * rows * half, transcendentals=0),
        compiler_params=pltpu.CompilerParams(vmem_limit_bytes=32 * 1024 * 1024),
    )(taps, spectrum, receiver, slab)


def prepared(kernel, shape, levels, width, specs, operands):
    freq_local, _, height, _ = shape
    cells = freq_local * height * width
    return pl.pallas_call(
        kernel,
        out_shape=(
            jax.ShapeDtypeStruct((freq_local, 2, 2, width // LANES, height, LANES), jnp.float32),
            jax.ShapeDtypeStruct((freq_local, len(directions), 6, SUB, LANES), jnp.float32),
            jax.ShapeDtypeStruct((freq_local, SUB, LANES), jnp.float32),
            jax.ShapeDtypeStruct((levels, SUB, LANES), jnp.int32),
        ),
        in_specs=specs,
        out_specs=(VMEM, VMEM, VMEM, VMEM),
        cost_estimate=pl.CostEstimate(flops=100 * cells, bytes_accessed=24 * cells, transcendentals=0),
        compiler_params=pltpu.CompilerParams(vmem_limit_bytes=32 * 1024 * 1024),
    )(*operands)


def migrate(own, near, slabs, freq_total):
    freq_own, _, _, blocks, height, _ = own[0].shape
    freq_local = 2 * freq_own
    levels = slabs.shape[0]
    state = pltpu.VMEM((freq_local, 2, 2, blocks + 2 * REACH, height + 2 * SUB, LANES), jnp.float32)
    return pl.pallas_call(
        functools.partial(migrate_kernel, freq_total),
        out_shape=jax.ShapeDtypeStruct(slabs.shape, jnp.float32),
        in_specs=[VMEM] * 7,
        out_specs=VMEM,
        scratch_shapes=[
            state,
            state,
            pltpu.VMEM((levels, blocks, height, LANES), jnp.float32),
            pltpu.VMEM((levels, blocks, height, LANES), jnp.float32),
            pltpu.VMEM((freq_local, len(directions), 6, SUB, LANES), jnp.float32),
            pltpu.VMEM((freq_local, SUB, LANES), jnp.float32),
        ],
        compiler_params=pltpu.CompilerParams(vmem_limit_bytes=32 * 1024 * 1024),
    )(*own, *near, slabs)


def exchange(value, mask, size):
    return lax.ppermute(value, "freq", [(i, i ^ mask) for i in range(size)])


def far_bits(size):
    found = []
    bit = 2 * NEAR_COLUMNS
    while bit < size:
        found.append((bit, bit | sum(b for b, _ in found)))
        bit *= 2
    return found


def rows_split(value, upper):
    half = value.shape[-2] // 2
    low, high = value[..., :half, :], value[..., half:, :]
    return jnp.where(upper, high, low), jnp.where(upper, low, high)


def columns_split(value, upper, width):
    low, high = value[..., :width], value[..., value.shape[-1] - width :]
    return jnp.where(upper, high, low), jnp.where(upper, low, high)


def joined(mine, other, upper, axis):
    return jnp.where(
        upper, jnp.concatenate([other, mine], axis=axis), jnp.concatenate([mine, other], axis=axis)
    )


def fetch_slabs(own, got, turns, rank, size, width):
    upper_rows = (rank & NEAR_ROWS) != 0
    upper_columns = (rank & NEAR_COLUMNS) != 0
    mine, _ = rows_split(own, upper_rows)
    got, _ = rows_split(got, upper_rows)
    held = jnp.stack([mine, got])
    mine, other = columns_split(held, upper_columns, width)
    held = jnp.concatenate([mine, exchange(other, NEAR_COLUMNS, size)], axis=0)
    wanted = turns[0][:, :1, :1] & (NEAR_ROWS | NEAR_COLUMNS)
    carried = jnp.broadcast_to(held[:1], (wanted.shape[0], *held.shape[1:]))
    for c in range(1, held.shape[0]):
        carried = jnp.where(wanted == c, held[c][None], carried)
    far = far_bits(size)
    for i, (bit, mask) in enumerate(far):
        got = exchange(carried, mask, size)
        turn = turns[1 if i == len(far) - 1 else 0][:, :1, :1]
        carried = jnp.where((turn & bit) == 0, carried, got)
    return joined(carried, exchange(carried, NEAR_ROWS, size), upper_rows, -2)


def sums_to_owner(partial, owners, rank, size, half):
    upper_rows = (rank & NEAR_ROWS) != 0
    upper_columns = (rank & NEAR_COLUMNS) != 0
    partial, _ = columns_split(partial, upper_columns, half)
    mine, other = rows_split(partial, upper_rows)
    carried = mine + exchange(other, NEAR_ROWS, size)
    for _, mask in far_bits(size):
        carried = carried + exchange(carried, mask, size)

    def slot(place):
        return jnp.sum(jnp.where((owners == place)[:, None, None], carried, 0.0), axis=0)

    mine = jnp.stack([slot(rank), slot(rank ^ NEAR_ROWS)])
    other = jnp.stack([slot(rank ^ NEAR_COLUMNS), slot(rank ^ NEAR_ROWS ^ NEAR_COLUMNS)])
    both = joined(mine, exchange(other, NEAR_COLUMNS, size), upper_columns, -1)
    return joined(both[0], exchange(both[1], NEAR_ROWS, size), upper_rows, -2)


def local(receiver_data, source_spectrum, filter_taps, slowness, depth_owner, source_position):
    freq_local, _, height, breadth = receiver_data.shape
    levels = depth_owner.shape[0]
    size = lax.axis_size("freq")
    rank = lax.axis_index("freq")
    freq_total = size * freq_local
    half = breadth // 2
    border = REACH * sum(1 for _, step_y in directions if step_y) * levels
    width = half + LANES
    shape = receiver_data.shape

    near_slab = exchange(slowness[0], NEAR_ROWS, size)
    packed = pack(
        filter_taps, source_spectrum, receiver_data, near_slab, half, border
    )
    arrived = exchange(packed, NEAR_COLUMNS, size)
    *own, own_turn = prepared(
        functools.partial(prepare_own_kernel, freq_total),
        shape,
        levels,
        width,
        [SMEM, SMEM, SMEM, SMEM, VMEM, pl.BlockSpec(memory_space=pl.ANY)],
        (depth_owner, source_position, filter_taps, source_spectrum, receiver_data, packed),
    )
    *near, near_turn = prepared(
        functools.partial(prepare_near_kernel, freq_total, breadth, border),
        shape,
        levels,
        width,
        [SMEM, SMEM, VMEM],
        (depth_owner, source_position, arrived),
    )
    turns = (own_turn, near_turn)
    slabs = fetch_slabs(slowness[0], near_slab, turns, rank, size, width)
    partial = migrate(own, near, slabs, freq_total)
    return sums_to_owner(partial, depth_owner, rank, size, half)[None]


def solution(mesh):
    return jax.shard_map(
        local,
        mesh=mesh,
        in_specs=(
            P(("shot", "freq"), None, None, None),
            P("freq", None),
            P("freq", None, None),
            P("freq", None, None),
            P("shot"),
            P("shot"),
        ),
        out_specs=P(("shot", "freq"), None, None),
        check_vma=False,
    )
```

```python
import functools
import math

import jax
import jax.numpy as jnp
from jax import lax
from jax.experimental import pallas as pl
from jax.experimental.pallas import tpu as pltpu
from jax.sharding import PartitionSpec as P

lens_rate = 3.0
wave_rate = 0.5
greatest_slowness = 2.0
directions = ((1, 0), (0, 1), (1, 1), (1, -1))
LANES = 128
SUB = 8
UNROLL = 2
REACH = 2
NEAR_ROWS = 1
NEAR_COLUMNS = 2
TWO_OVER_PI = 2.0 / math.pi
PI_2 = (1.5703125, 4.837512969970703125e-4, 7.54978995489188216e-8)


def small_cos_sin(r):
    r2 = r * r
    s = r + r * r2 * (-1.6666654611e-1 + r2 * (8.3321608736e-3 + r2 * -1.9515295891e-4))
    c = (1.0 - 0.5 * r2) + r2 * r2 * (
        4.166664568298827e-2 + r2 * (-1.388731625493765e-3 + r2 * 2.443315711809948e-5)
    )
    return c, s


def cos_sin(x):
    turns = jnp.floor(x * TWO_OVER_PI + 0.5)
    r = x - turns * PI_2[0]
    r = r - turns * PI_2[1]
    r = r - turns * PI_2[2]
    c, s = small_cos_sin(r)
    quadrant = turns.astype(jnp.int32)
    odd = (quadrant & 1) == 1
    cos_value = jnp.where(odd, s, c)
    sin_value = jnp.where(odd, c, s)
    cos_value = jnp.where(((quadrant + 1) & 2) == 2, -cos_value, cos_value)
    sin_value = jnp.where((quadrant & 2) == 2, -sin_value, sin_value)
    return cos_value, sin_value


def quotient(x, divisor):
    return jnp.floor((x.astype(jnp.float32) + 0.5) * (1.0 / divisor)).astype(jnp.int32)


def columns():
    return lax.broadcasted_iota(jnp.int32, (SUB, LANES), 1)


def interleave(blocks, shifts=None):
    count = len(blocks)
    out = []
    for c in range(count):
        column = columns() * count + c
        pick, source = column & (LANES - 1), column >> (LANES.bit_length() - 1)
        value = None
        for b in range(count):
            at = pick if shifts is None or shifts[b] is None else (pick + shifts[b]) & (LANES - 1)
            found = jnp.take_along_axis(blocks[b], at, axis=1)
            value = found if value is None else jnp.where(source == b, found, value)
        out.append(value)
    return out


def deinterleave(blocks):
    count = len(blocks)
    out = []
    for b in range(count):
        column = columns() + LANES * b
        pick = quotient(column, count)
        source = column - pick * count
        value = jnp.take_along_axis(blocks[0], pick, axis=1)
        for c in range(1, count):
            value = jnp.where(source == c, jnp.take_along_axis(blocks[c], pick, axis=1), value)
        out.append(value)
    return out


def tile(ref, f, field, part, block, group, shift=0):
    return ref.at[f, field, part, block, pl.ds(SUB * group + shift, SUB), :]


def spread_turn(owner_ref, turn_ref):
    for t in range(owner_ref.shape[0]):
        turn_ref[t] = jnp.full((SUB, LANES), owner_ref[t] ^ lax.axis_index("freq"), jnp.int32)


def tail_of(ref, rows, i):
    across = ref.shape[1] // LANES
    down = rows + SUB * (i // across)
    return ref.at[down : down + SUB, LANES * (i % across) : LANES * (i % across + 1)]


def tail_rows(freq_local, height, half, border):
    strips = -(-freq_local * 2 * (height // SUB) // (LANES // border))
    scalars = -(-freq_local * (len(directions) * 6 + 2) // LANES)
    return SUB * -(-(strips + scalars) // (half // LANES)), strips


def pack_kernel(border, taps_ref, spectrum_ref, receiver_ref, slab_ref, out_ref):
    freq_local, _, height, breadth = receiver_ref.shape
    half = out_ref.shape[1]
    groups = height // SUB
    _, strips = tail_rows(freq_local, height, half, border)
    lane = columns()
    to_lower = (lax.axis_index("freq") & NEAR_COLUMNS) != 0
    start = jnp.where(to_lower, 0, breadth - half)
    beside = pl.ds(pl.multiple_of(jnp.where(to_lower, half, half - LANES), LANES), LANES)
    rows = freq_local * 2 * height
    per = LANES // border
    strip = [jnp.zeros((SUB, LANES), jnp.float32) for _ in range(strips)]
    for f in range(freq_local):
        for part in range(2):
            row = (2 * f + part) * height
            for b in range(half // LANES):
                column = pl.ds(pl.multiple_of(start + LANES * b, LANES), LANES)
                out_ref[row : row + height, LANES * b : LANES * (b + 1)] = receiver_ref[f, part, :, column]
            for g in range(groups):
                value = receiver_ref[f, part, SUB * g : SUB * (g + 1), beside]
                value = jnp.where(to_lower, value, pltpu.roll(value, border, 1))
                i, at = divmod((2 * f + part) * groups + g, per)
                if at:
                    value = pltpu.roll(value, border * at, 1)
                strip[i] = jnp.where((lane >= border * at) & (lane < border * (at + 1)), value, strip[i])
    for i, value in enumerate(strip):
        tail_of(out_ref, rows, i)[...] = value
    scalars = [
        taps_ref[f, d, i] for f in range(freq_local) for d in range(len(directions)) for i in range(6)
    ] + [spectrum_ref[f, i] for f in range(freq_local) for i in range(2)]
    for b in range(-(-len(scalars) // LANES)):
        value = jnp.zeros((SUB, LANES), jnp.float32)
        for i, scalar in enumerate(scalars[LANES * b : LANES * (b + 1)]):
            value = jnp.where(lane == i, scalar, value)
        tail_of(out_ref, rows, strips + b)[...] = value


def prepare(freq_total, rank, first_column, owner_ref, position_ref, window_of, taps_of, wave_of, results):
    field_ref, taps_out_ref, rate_ref, turn_ref = results
    freq_local, _, _, blocks, height, _ = field_ref.shape
    groups = height // SUB
    lane = columns()
    row = lax.broadcasted_iota(jnp.int32, (SUB, LANES), 0)

    def number(f):
        return (rank * freq_local + f).astype(jnp.float32) + 1.0

    for f in range(freq_local):
        for d in range(len(directions)):
            for i in range(6):
                taps_out_ref[f, d, i] = jnp.broadcast_to(taps_of(f, d, i), (SUB, LANES))
        rate_ref[f] = jnp.full((SUB, LANES), number(f) * (lens_rate / freq_total), jnp.float32)
    spread_turn(owner_ref, turn_ref)

    for f in range(freq_local):
        for part in range(2):
            for g in range(groups):
                for b, value in enumerate(window_of(f, part, g)):
                    tile(field_ref, f, 1, part, b, g)[...] = -value if part else value

    src_row = position_ref[0].astype(jnp.float32)
    src_col = position_ref[1].astype(jnp.float32)
    waves = [(wave_of(f, 0), wave_of(f, 1)) for f in range(freq_local)]
    for g in range(groups):
        for b in range(blocks):
            d_row = (row + SUB * g).astype(jnp.float32) - src_row
            d_col = (lane * blocks + (first_column + b)).astype(jnp.float32) - src_col
            distance = jnp.sqrt(d_row * d_row + d_col * d_col + 1.0)
            amplitude = 1.0 / (1.0 + distance / (height / 4.0))
            for f, (w_re, w_im) in enumerate(waves):
                cos_value, sin_value = cos_sin(number(f) * (wave_rate / freq_total) * distance)
                base_re = amplitude * cos_value
                base_im = -amplitude * sin_value
                tile(field_ref, f, 0, 0, b, g)[...] = w_re * base_re - w_im * base_im
                tile(field_ref, f, 0, 1, b, g)[...] = w_re * base_im + w_im * base_re


def prepare_own_kernel(
    freq_total, owner_ref, position_ref, taps_ref, spectrum_ref, receiver_ref, packed_ref, *results
):
    blocks = results[0].shape[3]
    here = lax.axis_index("freq")
    first_column = jnp.where((here & NEAR_COLUMNS) != 0, receiver_ref.shape[3] - blocks * LANES, 0)

    def window_of(f, part, g):
        starts = [pl.multiple_of(first_column + LANES * b, LANES) for b in range(blocks)]
        return interleave(
            [receiver_ref[f, part, SUB * g : SUB * (g + 1), pl.ds(start, LANES)] for start in starts]
        )

    prepare(
        freq_total,
        here,
        first_column,
        owner_ref,
        position_ref,
        window_of,
        lambda f, d, i: taps_ref[f, d, i],
        lambda f, i: spectrum_ref[f, i],
        results,
    )


def prepare_near_kernel(freq_total, breadth, border, owner_ref, position_ref, packed_ref, *results):
    freq_local, _, _, blocks, height, _ = results[0].shape
    half = packed_ref.shape[1]
    groups = height // SUB
    here = lax.axis_index("freq")
    upper = (here & NEAR_COLUMNS) != 0
    first_column = jnp.where(upper, breadth - blocks * LANES, 0)
    rows = freq_local * 2 * height
    _, strips = tail_rows(freq_local, height, half, border)
    per = LANES // border
    taps_count = len(directions) * 6
    lane = columns()

    def main(f, part, g, b):
        row = (2 * f + part) * height + SUB * g
        return packed_ref[row : row + SUB, LANES * b : LANES * (b + 1)]

    def window_of(f, part, g):
        i, at = divmod((2 * f + part) * groups + g, per)
        strip = tail_of(packed_ref, rows, i)[...]
        mains = [main(f, part, g, b) for b in range(blocks - 1)]
        found = [strip if b == 0 else mains[b - 1] for b in range(blocks)]
        lower = mains + [strip]
        shifts = [None] * blocks
        shifts[0] = jnp.where(upper, border * (at + 1), 0)
        shifts[-1] = jnp.where(upper, 0, border * at)
        return interleave([jnp.where(upper, u, v) for u, v in zip(found, lower)], shifts)

    def scalar(i):
        value = tail_of(packed_ref, rows, strips + i // LANES)[...]
        return jnp.broadcast_to(value[:, i % LANES : i % LANES + 1], (SUB, LANES))

    prepare(
        freq_total,
        here ^ NEAR_COLUMNS,
        first_column,
        owner_ref,
        position_ref,
        window_of,
        lambda f, d, i: scalar(f * taps_count + 6 * d + i),
        lambda f, i: scalar(freq_local * taps_count + 2 * f + i),
        results,
    )


def migrate_kernel(
    freq_total,
    own_ref,
    own_taps_ref,
    own_rate_ref,
    near_ref,
    near_taps_ref,
    near_rate_ref,
    slab_ref,
    out_ref,
    a_ref,
    b_ref,
    v_ref,
    c_ref,
    taps_ref,
    rate_ref,
):
    freq_own = own_ref.shape[0]
    freq_local = 2 * freq_own
    levels, height, breadth = slab_ref.shape
    blocks = breadth // LANES
    groups = height // SUB
    lane = lax.broadcasted_iota(jnp.int32, (SUB, LANES), 1)
    not_first = lane > 0
    not_last = lane < LANES - 1

    def load(ref, f, field, part, block, group, shift=0):
        return tile(ref, f, field, part, block + REACH, group + 1, shift)[...]

    def store(ref, f, field, part, block, group, value):
        tile(ref, f, field, part, block + REACH, group + 1)[...] = value

    for side, (one_taps_ref, one_rate_ref) in enumerate(
        ((own_taps_ref, own_rate_ref), (near_taps_ref, near_rate_ref))
    ):
        for f in range(freq_own):
            rate_ref[side * freq_own + f] = one_rate_ref[f]
            for d in range(len(directions)):
                for i in range(6):
                    taps_ref[side * freq_own + f, d, i] = one_taps_ref[f, d, i]

    zero = jnp.zeros((SUB, LANES), jnp.float32)

    @pl.loop(0, freq_local)
    def _(f):
        for ref in (a_ref, b_ref):
            for field in range(2):
                for part in range(2):
                    for block in range(blocks + 2 * REACH):
                        tile(ref, f, field, part, block, 0)[...] = zero
                        tile(ref, f, field, part, block, groups + 1)[...] = zero

    def rows_of(g):
        return pl.ds(pl.multiple_of(SUB * g, SUB), SUB)

    def take_slab(t, g):
        rows = rows_of(g)
        loaded = [slab_ref[t, rows, LANES * b : LANES * (b + 1)] for b in range(blocks)]
        for b, value in enumerate(interleave(loaded)):
            v_ref[t, b, rows, :] = value

    def give_sum(t, g):
        rows = rows_of(g)
        for b, value in enumerate(deinterleave([c_ref[t, b, rows] for b in range(blocks)])):
            out_ref[t, rows, LANES * b : LANES * (b + 1)] = value * (1.0 / math.sqrt(freq_total))

    def beside(work, t, f):
        share = -(-groups // freq_local)
        for k in range(share):
            work(t, jnp.minimum(f * share + k, groups - 1))

    for g in range(groups):
        take_slab(0, g)

    def lens(t, get):
        step_rate = lens_rate / freq_total
        step = small_cos_sin if step_rate * greatest_slowness < math.pi / 4.0 else cos_sin
        apart = NEAR_COLUMNS * freq_own
        side = jnp.where((lax.axis_index("freq") & NEAR_COLUMNS) != 0, -1.0, 1.0)

        def plus(one, other):
            return one[0] * other[0] - one[1] * other[1], one[1] * other[0] + one[0] * other[1]

        for g in range(groups):
            for b in range(blocks):
                slow = v_ref[t, b, SUB * g : SUB * (g + 1), :]
                by_one = step(step_rate * slow)
                far = by_one
                if apart & (apart - 1) == 0:
                    for _ in range(apart.bit_length() - 1):
                        far = far[0] * far[0] - far[1] * far[1], 2.0 * far[0] * far[1]
                else:
                    far = cos_sin(apart * step_rate * slow)
                own = [cos_sin(rate_ref[0] * slow)]
                near = [plus(own[0], (far[0], side * far[1]))]
                for _ in range(1, freq_own):
                    own.append(plus(own[-1], by_one))
                    near.append(plus(near[-1], by_one))
                for f, (cos_value, sin_value) in enumerate(own + near):
                    for field in range(2):
                        re, im = get(f, field, 0, b, g), get(f, field, 1, b, g)
                        store(a_ref, f, field, 0, b, g, re * cos_value + im * sin_value)
                        store(a_ref, f, field, 1, b, g, im * cos_value - re * sin_value)

    def filtered(src, f, field, b, g, d, taps):
        step_x, step_y = directions[d]

        def at(part, k):
            return load(src, f, field, part, b + k * step_y, g, k * step_x)

        c0r, c0i, c1r, c1i, c2r, c2i = taps
        re, im = at(0, 0), at(1, 0)
        p1r, p1i = at(0, 1) + at(0, -1), at(1, 1) + at(1, -1)
        p2r, p2i = at(0, 2) + at(0, -2), at(1, 2) + at(1, -2)
        both = (re + im) * c0r + (p1r + p1i) * c1r + (p2r + p2i) * c2r
        from_re = re * (c0i - c0r) + p1r * (c1i - c1r) + p2r * (c2i - c2r)
        from_im = im * (c0r + c0i) + p1i * (c1r + c1i) + p2i * (c2r + c2i)
        return both - from_im, both + from_re

    def sweep(src, dst, d, work=None, level=None):
        @pl.loop(0, freq_local, unroll=UNROLL)
        def _(f):
            taps = [taps_ref[f, d, i] for i in range(6)]
            if work is not None:
                beside(work, level, f)
            for field in range(2):
                for g in range(groups):
                    for b in range(blocks):
                        for part, value in enumerate(filtered(src, f, field, b, g, d, taps)):
                            store(dst, f, field, part, b, g, value)
                            if b < REACH:
                                edge = jnp.where(not_last, pltpu.roll(value, LANES - 1, 1), 0.0)
                                store(dst, f, field, part, b + blocks, g, edge)
                            if b >= blocks - REACH:
                                edge = jnp.where(not_first, pltpu.roll(value, 1, 1), 0.0)
                                store(dst, f, field, part, b - blocks, g, edge)

    def last_sweep(src, dst, d, t, more):
        @pl.loop(0, freq_local, unroll=UNROLL)
        def _(f):
            taps = [taps_ref[f, d, i] for i in range(6)]
            for b in range(blocks):
                for g in range(groups):
                    s_re, s_im = filtered(src, f, 0, b, g, d, taps)
                    r_re, r_im = filtered(src, f, 1, b, g, d, taps)
                    if more:
                        store(dst, f, 0, 0, b, g, s_re)
                        store(dst, f, 0, 1, b, g, s_im)
                        store(dst, f, 1, 0, b, g, r_re)
                        store(dst, f, 1, 1, b, g, r_im)
                    term = s_re * r_re - s_im * r_im
                    at = (t, b, slice(SUB * g, SUB * (g + 1)))
                    c_ref[at] = jnp.where(f == 0, term, c_ref[at] + term)

    def depth_step(t, more):
        if more:
            sweep(a_ref, b_ref, 0, take_slab, t + 1)
        else:
            sweep(a_ref, b_ref, 0)
        sweep(b_ref, a_ref, 1, give_sum, jnp.maximum(t - 1, 0))
        sweep(a_ref, b_ref, 2)
        last_sweep(b_ref, a_ref, 3, t, more)

    def carried(f, field, part, b, g):
        return load(a_ref, f, field, part, b, g)

    def surface(f, field, part, b, g):
        ref = own_ref if f < freq_own else near_ref
        return tile(ref, f % freq_own, field, part, b, g)[...]

    lens(0, surface)

    @pl.loop(0, levels - 1)
    def _(t):
        @pl.when(t > 0)
        def _():
            lens(t, carried)

        depth_step(t, True)

    if levels > 1:
        lens(levels - 1, carried)
    depth_step(levels - 1, False)
    for g in range(groups):
        give_sum(levels - 1, g)


SMEM = pl.BlockSpec(memory_space=pltpu.SMEM)
VMEM = pl.BlockSpec(memory_space=pltpu.VMEM)


def pack(taps, spectrum, receiver, slab, half, border):
    freq_local, _, height, _ = receiver.shape
    rows = freq_local * 2 * height + tail_rows(freq_local, height, half, border)[0]
    return pl.pallas_call(
        functools.partial(pack_kernel, border),
        out_shape=jax.ShapeDtypeStruct((rows, half), jnp.float32),
        in_specs=[SMEM, SMEM, VMEM, pl.BlockSpec(memory_space=pl.ANY)],
        out_specs=VMEM,
        cost_estimate=pl.CostEstimate(flops=0, bytes_accessed=8 * rows * half, transcendentals=0),
        compiler_params=pltpu.CompilerParams(vmem_limit_bytes=32 * 1024 * 1024),
    )(taps, spectrum, receiver, slab)


def prepared(kernel, shape, levels, width, specs, operands):
    freq_local, _, height, _ = shape
    cells = freq_local * height * width
    return pl.pallas_call(
        kernel,
        out_shape=(
            jax.ShapeDtypeStruct((freq_local, 2, 2, width // LANES, height, LANES), jnp.float32),
            jax.ShapeDtypeStruct((freq_local, len(directions), 6, SUB, LANES), jnp.float32),
            jax.ShapeDtypeStruct((freq_local, SUB, LANES), jnp.float32),
            jax.ShapeDtypeStruct((levels, SUB, LANES), jnp.int32),
        ),
        in_specs=specs,
        out_specs=(VMEM, VMEM, VMEM, VMEM),
        cost_estimate=pl.CostEstimate(flops=100 * cells, bytes_accessed=24 * cells, transcendentals=0),
        compiler_params=pltpu.CompilerParams(vmem_limit_bytes=32 * 1024 * 1024),
    )(*operands)


def migrate(own, near, slabs, freq_total):
    freq_own, _, _, blocks, height, _ = own[0].shape
    freq_local = 2 * freq_own
    levels = slabs.shape[0]
    state = pltpu.VMEM((freq_local, 2, 2, blocks + 2 * REACH, height + 2 * SUB, LANES), jnp.float32)
    return pl.pallas_call(
        functools.partial(migrate_kernel, freq_total),
        out_shape=jax.ShapeDtypeStruct(slabs.shape, jnp.float32),
        in_specs=[VMEM] * 7,
        out_specs=VMEM,
        scratch_shapes=[
            state,
            state,
            pltpu.VMEM((levels, blocks, height, LANES), jnp.float32),
            pltpu.VMEM((levels, blocks, height, LANES), jnp.float32),
            pltpu.VMEM((freq_local, len(directions), 6, SUB, LANES), jnp.float32),
            pltpu.VMEM((freq_local, SUB, LANES), jnp.float32),
        ],
        compiler_params=pltpu.CompilerParams(vmem_limit_bytes=32 * 1024 * 1024),
    )(*own, *near, slabs)


def exchange(value, mask, size):
    return lax.ppermute(value, "freq", [(i, i ^ mask) for i in range(size)])


def far_bits(size):
    found = []
    bit = 2 * NEAR_COLUMNS
    while bit < size:
        found.append((bit, bit | sum(b for b, _ in found)))
        bit *= 2
    return found


def rows_split(value, upper):
    half = value.shape[-2] // 2
    low, high = value[..., :half, :], value[..., half:, :]
    return jnp.where(upper, high, low), jnp.where(upper, low, high)


def columns_split(value, upper, width):
    low, high = value[..., :width], value[..., value.shape[-1] - width :]
    return jnp.where(upper, high, low), jnp.where(upper, low, high)


def joined(mine, other, upper, axis):
    return jnp.where(
        upper, jnp.concatenate([other, mine], axis=axis), jnp.concatenate([mine, other], axis=axis)
    )


def fetch_slabs(own, got, turns, rank, size, width):
    upper_rows = (rank & NEAR_ROWS) != 0
    upper_columns = (rank & NEAR_COLUMNS) != 0
    mine, _ = rows_split(own, upper_rows)
    got, _ = rows_split(got, upper_rows)
    held = jnp.stack([mine, got])
    mine, other = columns_split(held, upper_columns, width)
    held = jnp.concatenate([mine, exchange(other, NEAR_COLUMNS, size)], axis=0)
    wanted = turns[0][:, :1, :1] & (NEAR_ROWS | NEAR_COLUMNS)
    carried = jnp.broadcast_to(held[:1], (wanted.shape[0], *held.shape[1:]))
    for c in range(1, held.shape[0]):
        carried = jnp.where(wanted == c, held[c][None], carried)
    far = far_bits(size)
    for i, (bit, mask) in enumerate(far):
        got = exchange(carried, mask, size)
        turn = turns[1 if i == len(far) - 1 else 0][:, :1, :1]
        carried = jnp.where((turn & bit) == 0, carried, got)
    return joined(carried, exchange(carried, NEAR_ROWS, size), upper_rows, -2)


def sums_to_owner(partial, owners, rank, size, half):
    upper_rows = (rank & NEAR_ROWS) != 0
    upper_columns = (rank & NEAR_COLUMNS) != 0
    partial, _ = columns_split(partial, upper_columns, half)
    mine, other = rows_split(partial, upper_rows)
    carried = mine + exchange(other, NEAR_ROWS, size)
    for _, mask in far_bits(size):
        carried = carried + exchange(carried, mask, size)

    def slot(place):
        return jnp.sum(jnp.where((owners == place)[:, None, None], carried, 0.0), axis=0)

    mine = jnp.stack([slot(rank), slot(rank ^ NEAR_ROWS)])
    other = jnp.stack([slot(rank ^ NEAR_COLUMNS), slot(rank ^ NEAR_ROWS ^ NEAR_COLUMNS)])
    both = joined(mine, exchange(other, NEAR_COLUMNS, size), upper_columns, -1)
    return joined(both[0], exchange(both[1], NEAR_ROWS, size), upper_rows, -2)


def local(receiver_data, source_spectrum, filter_taps, slowness, depth_owner, source_position):
    freq_local, _, height, breadth = receiver_data.shape
    levels = depth_owner.shape[0]
    size = lax.axis_size("freq")
    rank = lax.axis_index("freq")
    freq_total = size * freq_local
    half = breadth // 2
    border = REACH * sum(1 for _, step_y in directions if step_y) * levels
    width = half + LANES
    shape = receiver_data.shape

    near_slab = exchange(slowness[0], NEAR_ROWS, size)
    packed = pack(
        filter_taps, source_spectrum, receiver_data, near_slab, half, border
    )
    arrived = exchange(packed, NEAR_COLUMNS, size)
    *own, own_turn = prepared(
        functools.partial(prepare_own_kernel, freq_total),
        shape,
        levels,
        width,
        [SMEM, SMEM, SMEM, SMEM, VMEM, pl.BlockSpec(memory_space=pl.ANY)],
        (depth_owner, source_position, filter_taps, source_spectrum, receiver_data, packed),
    )
    *near, near_turn = prepared(
        functools.partial(prepare_near_kernel, freq_total, breadth, border),
        shape,
        levels,
        width,
        [SMEM, SMEM, VMEM],
        (depth_owner, source_position, arrived),
    )
    turns = (own_turn, near_turn)
    slabs = fetch_slabs(slowness[0], near_slab, turns, rank, size, width)
    partial = migrate(own, near, slabs, freq_total)
    return sums_to_owner(partial, depth_owner, rank, size, half)[None]


def solution(mesh):
    return jax.shard_map(
        local,
        mesh=mesh,
        in_specs=(
            P(("shot", "freq"), None, None, None),
            P("freq", None),
            P("freq", None, None),
            P("freq", None, None),
            P("shot"),
            P("shot"),
        ),
        out_specs=P(("shot", "freq"), None, None),
        check_vma=False,
    )
```
